512 devices in a mesh: section: 32 (over y, z_hi), dp: 16 (over z_lo, x, core).
Axes of the slice: x: 4, y: 8, z: 8 (z_hi: 4, z_lo: 2; z = z_hi * 2 + z_lo), core: 2. Of those that a mesh axis runs over, the one named last changes fastest.
Arguments:
- block_inputs: bfloat16 [32, 4096, 2048], P('section', 'dp'), may hold values from -6 to 6
- target: bfloat16 [4096, 2048], P('dp'), may hold values from -6 to 6
- frozen_weight: bfloat16 [32, 2048, 2048], P('section', 'dp'), may hold values from -0.125 to 0.125
- adapter_down_weight: bfloat16 [32, 2048, 128], P('section', 'dp'), may hold values from -0.125 to 0.125
- adapter_up_weight: bfloat16 [32, 2048, 128], P('section', 'dp'), may hold values from -0.5 to 0.5
- start_modulation: bfloat16 [32, 16, 6144], P('section'), may hold values from -1.1953125 to 1.1953125
- finish_modulation: bfloat16 [32, 16, 6144], P('section'), may hold values from -1.1953125 to 1.1953125
- level_pairs: int32 [128, 2], P('dp'), may hold values from 0 to 15
Outputs:
- input_grads: bfloat16 [32, 4096, 2048], P('section', 'dp')
- down_grad: float32 [32, 2048, 128], P('section', 'dp')
- up_grad: float32 [32, 2048, 128], P('section', 'dp')
The draws below stay inside these ranges and needn't reach their ends.
Inputs may be any that keep to these rules, and one draw needn't show every extreme that they name: `level_pairs`: each row holds the start and the end time level of one micro-batch.
All inputs are finite; a program needn't handle non-finite values.
Results may differ from the reference program's by a relative error of at most 0.038.
Values may be sent and summed in bfloat16 or wider, within the bound.
No kernel may reach another device: no remote copies, remote signals or barrier semaphores. Data moves between devices by JAX's collectives and lax.ppermute only.
A program may use at most 64 MiB of HBM per device.

```python
import math
import jax
import jax.numpy as jnp
from jax import lax

HIDDEN_WIDTH = 2048
ADAPTER_RANK = 128
LEVELS = 16
BLOCK_COUNT = 32
TOKENS = 4096
BATCHES = 128


def with_ends(values, stream_key, low, top_value):
    longest = values.shape.index(max(values.shape))
    spots = []
    for shift in (0, 1):
        where = [jax.random.randint(jax.random.fold_in(stream_key, axis), (), 0, length) for axis, length in enumerate(values.shape)]
        where[longest] = (where[longest] + shift) % values.shape[longest]
        spots.append(tuple(where))
    return values.at[spots[0]].set(low).at[spots[1]].set(top_value)


def raised(drawn, key, source, target, blocks, factor):
    def block_of(dim):
        return (jnp.arange(drawn.shape[dim]) // (drawn.shape[dim] // blocks)).reshape((-1,) + (1,) * (drawn.ndim - 1 - dim))

    first = jax.random.permutation(key, blocks)[block_of(target)]
    far = (block_of(target) + blocks // 2) % blocks
    return jnp.where((block_of(source) == first) | (block_of(source) == far), factor * drawn, drawn)


def block_levels(stream_key, shape, cuts, least, top_value):
    loudness = 1.0
    for dim, shards_of in cuts:
        draws = jax.random.uniform(jax.random.fold_in(jax.random.fold_in(stream_key, 6), dim), (shards_of,), jnp.float32, least / len(cuts), top_value / len(cuts))
        loudness = loudness * jnp.repeat(jnp.exp(draws), shape[dim] // shards_of).reshape((-1,) + (1,) * (len(shape) - 1 - dim))
    return loudness


def gaussian(key, extent, deviation, reach, cuts=(), kind=jnp.bfloat16):
    values = jax.random.normal(key, extent, jnp.float32) * deviation
    if len(cuts) > 0:
        values = block_levels(key, extent, cuts, -0.22, 0.18) * values
    return jnp.clip(values, min=-reach, max=reach).astype(kind)


def noise_with(rng, extent, width, bound, split, heavy, kind=jnp.bfloat16):
    values = width * jax.random.normal(rng, extent, jnp.float32)
    if split:
        values = values * block_levels(rng, extent, split, -0.22, 0.18)
    return jnp.clip(raised(values, jax.random.fold_in(rng, 3), *heavy), -bound, bound).astype(kind)


def setup_inputs(seed: int = 0) -> dict:
    key_of = jax.random.split(jax.random.key(seed), 9)
    block_inputs = noise_with(key_of[0], (BLOCK_COUNT, TOKENS, HIDDEN_WIDTH), 1.0, 6.0, ((0, 32), (1, 16)), (1, 2, 16, 2.0))
    target = gaussian(key_of[1], (TOKENS, HIDDEN_WIDTH), 1.0, 6.0, ((0, 16),))
    frozen_weight = gaussian(key_of[2], (BLOCK_COUNT, HIDDEN_WIDTH, HIDDEN_WIDTH), HIDDEN_WIDTH ** -0.5, 0.125, ((0, 32), (1, 16)))
    adapter_down_weight = gaussian(key_of[3], (BLOCK_COUNT, HIDDEN_WIDTH, ADAPTER_RANK), HIDDEN_WIDTH ** -0.5, 0.125, ((0, 32), (1, 16)))
    adapter_up_weight = gaussian(key_of[4], (BLOCK_COUNT, HIDDEN_WIDTH, ADAPTER_RANK), ADAPTER_RANK ** -0.5, 0.5, ((0, 32), (1, 16)))
    start_modulation = gaussian(key_of[5], (BLOCK_COUNT, LEVELS, 3 * HIDDEN_WIDTH), 0.2, 1.1953125, ((0, 32),))
    finish_modulation = gaussian(key_of[6], (BLOCK_COUNT, LEVELS, 3 * HIDDEN_WIDTH), 0.2, 1.1953125, ((0, 32),))
    level_pairs = with_ends(jax.random.randint(key_of[7], (BATCHES, 2), 0, LEVELS), jax.random.fold_in(key_of[7], 1), 0, LEVELS - 1).astype(jnp.int32)
    return {"block_inputs": block_inputs, "target": target, "frozen_weight": frozen_weight, "adapter_down_weight": adapter_down_weight, "adapter_up_weight": adapter_up_weight, "start_modulation": start_modulation, "finish_modulation": finish_modulation, "level_pairs": level_pairs}


epsilon_norm = 1e-06

def activation(values):
    return jax.nn.gelu(values, approximate=True)

def row_modulation(from_table, to_table, level_pairs, block_rows):
    levels = from_table.shape[0]
    ladder = jnp.arange(levels, dtype=jnp.int32)[None, :]
    hot_from = (level_pairs[:, 0:1] == ladder).astype(jnp.bfloat16)
    hot_to = (level_pairs[:, 1:2] == ladder).astype(jnp.bfloat16)
    per_batch = jnp.dot(hot_from, from_table, preferred_element_type=jnp.float32) + jnp.dot(hot_to, to_table, preferred_element_type=jnp.float32)
    return jnp.repeat(per_batch, block_rows, axis=0)

def forward_sweep(inputs, modulation, weight, down_projected, up_projected):
    model_width = inputs.shape[1]
    shift_vec = modulation[:, :model_width]
    scale_vec = modulation[:, model_width:2 * model_width]
    values = inputs.astype(jnp.float32)
    inverse_rms = lax.rsqrt(lax.optimization_barrier(jnp.mean(values * values, axis=1, keepdims=True)) + epsilon_norm)
    normed = values * inverse_rms
    modulated = (normed * (1.0 + scale_vec) + shift_vec).astype(jnp.bfloat16)
    lowrank = jnp.dot(modulated, down_projected, preferred_element_type=jnp.float32).astype(jnp.bfloat16)
    preact = jnp.dot(modulated, weight, preferred_element_type=jnp.float32) + lax.dot_general(lowrank, up_projected, (((1,), (1,)), ((), ())), preferred_element_type=jnp.float32)
    return (normed, inverse_rms, modulated, lowrank, preact)

def backward_pass(cotangent, normed, inverse_rms, preact, scale_vec, gate_vec, weight, down_projected, up_projected):
    upstream = cotangent.astype(jnp.float32)
    outputs_unused, pullback = jax.vjp(activation, preact)
    grad_pre = pullback(upstream * gate_vec)[0].astype(jnp.bfloat16)
    grad_low = jnp.dot(grad_pre, up_projected, preferred_element_type=jnp.float32).astype(jnp.bfloat16)
    grad_mod = lax.dot_general(grad_pre, weight, (((1,), (1,)), ((), ())), preferred_element_type=jnp.float32)
    grad_mod = grad_mod + lax.dot_general(grad_low, down_projected, (((1,), (1,)), ((), ())), preferred_element_type=jnp.float32)
    grad_norm = grad_mod * (1.0 + scale_vec)
    centred = lax.optimization_barrier(jnp.mean(grad_norm * normed, axis=1, keepdims=True))
    grad_input = upstream + inverse_rms * (grad_norm - normed * centred)
    return (grad_input.astype(jnp.bfloat16), grad_pre, grad_low)

def reference(block_inputs, target, frozen_weight, adapter_down_weight, adapter_up_weight, start_modulation, finish_modulation, level_pairs):
    block_total = block_inputs.shape[0]
    token_total = block_inputs.shape[1]
    model_width = block_inputs.shape[2]
    block_rows = token_total // level_pairs.shape[0]
    grad_scale = 1.0 / math.sqrt(token_total)
    closing_modulation = row_modulation(start_modulation[block_total - 1], finish_modulation[block_total - 1], level_pairs, block_rows)
    closing_forward = forward_sweep(block_inputs[block_total - 1], closing_modulation, frozen_weight[block_total - 1], adapter_down_weight[block_total - 1], adapter_up_weight[block_total - 1])
    output = block_inputs[block_total - 1].astype(jnp.float32) + closing_modulation[:, 2 * model_width:] * activation(closing_forward[4])
    seed_grad = (output - target.astype(jnp.float32)).astype(jnp.bfloat16)

    def section_step(cotangent, reverse_index):
        block_position = block_total - 1 - reverse_index
        weight = frozen_weight[block_position]
        down_projected = adapter_down_weight[block_position]
        up_projected = adapter_up_weight[block_position]
        modulation = row_modulation(start_modulation[block_position], finish_modulation[block_position], level_pairs, block_rows)
        normed, inverse_rms, modulated, lowrank, preact = forward_sweep(block_inputs[block_position], modulation, weight, down_projected, up_projected)
        grad_input, grad_pre, grad_low = backward_pass(cotangent, normed, inverse_rms, preact, modulation[:, model_width:2 * model_width], modulation[:, 2 * model_width:], weight, down_projected, up_projected)
        down_part = lax.dot_general(modulated, grad_low, (((0,), (0,)), ((), ())), preferred_element_type=jnp.float32) * grad_scale
        up_part = lax.dot_general(grad_pre, lowrank, (((0,), (0,)), ((), ())), preferred_element_type=jnp.float32) * grad_scale
        return (grad_input, (grad_input, down_part, up_part))
    carry_unused, outputs = lax.scan(section_step, seed_grad, jnp.arange(block_total, dtype=jnp.int32))
    return (outputs[0][::-1], outputs[1][::-1], outputs[2][::-1])
```

```python
import functools
import math

import jax
import jax.numpy as jnp
from jax import lax
from jax.experimental import pallas as pl
from jax.experimental.pallas import tpu as pltpu
from jax.sharding import Mesh, PartitionSpec as P

EPSILON = 1e-06
AXES = ("y", "zh", "zl", "x", "c")
SIZES = (8, 4, 2, 4, 2)
STAGES, BLOCKS = SIZES[0], SIZES[1]
GROUP = ("zl", "x", "c")
PLANE = ("zh", "zl", "x", "c")
MEMBERS = 16
ROWS = 32
CHUNK = 512
SLOTS = 4
LAST_DIMS = (((1,), (1,)), ((), ()))
FIRST_DIMS = (((0,), (0,)), ((), ()))
SLOPE = math.sqrt(2.0 / math.pi)
CUBIC = 0.044715
MIB = 2**20


def dot(left, right, dims=(((1,), (0,)), ((), ()))):
    return lax.dot_general(left, right, dims, preferred_element_type=jnp.float32)


def per_batch_modulation(from_table, to_table, level_pairs):
    ladder = jnp.arange(from_table.shape[0], dtype=jnp.int32)[None, :]
    hot_from = (level_pairs[:, 0:1] == ladder).astype(jnp.bfloat16)
    hot_to = (level_pairs[:, 1:2] == ladder).astype(jnp.bfloat16)
    return dot(hot_from, from_table) + dot(hot_to, to_table)


def forward_kernel(batches, width, place, x, mod, target, wd, up, own_down, own_up, d, h, inv, *rest):
    seeds, (downs, columns, sems, own_sems) = rest[:batches], rest[batches:]
    chunks = width // CHUNK
    total = BLOCKS * chunks
    own = (
        pltpu.make_async_copy(wd.at[place[0], :, width:], own_down, own_sems.at[0]),
        pltpu.make_async_copy(up.at[place[0]], own_up, own_sems.at[1]),
    )

    def fetch_down(b):
        return pltpu.make_async_copy(wd.at[b, :, width:], downs.at[b], sems.at[0, b])

    def fetch_columns(index):
        b, j, slot = BLOCKS - 1 - index // chunks, index % chunks, index % SLOTS
        return pltpu.make_async_copy(wd.at[b, :, pl.ds(j * CHUNK, CHUNK)], columns.at[slot], sems.at[1, slot])

    for index in range(total):
        b, j = BLOCKS - 1 - index // chunks, index % chunks
        if index == 0:
            fetch_down(b).start()
            for ahead in range(SLOTS):
                fetch_columns(ahead).start()
            for other in reversed(range(BLOCKS - 1)):
                fetch_down(other).start()
            for copy in own:
                copy.start()
        if j == 0:
            pieces = []
            for m in range(batches):
                r = pl.ds(m * ROWS, ROWS)
                values = x[b, r, :].astype(jnp.float32)
                rms = lax.rsqrt(jnp.mean(values * values, axis=1, keepdims=True) + EPSILON)
                normed = values * rms
                h[b, r, :] = normed
                inv[b, r, :] = jnp.broadcast_to(rms, (ROWS, inv.shape[2]))
                shift = mod[b, pl.ds(m, 1), 0:width]
                scale = mod[b, pl.ds(m, 1), width : 2 * width]
                pieces.append((normed * (1.0 + scale) + shift).astype(jnp.bfloat16))
            modulated = jnp.concatenate(pieces, axis=0)
            fetch_down(b).wait()
            low = dot(modulated, downs[b]).astype(jnp.bfloat16)
        c = pl.ds(j * CHUNK, CHUNK)
        fetch_columns(index).wait()
        pre = dot(modulated, columns[index % SLOTS]) + dot(low, up[b, c, :], LAST_DIMS)
        if index + SLOTS < total:
            fetch_columns(index + SLOTS).start()
        squared = pre * pre
        bent = jnp.tanh(SLOPE * pre * (1.0 + CUBIC * squared))
        half = 0.5 * (1.0 + bent)
        slope = half + 0.5 * pre * (1.0 - bent * bent) * (SLOPE * (1.0 + 3.0 * CUBIC * squared))
        for m in range(batches):
            s = slice(m * ROWS, (m + 1) * ROWS)
            gate = mod[b, pl.ds(m, 1), pl.ds(2 * width + j * CHUNK, CHUNK)]
            d[b, s, c] = slope[s] * gate
            if b == BLOCKS - 1:
                out = x[b, s, c].astype(jnp.float32) + gate * (pre[s] * half[s])
                seeds[m][:, c] = (out - target[s, c].astype(jnp.float32)).astype(jnp.bfloat16)
    for copy in own:
        copy.wait()


def chain_kernel(active_stage, m, width, stage, gin, wd, up, d, h, mod, inv, gs_in, us_in, gout, gs, us, g_keep, u_keep, sems):
    r = pl.ds(m * ROWS, ROWS)

    def store_u(b):
        return pltpu.make_async_copy(u_keep.at[b], us.at[b, r, :], sems.at[0, b])

    def store_g(b):
        return pltpu.make_async_copy(g_keep.at[b], gs.at[b, r, :], sems.at[1, b])

    def block(step, carry):
        b = BLOCKS - 1 - step
        u = (d[b, r, :] * gout[...].astype(jnp.float32)).astype(jnp.bfloat16)
        u_keep[b] = u
        store_u(b).start()
        low = dot(u, up[b]).astype(jnp.bfloat16)
        scaled, total = [], None
        for j in range(width // CHUNK):
            c = pl.ds(j * CHUNK, CHUNK)
            grad = dot(u, wd[b, c, :width], LAST_DIMS) + dot(low, wd[b, c, width:], LAST_DIMS)
            grad = grad * (1.0 + mod[b, pl.ds(m, 1), pl.ds(width + j * CHUNK, CHUNK)])
            scaled.append(grad)
            part = jnp.sum(grad * h[b, r, c], axis=1, keepdims=True)
            total = part if total is None else total + part
        centred = total * (1.0 / width)
        rms = inv[b, r, 0:1]
        for j in range(width // CHUNK):
            c = pl.ds(j * CHUNK, CHUNK)
            upstream = gout[:, c].astype(jnp.float32)
            value = (upstream + rms * (scaled[j] - h[b, r, c] * centred)).astype(jnp.bfloat16)
            gout[:, c] = value
            g_keep[b, :, c] = value
        store_g(b).start()
        return carry

    @pl.when(stage[0] == active_stage)
    def run():
        gout[...] = gin[...]
        lax.fori_loop(0, BLOCKS, block, 0)
        for b in range(BLOCKS):
            store_u(b).wait()
            store_g(b).wait()


VMEM = pl.BlockSpec(memory_space=pltpu.VMEM)
ANY = pl.BlockSpec(memory_space=pl.ANY)
SMEM = pl.BlockSpec(memory_space=pltpu.SMEM)


def resident(value):
    return pltpu.with_memory_space_constraint(value, pltpu.VMEM)


def per_device(block_inputs, target, frozen_weight, adapter_down, adapter_up, start_modulation, finish_modulation, level_pairs):
    stage = lax.axis_index("y")
    place = lax.axis_index("zh")
    tokens, width = block_inputs.shape[1:]
    rank = adapter_down.shape[2]
    share = tokens // BLOCKS
    batches = share // ROWS
    grad_scale = 1.0 / math.sqrt(tokens * MEMBERS)

    wd = jnp.concatenate([frozen_weight[0], adapter_down[0]], axis=1)
    wd = lax.all_gather(wd, PLANE, axis=0, tiled=True).reshape(BLOCKS, width, width + rank)
    up = lax.all_gather(adapter_up[0], PLANE, axis=0, tiled=True).reshape(BLOCKS, width, rank)

    own_mod = per_batch_modulation(start_modulation[0], finish_modulation[0], level_pairs)
    mod = lax.all_to_all(own_mod, "zh", 0, 0, tiled=True).reshape(BLOCKS, batches, 3 * width)
    x = lax.all_to_all(block_inputs[0], "zh", 0, 0, tiled=True).reshape(BLOCKS, share, width)

    own_target = lax.dynamic_slice_in_dim(target, place * share, share, 0)
    stage = stage.astype(jnp.int32).reshape(1)
    place = place.astype(jnp.int32).reshape(1)
    values = block_inputs[0].astype(jnp.float32)
    normed = values * lax.rsqrt(jnp.mean(values * values, axis=1, keepdims=True) + EPSILON)
    row_mod = jnp.repeat(own_mod[:, : 2 * width], ROWS, axis=0)
    modulated = (normed * (1.0 + row_mod[:, width:]) + row_mod[:, :width]).astype(jnp.bfloat16)
    gs = jnp.zeros((BLOCKS, share, width), jnp.bfloat16)
    us = jnp.zeros((BLOCKS, share, width), jnp.bfloat16)
    x, mod, stage, place, own_target, modulated, gs, us = lax.optimization_barrier(
        (x, mod, stage, place, own_target, modulated, gs, us)
    )
    wd_near, up_near, mod_near = resident(wd), resident(up), resident(mod)
    own_down, own_up, d, h, inv, *arrived = pl.pallas_call(
        functools.partial(forward_kernel, batches, width),
        out_shape=[
            jax.ShapeDtypeStruct((width, rank), wd.dtype),
            jax.ShapeDtypeStruct((width, rank), up.dtype),
            pltpu.VMEM((BLOCKS, share, width), jnp.float32),
            pltpu.VMEM((BLOCKS, share, width), jnp.float32),
            pltpu.VMEM((BLOCKS, share, rank), jnp.float32),
        ]
        + [pltpu.VMEM((ROWS, width), jnp.bfloat16)] * batches,
        in_specs=[SMEM] + [VMEM] * 3 + [ANY, VMEM],
        out_specs=[ANY] * 2 + [VMEM] * (3 + batches),
        scratch_shapes=[
            pltpu.VMEM((BLOCKS, width, rank), jnp.bfloat16),
            pltpu.VMEM((SLOTS, width, CHUNK), jnp.bfloat16),
            pltpu.SemaphoreType.DMA((2, BLOCKS)),
            pltpu.SemaphoreType.DMA((2,)),
        ],
        compiler_params=pltpu.CompilerParams(vmem_limit_bytes=16 * MIB),
        name="forward",
    )(place, x, mod_near, own_target, wd, up_near)

    d_near, h_near, inv_near = (resident(v) for v in (d, h, inv))
    for step in range(STAGES):
        for m in range(batches):
            gout, gs, us = pl.pallas_call(
                functools.partial(chain_kernel, STAGES - 1 - step, m, width),
                out_shape=[
                    jax.ShapeDtypeStruct((ROWS, width), jnp.bfloat16),
                    jax.ShapeDtypeStruct(gs.shape, gs.dtype),
                    jax.ShapeDtypeStruct(us.shape, us.dtype),
                ],
                in_specs=[SMEM] + [VMEM] * 7 + [ANY] * 2,
                out_specs=[VMEM, ANY, ANY],
                scratch_shapes=[
                    pltpu.VMEM((BLOCKS, ROWS, width), jnp.bfloat16),
                    pltpu.VMEM((BLOCKS, ROWS, width), jnp.bfloat16),
                    pltpu.SemaphoreType.DMA((2, BLOCKS)),
                ],
                input_output_aliases={8: 1, 9: 2},
                compiler_params=pltpu.CompilerParams(vmem_limit_bytes=8 * MIB),
                cost_estimate=pl.CostEstimate(flops=2 * BLOCKS * ROWS * width * width, bytes_accessed=4 * MIB, transcendentals=0),
                name="relay",
            )(stage, resident(arrived[m]), wd_near, up_near, d_near, h_near, mod_near, inv_near, gs, us)
            if step < STAGES - 1:
                arrived[m] = lax.ppermute(gout, "y", [(STAGES - 1 - step, STAGES - 2 - step)])

    gs, us, modulated, own_down, own_up = lax.optimization_barrier((gs, us, modulated, own_down, own_up))
    grads = lax.all_to_all(gs.reshape(tokens, width), "zh", 0, 0, tiled=True)
    own_pre = lax.all_to_all(us.reshape(tokens, width), "zh", 0, 0, tiled=True)

    lowrank = dot(modulated, own_down).astype(jnp.bfloat16)
    grad_low = dot(own_pre, own_up).astype(jnp.bfloat16)
    down_part = dot(modulated, grad_low, FIRST_DIMS).astype(jnp.bfloat16)
    up_part = dot(own_pre, lowrank, FIRST_DIMS).astype(jnp.bfloat16)
    owned = width // MEMBERS
    parts = jnp.concatenate([down_part.reshape(MEMBERS, owned, rank), up_part.reshape(MEMBERS, owned, rank)], axis=1)
    parts = lax.all_to_all(parts, GROUP, 0, 0, tiled=True)
    total = jnp.sum(parts.astype(jnp.float32), axis=0) * grad_scale
    return grads[None], total[None, :owned], total[None, owned:]


def solution(mesh):
    split = Mesh(mesh.devices.reshape(SIZES), AXES)
    blocks = ("y", "zh")
    return jax.shard_map(
        per_device,
        mesh=split,
        in_specs=(
            P(blocks, GROUP, None),
            P(GROUP, None),
            P(blocks, GROUP, None),
            P(blocks, GROUP, None),
            P(blocks, GROUP, None),
            P(blocks, None, None),
            P(blocks, None, None),
            P(GROUP, None),
        ),
        out_specs=(P(blocks, GROUP, None), P(blocks, GROUP, None), P(blocks, GROUP, None)),
        check_vma=False,
    )
```

```python
import functools
import math

import jax
import jax.numpy as jnp
from jax import lax
from jax.experimental import pallas as pl
from jax.experimental.pallas import tpu as pltpu
from jax.sharding import Mesh, PartitionSpec as P

EPSILON = 1e-06
AXES = ("y", "zh", "zl", "x", "c")
SIZES = (8, 4, 2, 4, 2)
STAGES, BLOCKS, CORES = SIZES[0], SIZES[1], SIZES[4]
GROUP = ("zl", "x", "c")
CHIPS = ("zl", "x")
PLANE = ("zh", "zl", "x", "c")
MEMBERS = 16
ROWS = 32
CHUNK = 512
SLOTS = 4
ROW_DOT = (((1,), (0,)), ((), ()))
LAST_DIMS = (((1,), (1,)), ((), ()))
FIRST_DIMS = (((0,), (0,)), ((), ()))
SLOPE = math.sqrt(2.0 / math.pi)
CUBIC = 0.044715
MIB = 2**20


def dot(left, right, dims=ROW_DOT):
    return lax.dot_general(left, right, dims, preferred_element_type=jnp.float32)


def per_batch_modulation(from_table, to_table, level_pairs):
    ladder = jnp.arange(from_table.shape[0], dtype=jnp.int32)[None, :]
    hot_from = (level_pairs[:, 0:1] == ladder).astype(jnp.bfloat16)
    hot_to = (level_pairs[:, 1:2] == ladder).astype(jnp.bfloat16)
    return dot(hot_from, from_table) + dot(hot_to, to_table)


def slab_kernel(width, rank, weight, down, up, slab):
    slab[:width, :] = weight[...].T
    slab[width : width + rank, :] = down[...].T
    slab[width + rank :, :] = up[...]


def forward_kernel(batches, width, rank, place, x, mod, target, slabs, own, d, h, inv, *rest):
    seeds, (adapters, columns, sems) = rest[:batches], rest[3 * batches :]
    own_copy = pltpu.make_async_copy(slabs.at[place[0], :, width:, :], own, sems.at[0, BLOCKS])
    chunks = width // CHUNK
    total = BLOCKS * chunks
    per_chunk = CHUNK // slabs.shape[3]

    def fetch_adapters(b):
        return pltpu.make_async_copy(slabs.at[b, :, width:, :], adapters.at[b], sems.at[0, b])

    def fetch_columns(index):
        b, j, slot = BLOCKS - 1 - index // chunks, index % chunks, index % SLOTS
        return pltpu.make_async_copy(slabs.at[b, :, pl.ds(j * CHUNK, CHUNK), :], columns.at[slot], sems.at[1, slot])

    fetch_adapters(BLOCKS - 1).start()
    for ahead in range(SLOTS):
        fetch_columns(ahead).start()
    for other in reversed(range(BLOCKS - 1)):
        fetch_adapters(other).start()
    own_copy.start()
    for index in range(total):
        b, j = BLOCKS - 1 - index // chunks, index % chunks
        if j == 0:
            pieces = []
            for m in range(batches):
                r = pl.ds(m * ROWS, ROWS)
                values = x[b, r, :].astype(jnp.float32)
                rms = lax.rsqrt(jnp.mean(values * values, axis=1, keepdims=True) + EPSILON)
                normed = values * rms
                h[b, r, :] = normed
                inv[b, r, :] = jnp.broadcast_to(rms, (ROWS, inv.shape[2]))
                shift = mod[b, pl.ds(m, 1), 0:width]
                scale = mod[b, pl.ds(m, 1), width : 2 * width]
                pieces.append((normed * (1.0 + scale) + shift).astype(jnp.bfloat16))
            modulated = jnp.concatenate(pieces, axis=0)
            fetch_adapters(b).wait()
            down = jnp.concatenate([adapters[b, i, :rank, :] for i in range(MEMBERS)], axis=1)
            low = dot(modulated, down, LAST_DIMS).astype(jnp.bfloat16)
        c = pl.ds(j * CHUNK, CHUNK)
        fetch_columns(index).wait()
        slot = index % SLOTS
        up = jnp.concatenate([adapters[b, j * per_chunk + i, rank:, :] for i in range(per_chunk)], axis=0)
        weight = jnp.concatenate([columns[slot, i] for i in range(MEMBERS)], axis=1)
        pre = dot(modulated, weight, LAST_DIMS) + dot(low, up, LAST_DIMS)
        if index + SLOTS < total:
            fetch_columns(index + SLOTS).start()
        squared = pre * pre
        bent = jnp.tanh(SLOPE * pre * (1.0 + CUBIC * squared))
        half = 0.5 * (1.0 + bent)
        slope = half + 0.5 * pre * (1.0 - bent * bent) * (SLOPE * (1.0 + 3.0 * CUBIC * squared))
        for m in range(batches):
            s = slice(m * ROWS, (m + 1) * ROWS)
            gate = mod[b, pl.ds(m, 1), pl.ds(2 * width + j * CHUNK, CHUNK)]
            d[b, s, c] = slope[s] * gate
            if b == BLOCKS - 1:
                out = x[b, s, c].astype(jnp.float32) + gate * (pre[s] * half[s])
                seeds[m][:, c] = (out - target[s, c].astype(jnp.float32)).astype(jnp.bfloat16)
    own_copy.wait()


def relay_kernel(active_stage, m, width, rank, stage, gin, slabs, d, h, mod, inv, gs_in, us_in, gout, gs, us, g_keep, u_keep, sems):
    r = pl.ds(m * ROWS, ROWS)
    owned = slabs.shape[3]

    def store_u(b):
        return pltpu.make_async_copy(u_keep.at[b], us.at[b], sems.at[0, b])

    def store_g(b):
        return pltpu.make_async_copy(g_keep.at[b], gs.at[b], sems.at[1, b])

    def block(step, carry):
        b = BLOCKS - 1 - step
        u = (d[b, r, :] * gout[...].astype(jnp.float32)).astype(jnp.bfloat16)
        u_keep[b] = u
        store_u(b).start()
        up = jnp.concatenate([slabs[b, i, width + rank :, :] for i in range(MEMBERS)], axis=0)
        low = dot(u, up).astype(jnp.bfloat16)
        joined = jnp.concatenate([u, low], axis=1)
        scaled, total = [], None
        for i in range(MEMBERS):
            c = pl.ds(i * owned, owned)
            grad = dot(joined, slabs[b, i, : width + rank, :])
            grad = grad * (1.0 + mod[b, pl.ds(m, 1), pl.ds(width + i * owned, owned)])
            scaled.append(grad)
            part = grad * h[b, r, c]
            total = part if total is None else total + part
        centred = jnp.sum(total, axis=1, keepdims=True) * (1.0 / width)
        rms = inv[b, r, :]
        for i in range(MEMBERS):
            c = pl.ds(i * owned, owned)
            value = gout[:, c].astype(jnp.float32) + rms * (scaled[i] - h[b, r, c] * centred)
            value = value.astype(jnp.bfloat16)
            gout[:, c] = value
            g_keep[b, :, c] = value
        store_g(b).start()
        return carry

    @pl.when(stage[0] == active_stage)
    def run():
        gout[...] = gin[...]
        lax.fori_loop(0, BLOCKS, block, 0)
        for b in range(BLOCKS):
            store_u(b).wait()
            store_g(b).wait()


def grads_kernel(rank, core, own, *refs):
    count = (len(refs) - 2) // 2
    pres, mixes, (mine, theirs) = refs[:count], refs[count : 2 * count], refs[2 * count :]
    down = jnp.concatenate([own[i, :rank, :] for i in range(MEMBERS)], axis=1)
    up = jnp.concatenate([own[i, rank:, :] for i in range(MEMBERS)], axis=0)
    pre = jnp.concatenate([ref[...] for ref in pres], axis=0)
    mixed = jnp.concatenate([ref[...] for ref in mixes], axis=0)
    lowrank = dot(mixed, down, LAST_DIMS).astype(jnp.bfloat16)
    grad_low = dot(pre, up).astype(jnp.bfloat16)
    owned = own.shape[2]
    for row, (left, right) in ((0, (grad_low, mixed)), (rank, (lowrank, pre))):
        part = dot(left.T, right).astype(jnp.bfloat16)
        for i in range(MEMBERS // CORES):
            pair = [part[:, (CORES * i + c) * owned : (CORES * i + c + 1) * owned] for c in range(CORES)]
            mine[i, row : row + rank, :] = jnp.where(core[0] == 0, pair[0], pair[1])
            theirs[i, row : row + rank, :] = jnp.where(core[0] == 0, pair[1], pair[0])


def total_kernel(rank, scale, parts, down, up):
    total = jnp.sum(parts[...].astype(jnp.float32), axis=0) * scale
    down[0] = total[:rank, :].T
    up[0] = total[rank:, :].T


VMEM = pl.BlockSpec(memory_space=pltpu.VMEM)
ANY = pl.BlockSpec(memory_space=pl.ANY)
HBM = pl.BlockSpec(memory_space=pltpu.HBM)
SMEM = pl.BlockSpec(memory_space=pltpu.SMEM)


def resident(value):
    return pltpu.with_memory_space_constraint(value, pltpu.VMEM)


def far(value):
    return pltpu.with_memory_space_constraint(value, pltpu.HBM)


def per_device(block_inputs, target, frozen_weight, adapter_down, adapter_up, start_modulation, finish_modulation, level_pairs):
    stage = lax.axis_index("y")
    place = lax.axis_index("zh")
    core = lax.axis_index("c")
    tokens, width = block_inputs.shape[1:]
    owned, rank = adapter_down.shape[1:]
    share = tokens // BLOCKS
    batches = share // ROWS
    grad_scale = 1.0 / math.sqrt(tokens * MEMBERS)

    slab = pl.pallas_call(
        functools.partial(slab_kernel, width, rank),
        out_shape=jax.ShapeDtypeStruct((width + 2 * rank, owned), jnp.bfloat16),
        in_specs=[VMEM] * 3,
        out_specs=VMEM,
        name="slab",
    )(frozen_weight[0], adapter_down[0], adapter_up[0])
    slabs = lax.all_gather(slab, PLANE, axis=0, tiled=True)
    slabs = slabs.reshape(BLOCKS, MEMBERS, width + 2 * rank, owned)

    own_mod = per_batch_modulation(start_modulation[0], finish_modulation[0], level_pairs)
    mod = lax.all_to_all(own_mod, "zh", 0, 0, tiled=True).reshape(BLOCKS, batches, 3 * width)
    x = lax.all_to_all(block_inputs[0], "zh", 0, 0, tiled=True).reshape(BLOCKS, share, width)
    own_target = lax.dynamic_slice_in_dim(target, place * share, share, 0)

    values = block_inputs[0].astype(jnp.float32)
    normed = values * lax.rsqrt(jnp.mean(values * values, axis=1, keepdims=True) + EPSILON)
    row_mod = jnp.repeat(own_mod[:, : 2 * width], ROWS, axis=0)
    modulated = (normed * (1.0 + row_mod[:, width:]) + row_mod[:, :width]).astype(jnp.bfloat16)
    modulated = modulated.reshape(BLOCKS, batches, ROWS, width)
    modulated = [modulated[:, m].reshape(BLOCKS * ROWS, width) for m in range(batches)]
    stage, place, core = (index.astype(jnp.int32).reshape(1) for index in (stage, place, core))
    x, mod, stage, place, core, own_target, modulated = lax.optimization_barrier(
        (x, mod, stage, place, core, own_target, modulated)
    )

    slabs_near, mod_near = resident(slabs), resident(mod)
    own, d, h, inv, *rest = pl.pallas_call(
        functools.partial(forward_kernel, batches, width, rank),
        out_shape=[
            jax.ShapeDtypeStruct((MEMBERS, 2 * rank, owned), jnp.bfloat16),
            pltpu.VMEM((BLOCKS, share, width), jnp.float32),
            pltpu.VMEM((BLOCKS, share, width), jnp.float32),
            pltpu.VMEM((BLOCKS, share, owned), jnp.float32),
        ]
        + [pltpu.VMEM((ROWS, width), jnp.bfloat16)] * batches
        + [pltpu.HBM((BLOCKS, ROWS, width), jnp.bfloat16)] * (2 * batches),
        in_specs=[SMEM] + [VMEM] * 3 + [ANY],
        out_specs=[ANY] + [VMEM] * (3 + batches) + [HBM] * (2 * batches),
        scratch_shapes=[
            pltpu.VMEM((BLOCKS, MEMBERS, 2 * rank, owned), jnp.bfloat16),
            pltpu.VMEM((SLOTS, MEMBERS, CHUNK, owned), jnp.bfloat16),
            pltpu.SemaphoreType.DMA((2, BLOCKS + 1)),
        ],
        compiler_params=pltpu.CompilerParams(vmem_limit_bytes=16 * MIB),
        cost_estimate=pl.CostEstimate(flops=2 * BLOCKS * share * width * width, bytes_accessed=40 * MIB, transcendentals=0),
        name="forward",
    )(place, x, mod_near, own_target, slabs)

    d_near, h_near, inv_near = (resident(v) for v in (d, h, inv))
    arrived, gs, us = rest[:batches], rest[batches : 2 * batches], rest[2 * batches :]
    for step in range(STAGES):
        for m in range(batches):
            gout, gs[m], us[m] = pl.pallas_call(
                functools.partial(relay_kernel, STAGES - 1 - step, m, width, rank),
                out_shape=[pltpu.VMEM((ROWS, width), jnp.bfloat16)]
                + [pltpu.HBM((BLOCKS, ROWS, width), jnp.bfloat16)] * 2,
                in_specs=[SMEM] + [VMEM] * 6 + [HBM] * 2,
                out_specs=[VMEM] + [HBM] * 2,
                scratch_shapes=[
                    pltpu.VMEM((BLOCKS, ROWS, width), jnp.bfloat16),
                    pltpu.VMEM((BLOCKS, ROWS, width), jnp.bfloat16),
                    pltpu.SemaphoreType.DMA((2, BLOCKS)),
                ],
                input_output_aliases={7: 1, 8: 2},
                compiler_params=pltpu.CompilerParams(vmem_limit_bytes=4 * MIB),
                cost_estimate=pl.CostEstimate(flops=2 * BLOCKS * ROWS * width * width, bytes_accessed=4 * MIB, transcendentals=0),
                name="relay",
            )(stage, resident(arrived[m]), slabs_near, d_near, h_near, mod_near, inv_near, far(gs[m]), far(us[m]))
            if step < STAGES - 1:
                arrived[m] = lax.ppermute(gout, "y", [(STAGES - 1 - step, STAGES - 2 - step)])

    own_pre = [lax.all_to_all(u, "zh", 0, 0, tiled=True).reshape(BLOCKS * ROWS, width) for u in us]
    grads = [lax.all_to_all(g, "zh", 0, 0, tiled=True) for g in gs]
    grads = jnp.stack(grads, axis=1).reshape(tokens, width)

    half = MEMBERS // CORES
    mine, theirs = pl.pallas_call(
        functools.partial(grads_kernel, rank),
        out_shape=[jax.ShapeDtypeStruct((half, 2 * rank, owned), jnp.bfloat16)] * 2,
        in_specs=[SMEM] + [VMEM] * (1 + 2 * batches),
        out_specs=[VMEM] * 2,
        compiler_params=pltpu.CompilerParams(vmem_limit_bytes=16 * MIB),
        name="grads",
    )(core, own, *own_pre, *modulated)
    theirs = lax.ppermute(theirs, "c", [(0, 1), (1, 0)])
    parts = (mine.astype(jnp.float32) + theirs.astype(jnp.float32)).astype(jnp.bfloat16)
    parts = lax.all_to_all(parts, CHIPS, 0, 0, tiled=True)
    down_grad, up_grad = pl.pallas_call(
        functools.partial(total_kernel, rank, grad_scale),
        out_shape=[jax.ShapeDtypeStruct((1, owned, rank), jnp.float32)] * 2,
        in_specs=[VMEM],
        out_specs=[VMEM] * 2,
        name="total",
    )(parts)
    return grads[None], down_grad, up_grad


def solution(mesh):
    split = Mesh(mesh.devices.reshape(SIZES), AXES)
    blocks = ("y", "zh")
    return jax.shard_map(
        per_device,
        mesh=split,
        in_specs=(
            P(blocks, GROUP, None),
            P(GROUP, None),
            P(blocks, GROUP, None),
            P(blocks, GROUP, None),
            P(blocks, GROUP, None),
            P(blocks, None, None),
            P(blocks, None, None),
            P(GROUP, None),
        ),
        out_specs=(P(blocks, GROUP, None), P(blocks, GROUP, None), P(blocks, GROUP, None)),
        check_vma=False,
    )
```

```python
import functools
import math

import jax
import jax.numpy as jnp
from jax import lax
from jax.experimental import pallas as pl
from jax.experimental.pallas import tpu as pltpu
from jax.sharding import Mesh, PartitionSpec as P

EPSILON = 1e-06
AXES = ("y", "zh", "zl", "x", "c")
SIZES = (8, 4, 2, 4, 2)
STAGES, BLOCKS, CORES = SIZES[0], SIZES[1], SIZES[4]
GROUP = ("zl", "x", "c")
CHIPS = ("zl", "x")
PLANE = ("zh", "zl", "x", "c")
MEMBERS = 16
ROWS = 32
CHUNK = 512
PIECES = 4
ROW_DOT = (((1,), (0,)), ((), ()))
LAST_DIMS = (((1,), (1,)), ((), ()))
FIRST_DIMS = (((0,), (0,)), ((), ()))
SLOPE = math.sqrt(2.0 / math.pi)
CUBIC = 0.044715
MIB = 2**20


def dot(left, right, dims=ROW_DOT):
    return lax.dot_general(left, right, dims, preferred_element_type=jnp.float32)


def per_batch_modulation(from_table, to_table, level_pairs):
    ladder = jnp.arange(from_table.shape[0], dtype=jnp.int32)[None, :]
    hot_from = (level_pairs[:, 0:1] == ladder).astype(jnp.bfloat16)
    hot_to = (level_pairs[:, 1:2] == ladder).astype(jnp.bfloat16)
    return dot(hot_from, from_table) + dot(hot_to, to_table)


def slab_kernel(width, rank, weight, down, up, slab):
    slab[:width, :] = weight[...].T
    slab[width : width + rank, :] = down[...].T
    slab[width + rank :, :] = up[...]


def relay_block(b, batches, width, rank, rows, slab, g, d, h, mod, inv, g_keep, u_keep):
    owned = slab(0).shape[1]
    u = (d[b, rows, :] * g[...].astype(jnp.float32)).astype(jnp.bfloat16)
    u_keep[b] = u
    up = jnp.concatenate([slab(i)[width + rank :, :] for i in range(MEMBERS)], axis=0)
    low = dot(u, up).astype(jnp.bfloat16)
    joined = jnp.concatenate([u, low], axis=1)
    scaled, total = [], None
    for i in range(MEMBERS):
        c = pl.ds(i * owned, owned)
        grad = dot(joined, slab(i)[: width + rank, :])
        scale = [1.0 + mod[b, pl.ds(m, 1), pl.ds(width + i * owned, owned)] for m in batches]
        pieces = [grad[n * ROWS : (n + 1) * ROWS] * scale[n] for n in range(len(batches))]
        grad = pieces[0] if len(pieces) == 1 else jnp.concatenate(pieces, axis=0)
        scaled.append(grad)
        part = grad * h[b, rows, c]
        total = part if total is None else total + part
    centred = jnp.sum(total, axis=1, keepdims=True) * (1.0 / width)
    rms = inv[b, rows, :]
    for i in range(MEMBERS):
        c = pl.ds(i * owned, owned)
        value = g[:, c].astype(jnp.float32) + rms * (scaled[i] - h[b, rows, c] * centred)
        value = value.astype(jnp.bfloat16)
        g[:, c] = value
        g_keep[b, :, c] = value


def first_kernel(
    batches, width, rank, stage, place, x, mod, target, slabs, own, d, h, inv, gs, us, *rest
):
    gouts, (g, g_keep, u_keep, near, fetched, stored) = rest[:batches], rest[batches:]
    share = batches * ROWS
    per_chunk = CHUNK // slabs.shape[3]
    quarter = MEMBERS // PIECES
    own_copy = pltpu.make_async_copy(slabs.at[place[0], :, width:, :], own, stored.at[2, 0])

    def fetch(step, piece):
        members = pl.ds(piece * quarter, quarter)
        slot = lax.rem(step, 2)
        return pltpu.make_async_copy(
            slabs.at[BLOCKS - 1 - step, members], near.at[slot, members], fetched.at[slot, piece]
        )

    def store_u(b):
        return pltpu.make_async_copy(u_keep.at[b], us.at[b], stored.at[0, b])

    def store_g(b):
        return pltpu.make_async_copy(g_keep.at[b], gs.at[b], stored.at[1, b])

    def block(step, carry):
        b = BLOCKS - 1 - step
        slot = lax.rem(step, 2)
        for piece in range(PIECES):
            fetch(step, piece).wait()

        @pl.when(step < BLOCKS - 1)
        def ahead():
            for piece in range(PIECES):
                fetch(step + 1, piece).start()

        def slab(i):
            return near.at[slot, i]

        pieces = []
        for m in range(batches):
            r = pl.ds(m * ROWS, ROWS)
            values = x[b, r, :].astype(jnp.float32)
            rms = lax.rsqrt(jnp.mean(values * values, axis=1, keepdims=True) + EPSILON)
            normed = values * rms
            h[b, r, :] = normed
            inv[b, r, :] = jnp.broadcast_to(rms, (ROWS, inv.shape[2]))
            shift = mod[b, pl.ds(m, 1), 0:width]
            scale = mod[b, pl.ds(m, 1), width : 2 * width]
            pieces.append((normed * (1.0 + scale) + shift).astype(jnp.bfloat16))
        modulated = jnp.concatenate(pieces, axis=0)
        down = jnp.concatenate([slab(i)[width : width + rank, :] for i in range(MEMBERS)], axis=1)
        low = dot(modulated, down, LAST_DIMS).astype(jnp.bfloat16)
        for j in range(width // CHUNK):
            c = pl.ds(j * CHUNK, CHUNK)
            up = jnp.concatenate([slab(j * per_chunk + i)[width + rank :, :] for i in range(per_chunk)], axis=0)
            weight = jnp.concatenate([slab(i)[c, :] for i in range(MEMBERS)], axis=1)
            pre = dot(modulated, weight, LAST_DIMS) + dot(low, up, LAST_DIMS)
            squared = pre * pre
            bent = jnp.tanh(SLOPE * pre * (1.0 + CUBIC * squared))
            half = 0.5 * (1.0 + bent)
            slope = half + 0.5 * pre * (1.0 - bent * bent) * (SLOPE * (1.0 + 3.0 * CUBIC * squared))
            gate = [mod[b, pl.ds(m, 1), pl.ds(2 * width + j * CHUNK, CHUNK)] for m in range(batches)]
            for m in range(batches):
                s = slice(m * ROWS, (m + 1) * ROWS)
                d[b, s, c] = slope[s] * gate[m]

            @pl.when(step == 0)
            def close():
                for m in range(batches):
                    s = slice(m * ROWS, (m + 1) * ROWS)
                    out = x[b, s, c].astype(jnp.float32) + gate[m] * (pre[s] * half[s])
                    g[s, c] = (out - target[s, c].astype(jnp.float32)).astype(jnp.bfloat16)

        @pl.when(stage[0] == STAGES - 1)
        def relay():
            relay_block(
                b, range(batches), width, rank, pl.ds(0, share), slab, g, d, h, mod, inv, g_keep, u_keep
            )
            store_u(b).start()
            store_g(b).start()

        return carry

    for piece in range(PIECES):
        fetch(0, piece).start()
    own_copy.start()
    lax.fori_loop(0, BLOCKS, block, 0)
    own_copy.wait()
    for m in range(batches):
        gouts[m][...] = g[m * ROWS : (m + 1) * ROWS, :]

    @pl.when(stage[0] == STAGES - 1)
    def finish():
        for b in range(BLOCKS):
            store_u(b).wait()
            store_g(b).wait()


def relay_kernel(
    active_stage, m, width, rank, stage, gin, slabs, d, h, mod, inv, gs_in, us_in, gout, gs, us, g_keep, u_keep, stored
):
    rows = pl.ds(m * ROWS, ROWS)

    def store_u(b):
        return pltpu.make_async_copy(u_keep.at[b], us.at[b, rows, :], stored.at[0, b])

    def store_g(b):
        return pltpu.make_async_copy(g_keep.at[b], gs.at[b, rows, :], stored.at[1, b])

    def block(step, carry):
        b = BLOCKS - 1 - step
        relay_block(
            b, [m], width, rank, rows, lambda i: slabs.at[b, i], gout, d, h, mod, inv, g_keep, u_keep
        )
        store_u(b).start()
        store_g(b).start()
        return carry

    @pl.when(stage[0] == active_stage)
    def run():
        gout[...] = gin[...]
        lax.fori_loop(0, BLOCKS, block, 0)
        for b in range(BLOCKS):
            store_u(b).wait()
            store_g(b).wait()


def grads_kernel(rank, core, own, pre_ref, mixed_ref, mine, theirs):
    down = jnp.concatenate([own[i, :rank, :] for i in range(MEMBERS)], axis=1)
    up = jnp.concatenate([own[i, rank:, :] for i in range(MEMBERS)], axis=0)
    pre, mixed = pre_ref[...], mixed_ref[...]
    lowrank = dot(mixed, down, LAST_DIMS).astype(jnp.bfloat16)
    grad_low = dot(pre, up).astype(jnp.bfloat16)
    owned = own.shape[2]
    for row, (left, right) in ((0, (grad_low, mixed)), (rank, (lowrank, pre))):
        part = dot(left.T, right).astype(jnp.bfloat16)
        for i in range(MEMBERS // CORES):
            pair = [part[:, (CORES * i + c) * owned : (CORES * i + c + 1) * owned] for c in range(CORES)]
            mine[i, row : row + rank, :] = jnp.where(core[0] == 0, pair[0], pair[1])
            theirs[i, row : row + rank, :] = jnp.where(core[0] == 0, pair[1], pair[0])


def total_kernel(rank, scale, parts, down, up):
    total = jnp.sum(parts[...].astype(jnp.float32), axis=0) * scale
    down[0] = total[:rank, :].T
    up[0] = total[rank:, :].T


VMEM = pl.BlockSpec(memory_space=pltpu.VMEM)
ANY = pl.BlockSpec(memory_space=pl.ANY)
HBM = pl.BlockSpec(memory_space=pltpu.HBM)
SMEM = pl.BlockSpec(memory_space=pltpu.SMEM)


def resident(value):
    return pltpu.with_memory_space_constraint(value, pltpu.VMEM)


def far(value):
    return pltpu.with_memory_space_constraint(value, pltpu.HBM)


def per_device(block_inputs, target, frozen_weight, adapter_down, adapter_up, start_modulation, finish_modulation, level_pairs):
    stage = lax.axis_index("y")
    place = lax.axis_index("zh")
    core = lax.axis_index("c")
    tokens, width = block_inputs.shape[1:]
    owned, rank = adapter_down.shape[1:]
    share = tokens // BLOCKS
    batches = share // ROWS
    grad_scale = 1.0 / math.sqrt(tokens * MEMBERS)

    slab = pl.pallas_call(
        functools.partial(slab_kernel, width, rank),
        out_shape=jax.ShapeDtypeStruct((width + 2 * rank, owned), jnp.bfloat16),
        in_specs=[VMEM] * 3,
        out_specs=VMEM,
        name="slab",
    )(frozen_weight[0], adapter_down[0], adapter_up[0])
    slabs = lax.all_gather(slab, PLANE, axis=0, tiled=True)
    slabs = slabs.reshape(BLOCKS, MEMBERS, width + 2 * rank, owned)

    own_mod = per_batch_modulation(start_modulation[0], finish_modulation[0], level_pairs)
    mod = lax.all_to_all(own_mod, "zh", 0, 0, tiled=True).reshape(BLOCKS, batches, 3 * width)
    x = lax.all_to_all(block_inputs[0], "zh", 0, 0, tiled=True).reshape(BLOCKS, share, width)
    own_target = lax.dynamic_slice_in_dim(target, place * share, share, 0)

    values = block_inputs[0].astype(jnp.float32)
    normed = values * lax.rsqrt(jnp.mean(values * values, axis=1, keepdims=True) + EPSILON)
    row_mod = jnp.repeat(own_mod[:, : 2 * width], ROWS, axis=0)
    modulated = (normed * (1.0 + row_mod[:, width:]) + row_mod[:, :width]).astype(jnp.bfloat16)
    stage, place, core = (index.astype(jnp.int32).reshape(1) for index in (stage, place, core))
    x, mod, stage, place, core, own_target, modulated = lax.optimization_barrier(
        (x, mod, stage, place, core, own_target, modulated)
    )

    slabs_near, mod_near = resident(slabs), resident(mod)
    kept_shape = (BLOCKS, share, width)
    own, d, h, inv, gs, us, *sent = pl.pallas_call(
        functools.partial(first_kernel, batches, width, rank),
        out_shape=[
            jax.ShapeDtypeStruct((MEMBERS, 2 * rank, owned), jnp.bfloat16),
            pltpu.VMEM(kept_shape, jnp.float32),
            pltpu.VMEM(kept_shape, jnp.float32),
            pltpu.VMEM((BLOCKS, share, owned), jnp.float32),
            pltpu.HBM(kept_shape, jnp.bfloat16),
            pltpu.HBM(kept_shape, jnp.bfloat16),
        ]
        + [pltpu.VMEM((ROWS, width), jnp.bfloat16)] * batches,
        in_specs=[SMEM] * 2 + [VMEM] * 3 + [HBM],
        out_specs=[ANY] + [VMEM] * 3 + [HBM] * 2 + [VMEM] * batches,
        scratch_shapes=[
            pltpu.VMEM((share, width), jnp.bfloat16),
            pltpu.VMEM(kept_shape, jnp.bfloat16),
            pltpu.VMEM(kept_shape, jnp.bfloat16),
            pltpu.VMEM((2,) + slabs.shape[1:], jnp.bfloat16),
            pltpu.SemaphoreType.DMA((2, PIECES)),
            pltpu.SemaphoreType.DMA((3, BLOCKS)),
        ],
        compiler_params=pltpu.CompilerParams(vmem_limit_bytes=26 * MIB),
        cost_estimate=pl.CostEstimate(flops=4 * BLOCKS * share * width * width, bytes_accessed=40 * MIB, transcendentals=0),
        name="first",
    )(stage, place, x, mod_near, own_target, far(slabs))

    d_near, h_near, inv_near = (resident(v) for v in (d, h, inv))

    def relay(active_stage, m, gin, gs, us):
        return pl.pallas_call(
            functools.partial(relay_kernel, active_stage, m, width, rank),
            out_shape=[pltpu.VMEM((ROWS, width), jnp.bfloat16)] + [pltpu.HBM(kept_shape, jnp.bfloat16)] * 2,
            in_specs=[SMEM] + [VMEM] * 6 + [HBM] * 2,
            out_specs=[VMEM] + [HBM] * 2,
            scratch_shapes=[
                pltpu.VMEM((BLOCKS, ROWS, width), jnp.bfloat16),
                pltpu.VMEM((BLOCKS, ROWS, width), jnp.bfloat16),
                pltpu.SemaphoreType.DMA((2, BLOCKS)),
            ],
            input_output_aliases={7: 1, 8: 2},
            compiler_params=pltpu.CompilerParams(vmem_limit_bytes=4 * MIB),
            cost_estimate=pl.CostEstimate(flops=2 * BLOCKS * ROWS * width * width, bytes_accessed=4 * MIB, transcendentals=0),
            name="relay",
        )(stage, resident(gin), slabs_near, d_near, h_near, mod_near, inv_near, far(gs), far(us))

    _, gs, us = relay(STAGES, 0, sent[0], gs, us)
    for step in range(1, STAGES):
        arrived = [lax.ppermute(out, "y", [(STAGES - step, STAGES - 1 - step)]) for out in sent]
        sent = []
        for m in range(batches):
            gout, gs, us = relay(STAGES - 1 - step, m, arrived[m], gs, us)
            sent.append(gout)

    gs, us, modulated = lax.optimization_barrier((gs, us, modulated))
    own_pre = lax.all_to_all(us.reshape(tokens, width), "zh", 0, 0, tiled=True)
    half = MEMBERS // CORES
    mine, theirs = pl.pallas_call(
        functools.partial(grads_kernel, rank),
        out_shape=[jax.ShapeDtypeStruct((half, 2 * rank, owned), jnp.bfloat16)] * 2,
        in_specs=[SMEM] + [VMEM] * 3,
        out_specs=[VMEM] * 2,
        compiler_params=pltpu.CompilerParams(vmem_limit_bytes=16 * MIB),
        name="grads",
    )(core, own, own_pre, modulated)
    theirs = lax.ppermute(theirs, "c", [(0, 1), (1, 0)])
    parts = (mine.astype(jnp.float32) + theirs.astype(jnp.float32)).astype(jnp.bfloat16)
    parts, gs = lax.optimization_barrier((parts, gs))
    grads = lax.all_to_all(gs.reshape(tokens, width), "zh", 0, 0, tiled=True)
    parts = lax.all_to_all(parts, CHIPS, 0, 0, tiled=True)
    down_grad, up_grad = pl.pallas_call(
        functools.partial(total_kernel, rank, grad_scale),
        out_shape=[jax.ShapeDtypeStruct((1, owned, rank), jnp.float32)] * 2,
        in_specs=[VMEM],
        out_specs=[VMEM] * 2,
        name="total",
    )(parts)
    return grads[None], down_grad, up_grad


def solution(mesh):
    split = Mesh(mesh.devices.reshape(SIZES), AXES)
    blocks = ("y", "zh")
    return jax.shard_map(
        per_device,
        mesh=split,
        in_specs=(
            P(blocks, GROUP, None),
            P(GROUP, None),
            P(blocks, GROUP, None),
            P(blocks, GROUP, None),
            P(blocks, GROUP, None),
            P(blocks, None, None),
            P(blocks, None, None),
            P(GROUP, None),
        ),
        out_specs=(P(blocks, GROUP, None), P(blocks, GROUP, None), P(blocks, GROUP, None)),
        check_vma=False,
    )
```

```python
import functools
import math

import jax
import jax.numpy as jnp
from jax import lax
from jax.experimental import pallas as pl
from jax.experimental.pallas import tpu as pltpu
from jax.sharding import Mesh, PartitionSpec as P

EPSILON = 1e-06
AXES = ("y", "zh", "zl", "x", "c")
SIZES = (8, 4, 2, 4, 2)
STAGES, BLOCKS, CORES = SIZES[0], SIZES[1], SIZES[4]
GROUP = ("zl", "x", "c")
CHIPS = ("zl", "x")
PLANE = ("zh", "zl", "x", "c")
MEMBERS = 16
ROWS = 32
CHUNK = 512
PIECES = 4
ROW_DOT = (((1,), (0,)), ((), ()))
LAST_DIMS = (((1,), (1,)), ((), ()))
FIRST_DIMS = (((0,), (0,)), ((), ()))
SLOPE = math.sqrt(2.0 / math.pi)
CUBIC = 0.044715
MIB = 2**20


def dot(left, right, dims=ROW_DOT):
    return lax.dot_general(left, right, dims, preferred_element_type=jnp.float32)


def per_batch_modulation(from_table, to_table, level_pairs):
    ladder = jnp.arange(from_table.shape[0], dtype=jnp.int32)[None, :]
    hot_from = (level_pairs[:, 0:1] == ladder).astype(jnp.bfloat16)
    hot_to = (level_pairs[:, 1:2] == ladder).astype(jnp.bfloat16)
    return dot(hot_from, from_table) + dot(hot_to, to_table)


def slab_kernel(width, rank, weight, down, up, slab):
    slab[:width, :] = weight[...].T
    slab[width : width + rank, :] = down[...].T
    slab[width + rank :, :] = up[...]


def relay_block(b, batches, width, rank, rows, slab, g, d, h, mod, inv, g_keep, u_keep):
    owned = slab(0).shape[1]
    u = (d[b, rows, :] * g[...].astype(jnp.float32)).astype(jnp.bfloat16)
    u_keep[b] = u
    up = jnp.concatenate([slab(i)[width + rank :, :] for i in range(MEMBERS)], axis=0)
    low = dot(u, up).astype(jnp.bfloat16)
    joined = jnp.concatenate([u, low], axis=1)
    scaled, total = [], None
    for i in range(MEMBERS):
        c = pl.ds(i * owned, owned)
        grad = dot(joined, slab(i)[: width + rank, :])
        scale = [1.0 + mod[b, pl.ds(m, 1), pl.ds(width + i * owned, owned)] for m in batches]
        pieces = [grad[n * ROWS : (n + 1) * ROWS] * scale[n] for n in range(len(batches))]
        grad = pieces[0] if len(pieces) == 1 else jnp.concatenate(pieces, axis=0)
        scaled.append(grad)
        part = grad * h[b, rows, c]
        total = part if total is None else total + part
    centred = jnp.sum(total, axis=1, keepdims=True) * (1.0 / width)
    rms = inv[b, rows, :]
    for i in range(MEMBERS):
        c = pl.ds(i * owned, owned)
        value = g[:, c].astype(jnp.float32) + rms * (scaled[i] - h[b, rows, c] * centred)
        value = value.astype(jnp.bfloat16)
        g[:, c] = value
        g_keep[b, :, c] = value


def first_kernel(
    batches, width, rank, stage, place, x, mod, target, slabs, own, d, h, inv, gs, us, *rest
):
    gouts, (g, g_keep, u_keep, preact, near, fetched, stored) = rest[:batches], rest[batches:]
    share = batches * ROWS
    per_chunk = CHUNK // slabs.shape[3]
    quarter = MEMBERS // PIECES
    own_copy = pltpu.make_async_copy(slabs.at[place[0], :, width:, :], own, stored.at[2, 0])

    def fetch(step, piece):
        members = pl.ds(piece * quarter, quarter)
        slot = lax.rem(step, 2)
        return pltpu.make_async_copy(
            slabs.at[BLOCKS - 1 - step, members], near.at[slot, members], fetched.at[slot, piece]
        )

    def store_u(b):
        return pltpu.make_async_copy(u_keep.at[b], us.at[b], stored.at[0, b])

    def store_g(b):
        return pltpu.make_async_copy(g_keep.at[b], gs.at[b], stored.at[1, b])

    def block(step, carry):
        b = BLOCKS - 1 - step
        slot = lax.rem(step, 2)
        for piece in range(PIECES):
            fetch(step, piece).wait()

        @pl.when(step < BLOCKS - 1)
        def ahead():
            for piece in range(PIECES):
                fetch(step + 1, piece).start()

        def slab(i):
            return near.at[slot, i]

        pieces = []
        for m in range(batches):
            r = pl.ds(m * ROWS, ROWS)
            values = x[b, r, :].astype(jnp.float32)
            rms = lax.rsqrt(jnp.mean(values * values, axis=1, keepdims=True) + EPSILON)
            normed = values * rms
            h[b, r, :] = normed
            inv[b, r, :] = jnp.broadcast_to(rms, (ROWS, inv.shape[2]))
            shift = mod[b, pl.ds(m, 1), 0:width]
            scale = mod[b, pl.ds(m, 1), width : 2 * width]
            pieces.append((normed * (1.0 + scale) + shift).astype(jnp.bfloat16))
        modulated = jnp.concatenate(pieces, axis=0)
        down = jnp.concatenate([slab(i)[width : width + rank, :] for i in range(MEMBERS)], axis=1)
        low = dot(modulated, down, LAST_DIMS).astype(jnp.bfloat16)
        for j in range(width // CHUNK):
            c = pl.ds(j * CHUNK, CHUNK)
            up = jnp.concatenate([slab(j * per_chunk + i)[width + rank :, :] for i in range(per_chunk)], axis=0)
            weight = jnp.concatenate([slab(i)[c, :] for i in range(MEMBERS)], axis=1)
            preact[:, c] = dot(weight, modulated, LAST_DIMS).T + dot(low, up, LAST_DIMS)
        for j in range(width // CHUNK):
            c = pl.ds(j * CHUNK, CHUNK)
            for m in range(batches):
                r = pl.ds(m * ROWS, ROWS)
                pre = preact[r, c]
                squared = pre * pre
                bent = jnp.tanh(SLOPE * pre * (1.0 + CUBIC * squared))
                half = 0.5 * (1.0 + bent)
                slope = half + 0.5 * pre * (1.0 - bent * bent) * (SLOPE * (1.0 + 3.0 * CUBIC * squared))
                gate = mod[b, pl.ds(m, 1), pl.ds(2 * width + j * CHUNK, CHUNK)]
                d[b, r, c] = slope * gate
                preact[r, c] = gate * (pre * half)

        @pl.when(step == 0)
        def close():
            out = x[b].astype(jnp.float32) + preact[...]
            g[...] = (out - target[...].astype(jnp.float32)).astype(jnp.bfloat16)

        @pl.when(stage[0] == STAGES - 1)
        def relay():
            relay_block(
                b, range(batches), width, rank, pl.ds(0, share), slab, g, d, h, mod, inv, g_keep, u_keep
            )
            store_u(b).start()
            store_g(b).start()

        return carry

    for piece in range(PIECES):
        fetch(0, piece).start()
    own_copy.start()
    lax.fori_loop(0, BLOCKS, block, 0)
    own_copy.wait()
    for m in range(batches):
        gouts[m][...] = g[m * ROWS : (m + 1) * ROWS, :]

    @pl.when(stage[0] == STAGES - 1)
    def finish():
        for b in range(BLOCKS):
            store_u(b).wait()
            store_g(b).wait()


def relay_kernel(
    active_stage, m, width, rank, stage, gin, slabs, d, h, mod, inv, gs_in, us_in, gout, gs, us, g_keep, u_keep, stored
):
    rows = pl.ds(m * ROWS, ROWS)

    def store_u(b):
        return pltpu.make_async_copy(u_keep.at[b], us.at[b, rows, :], stored.at[0, b])

    def store_g(b):
        return pltpu.make_async_copy(g_keep.at[b], gs.at[b, rows, :], stored.at[1, b])

    def block(step, carry):
        b = BLOCKS - 1 - step
        relay_block(
            b, [m], width, rank, rows, lambda i: slabs.at[b, i], gout, d, h, mod, inv, g_keep, u_keep
        )
        store_u(b).start()
        store_g(b).start()
        return carry

    @pl.when(stage[0] == active_stage)
    def run():
        gout[...] = gin[...]
        lax.fori_loop(0, BLOCKS, block, 0)
        for b in range(BLOCKS):
            store_u(b).wait()
            store_g(b).wait()


def grads_kernel(rank, core, own, pre_ref, mixed_ref, mine, theirs):
    down = jnp.concatenate([own[i, :rank, :] for i in range(MEMBERS)], axis=1)
    up = jnp.concatenate([own[i, rank:, :] for i in range(MEMBERS)], axis=0)
    pre, mixed = pre_ref[...], mixed_ref[...]
    lowrank = dot(mixed, down, LAST_DIMS).astype(jnp.bfloat16)
    grad_low = dot(pre, up).astype(jnp.bfloat16)
    owned = own.shape[2]
    for row, (left, right) in ((0, (grad_low, mixed)), (rank, (lowrank, pre))):
        part = dot(left.T, right).astype(jnp.bfloat16)
        for i in range(MEMBERS // CORES):
            pair = [part[:, (CORES * i + c) * owned : (CORES * i + c + 1) * owned] for c in range(CORES)]
            mine[i, row : row + rank, :] = jnp.where(core[0] == 0, pair[0], pair[1])
            theirs[i, row : row + rank, :] = jnp.where(core[0] == 0, pair[1], pair[0])


def split_kernel(place, kept, own, ahead, behind, sems):
    rows = kept.shape[1]
    half = rows // 2

    def piece(n, turn, first, count, target, start):
        source = kept.at[lax.rem(place[0] + turn, BLOCKS), pl.ds(first, count), :]
        return pltpu.make_async_copy(source, target.at[pl.ds(start, count), :], sems.at[n])

    copies = [
        piece(0, 0, 0, rows, own, 0),
        piece(1, 1, 0, rows, ahead, 0),
        piece(2, 2, 0, half, ahead, rows),
        piece(3, 3, 0, rows, behind, 0),
        piece(4, 2, half, half, behind, rows),
    ]
    for copy in copies:
        copy.start()
    for copy in copies:
        copy.wait()


def input_grads_kernel(place, own, ahead, behind, far_ahead, far_behind, out):
    rows = own.shape[0]
    half = rows // 2
    for turn, first, value in (
        (0, 0, own[...]),
        (1, 0, ahead[:rows, :]),
        (2, 0, far_ahead[...]),
        (2, half, far_behind[...]),
        (3, 0, behind[:rows, :]),
    ):
        start = pl.multiple_of(lax.rem(place[0] - turn + BLOCKS, BLOCKS) * rows + first, half)
        out[0, pl.ds(start, value.shape[0]), :] = value


def total_kernel(rank, scale, parts, down, up):
    total = jnp.sum(parts[...].astype(jnp.float32), axis=0) * scale
    down[0] = total[:rank, :].T
    up[0] = total[rank:, :].T


VMEM = pl.BlockSpec(memory_space=pltpu.VMEM)
ANY = pl.BlockSpec(memory_space=pl.ANY)
HBM = pl.BlockSpec(memory_space=pltpu.HBM)
SMEM = pl.BlockSpec(memory_space=pltpu.SMEM)


def resident(value):
    return pltpu.with_memory_space_constraint(value, pltpu.VMEM)


def far(value):
    return pltpu.with_memory_space_constraint(value, pltpu.HBM)


def per_device(block_inputs, target, frozen_weight, adapter_down, adapter_up, start_modulation, finish_modulation, level_pairs):
    stage = lax.axis_index("y")
    place = lax.axis_index("zh")
    core = lax.axis_index("c")
    tokens, width = block_inputs.shape[1:]
    owned, rank = adapter_down.shape[1:]
    share = tokens // BLOCKS
    batches = share // ROWS
    grad_scale = 1.0 / math.sqrt(tokens * MEMBERS)

    slab = pl.pallas_call(
        functools.partial(slab_kernel, width, rank),
        out_shape=jax.ShapeDtypeStruct((width + 2 * rank, owned), jnp.bfloat16),
        in_specs=[VMEM] * 3,
        out_specs=VMEM,
        name="slab",
    )(frozen_weight[0], adapter_down[0], adapter_up[0])
    slabs = lax.all_gather(slab, PLANE, axis=0, tiled=True)
    slabs = slabs.reshape(BLOCKS, MEMBERS, width + 2 * rank, owned)

    own_mod = per_batch_modulation(start_modulation[0], finish_modulation[0], level_pairs)
    mod = lax.all_to_all(own_mod, "zh", 0, 0, tiled=True).reshape(BLOCKS, batches, 3 * width)
    x = lax.all_to_all(block_inputs[0], "zh", 0, 0, tiled=True).reshape(BLOCKS, share, width)
    own_target = lax.dynamic_slice_in_dim(target, place * share, share, 0)

    values = block_inputs[0].astype(jnp.float32)
    normed = values * lax.rsqrt(jnp.mean(values * values, axis=1, keepdims=True) + EPSILON)
    row_mod = jnp.repeat(own_mod[:, : 2 * width], ROWS, axis=0)
    modulated = (normed * (1.0 + row_mod[:, width:]) + row_mod[:, :width]).astype(jnp.bfloat16)
    stage, place, core = (index.astype(jnp.int32).reshape(1) for index in (stage, place, core))
    x, mod, stage, place, core, own_target, modulated = lax.optimization_barrier(
        (x, mod, stage, place, core, own_target, modulated)
    )

    slabs_near, mod_near = resident(slabs), resident(mod)
    kept_shape = (BLOCKS, share, width)
    own, d, h, inv, gs, us, *sent = pl.pallas_call(
        functools.partial(first_kernel, batches, width, rank),
        out_shape=[
            pltpu.VMEM((MEMBERS, 2 * rank, owned), jnp.bfloat16),
            pltpu.VMEM(kept_shape, jnp.float32),
            pltpu.VMEM(kept_shape, jnp.float32),
            pltpu.VMEM((BLOCKS, share, owned), jnp.float32),
            pltpu.HBM(kept_shape, jnp.bfloat16),
            pltpu.HBM(kept_shape, jnp.bfloat16),
        ]
        + [pltpu.VMEM((ROWS, width), jnp.bfloat16)] * batches,
        in_specs=[SMEM] * 2 + [VMEM] * 3 + [HBM],
        out_specs=[VMEM] * 4 + [HBM] * 2 + [VMEM] * batches,
        scratch_shapes=[
            pltpu.VMEM((share, width), jnp.bfloat16),
            pltpu.VMEM(kept_shape, jnp.bfloat16),
            pltpu.VMEM(kept_shape, jnp.bfloat16),
            pltpu.VMEM((share, width), jnp.float32),
            pltpu.VMEM((2,) + slabs.shape[1:], jnp.bfloat16),
            pltpu.SemaphoreType.DMA((2, PIECES)),
            pltpu.SemaphoreType.DMA((3, BLOCKS)),
        ],
        compiler_params=pltpu.CompilerParams(vmem_limit_bytes=26 * MIB),
        cost_estimate=pl.CostEstimate(flops=4 * BLOCKS * share * width * width, bytes_accessed=40 * MIB, transcendentals=0),
        name="first",
    )(stage, place, x, mod_near, own_target, far(slabs))

    d_near, h_near, inv_near = (resident(v) for v in (d, h, inv))

    def relay(active_stage, m, gin, gs, us):
        return pl.pallas_call(
            functools.partial(relay_kernel, active_stage, m, width, rank),
            out_shape=[pltpu.VMEM((ROWS, width), jnp.bfloat16)] + [pltpu.HBM(kept_shape, jnp.bfloat16)] * 2,
            in_specs=[SMEM] + [VMEM] * 6 + [HBM] * 2,
            out_specs=[VMEM] + [HBM] * 2,
            scratch_shapes=[
                pltpu.VMEM((BLOCKS, ROWS, width), jnp.bfloat16),
                pltpu.VMEM((BLOCKS, ROWS, width), jnp.bfloat16),
                pltpu.SemaphoreType.DMA((2, BLOCKS)),
            ],
            input_output_aliases={7: 1, 8: 2},
            compiler_params=pltpu.CompilerParams(vmem_limit_bytes=4 * MIB),
            cost_estimate=pl.CostEstimate(flops=2 * BLOCKS * ROWS * width * width, bytes_accessed=4 * MIB, transcendentals=0),
            name="relay",
        )(stage, resident(gin), slabs_near, d_near, h_near, mod_near, inv_near, far(gs), far(us))

    _, gs, us = relay(STAGES, 0, sent[0], gs, us)
    for step in range(1, STAGES):
        arrived = [lax.ppermute(out, "y", [(STAGES - step, STAGES - 1 - step)]) for out in sent]
        sent = []
        for m in range(batches):
            gout, gs, us = relay(STAGES - 1 - step, m, arrived[m], gs, us)
            sent.append(gout)

    gs, us, modulated = lax.optimization_barrier((gs, us, modulated))
    own_pre = lax.all_to_all(us.reshape(tokens, width), "zh", 0, 0, tiled=True)
    def shifted(value, turn):
        return lax.ppermute(value, "zh", [(i, (i + turn) % BLOCKS) for i in range(BLOCKS)])

    own_pre, gs = lax.optimization_barrier((own_pre, gs))
    packed = (share + share // 2, width)
    near_grads, ahead, behind = pl.pallas_call(
        split_kernel,
        out_shape=[pltpu.VMEM((share, width), jnp.bfloat16)] + [pltpu.VMEM(packed, jnp.bfloat16)] * 2,
        in_specs=[SMEM, HBM],
        out_specs=[VMEM] * 3,
        scratch_shapes=[pltpu.SemaphoreType.DMA((5,))],
        compiler_params=pltpu.CompilerParams(vmem_limit_bytes=4 * MIB),
        name="split",
    )(place, far(gs))
    ahead, behind = shifted(ahead, 1), shifted(behind, -1)

    half = MEMBERS // CORES
    mine, theirs = pl.pallas_call(
        functools.partial(grads_kernel, rank),
        out_shape=[jax.ShapeDtypeStruct((half, 2 * rank, owned), jnp.bfloat16)] * 2,
        in_specs=[SMEM] + [VMEM] * 3,
        out_specs=[VMEM] * 2,
        compiler_params=pltpu.CompilerParams(vmem_limit_bytes=16 * MIB),
        name="grads",
    )(core, own, own_pre, modulated)
    theirs = lax.ppermute(theirs, "c", [(0, 1), (1, 0)])
    parts = (mine.astype(jnp.float32) + theirs.astype(jnp.float32)).astype(jnp.bfloat16)
    parts = lax.all_to_all(parts, CHIPS, 0, 0, tiled=True)
    ahead, behind, parts = lax.optimization_barrier((ahead, behind, parts))
    far_ahead, far_behind = shifted(ahead[share:], 1), shifted(behind[share:], -1)
    down_grad, up_grad = pl.pallas_call(
        functools.partial(total_kernel, rank, grad_scale),
        out_shape=[jax.ShapeDtypeStruct((1, owned, rank), jnp.float32)] * 2,
        in_specs=[VMEM],
        out_specs=[VMEM] * 2,
        name="total",
    )(parts)
    input_grads = pl.pallas_call(
        input_grads_kernel,
        out_shape=jax.ShapeDtypeStruct((1, tokens, width), jnp.bfloat16),
        in_specs=[SMEM] + [VMEM] * 5,
        out_specs=VMEM,
        compiler_params=pltpu.CompilerParams(vmem_limit_bytes=8 * MIB),
        name="input_grads",
    )(place, near_grads, ahead, behind, far_ahead, far_behind)
    return input_grads, down_grad, up_grad


def solution(mesh):
    split = Mesh(mesh.devices.reshape(SIZES), AXES)
    blocks = ("y", "zh")
    return jax.shard_map(
        per_device,
        mesh=split,
        in_specs=(
            P(blocks, GROUP, None),
            P(GROUP, None),
            P(blocks, GROUP, None),
            P(blocks, GROUP, None),
            P(blocks, GROUP, None),
            P(blocks, None, None),
            P(blocks, None, None),
            P(GROUP, None),
        ),
        out_specs=(P(blocks, GROUP, None), P(blocks, GROUP, None), P(blocks, GROUP, None)),
        check_vma=False,
    )
```

```python
import functools
import math

import jax
import jax.numpy as jnp
from jax import lax
from jax.experimental import pallas as pl
from jax.experimental.pallas import tpu as pltpu
from jax.sharding import Mesh, PartitionSpec as P

EPSILON = 1e-06
AXES = ("y", "zh", "zl", "x", "c")
SIZES = (8, 4, 2, 4, 2)
STAGES, BLOCKS, CORES = SIZES[0], SIZES[1], SIZES[4]
GROUP = ("zl", "x", "c")
CHIPS = ("zl", "x")
PLANE = ("zh", "zl", "x", "c")
MEMBERS = 16
ROWS = 32
CHUNK = 512
PIECES = 4
HEAD_ROWS = 1536
ROW_DOT = (((1,), (0,)), ((), ()))
LAST_DIMS = (((1,), (1,)), ((), ()))
FIRST_DIMS = (((0,), (0,)), ((), ()))
SLOPE = math.sqrt(2.0 / math.pi)
CUBIC = 0.044715
MIB = 2**20


def dot(left, right, dims=ROW_DOT):
    return lax.dot_general(left, right, dims, preferred_element_type=jnp.float32)


def per_batch_modulation(from_table, to_table, level_pairs):
    ladder = jnp.arange(from_table.shape[0], dtype=jnp.int32)[None, :]
    hot_from = (level_pairs[:, 0:1] == ladder).astype(jnp.bfloat16)
    hot_to = (level_pairs[:, 1:2] == ladder).astype(jnp.bfloat16)
    return dot(hot_from, from_table) + dot(hot_to, to_table)


def slab_kernel(width, rank, weight, down, up, head, rest):
    count = head.shape[0]
    turned = weight[...].T
    head[...] = turned[:count, :]
    rest[: width - count, :] = turned[count:, :]
    rest[width - count : width - count + rank, :] = down[...].T
    rest[width - count + rank :, :] = up[...]


RING = (0, -1, -2, -3, -4, 1, 2, 3)


def ring_bundle(piece):
    ring = SIZES[1] * SIZES[2]

    def step(value, turn):
        return lax.ppermute(value, ("zh", "zl"), [(i, (i + turn) % ring) for i in range(ring)])

    up_1, down_1 = step(piece, 1), step(piece, -1)
    up_2, down_2 = step(up_1, 1), step(down_1, -1)
    up_3, down_3 = step(up_2, 1), step(down_2, -1)
    return jnp.stack([piece, up_1, up_2, up_3, step(up_3, 1), down_1, down_2, down_3])


def row_bundles(bundle):
    row, middle = SIZES[3], bundle.shape[0] // 2

    def step(value, turn):
        return lax.ppermute(value, "x", [(i, (i + turn) % row) for i in range(row)])

    before, after = step(bundle, 1), step(bundle, -1)
    return [bundle, before, after, step(before[:middle], 1), step(after[middle:], -1)]


def place_kernel(ring_place, row_place, core, *refs):
    bundles, (out, sems) = refs[:-2], refs[-2:]
    ring, row = SIZES[1] * SIZES[2], SIZES[3]
    middle = len(RING) // 2
    copies = []
    for n, bundle in enumerate(bundles):
        kind, other = n % 5, n // 5
        turns = RING[:middle] if kind == 3 else RING[middle:] if kind == 4 else RING
        x = lax.rem(row_place[0] + (0, row - 1, 1, 2, 2)[kind], row)
        c = lax.rem(core[0] + other, CORES)
        for m, turn in enumerate(turns):
            z = lax.rem(ring_place[0] + turn + ring, ring)
            member = (lax.rem(z, SIZES[2]) * row + x) * CORES + c
            copies.append(pltpu.make_async_copy(bundle.at[m], out.at[z // SIZES[2], member], sems.at[n, m]))
    for copy in copies:
        copy.start()
    for copy in copies:
        copy.wait()


def relay_block(b, batches, width, rank, rows, times, up_of, g, d, h, mod, inv, g_keep, u_keep):
    owned = width // MEMBERS
    u = (d[b, rows, :] * g[...].astype(jnp.float32)).astype(jnp.bfloat16)
    u_keep[b] = u
    up = jnp.concatenate([up_of(i) for i in range(MEMBERS)], axis=0)
    low = dot(u, up).astype(jnp.bfloat16)
    joined = jnp.concatenate([u, low], axis=1)
    scaled, total = [], None
    for i in range(MEMBERS):
        c = pl.ds(i * owned, owned)
        grad = times(joined, i)
        scale = [1.0 + mod[b, pl.ds(m, 1), pl.ds(width + i * owned, owned)] for m in batches]
        pieces = [grad[n * ROWS : (n + 1) * ROWS] * scale[n] for n in range(len(batches))]
        grad = pieces[0] if len(pieces) == 1 else jnp.concatenate(pieces, axis=0)
        scaled.append(grad)
        part = grad * h[b, rows, c]
        total = part if total is None else total + part
    centred = jnp.sum(total, axis=1, keepdims=True) * (1.0 / width)
    rms = inv[b, rows, :]
    for i in range(MEMBERS):
        c = pl.ds(i * owned, owned)
        value = g[:, c].astype(jnp.float32) + rms * (scaled[i] - h[b, rows, c] * centred)
        value = value.astype(jnp.bfloat16)
        g[:, c] = value
        g_keep[b, :, c] = value


def first_kernel(
    batches, width, rank, stage, place, x, mod, target, heads, rests, own, d, h, inv, gs, us, *rest
):
    gouts, (g, g_keep, u_keep, preact, near, fetched, stored) = rest[:batches], rest[batches:]
    share = batches * ROWS
    per_chunk = CHUNK // heads.shape[3]
    count = heads.shape[2]
    quarter = MEMBERS // PIECES
    own_copy = pltpu.make_async_copy(rests.at[place[0], :, width - count :, :], own, stored.at[2, 0])

    def fetch(step, piece):
        members = pl.ds(piece * quarter, quarter)
        slot = lax.rem(step, 2)
        b = BLOCKS - 1 - step
        return (
            pltpu.make_async_copy(heads.at[b, members], near.at[slot, members, :count, :], fetched.at[slot, 0, piece]),
            pltpu.make_async_copy(rests.at[b, members], near.at[slot, members, count:, :], fetched.at[slot, 1, piece]),
        )

    def store_u(b):
        return pltpu.make_async_copy(u_keep.at[b], us.at[b], stored.at[0, b])

    def store_g(b):
        return pltpu.make_async_copy(g_keep.at[b], gs.at[b], stored.at[1, b])

    def block(step, carry):
        b = BLOCKS - 1 - step
        slot = lax.rem(step, 2)
        for piece in range(PIECES):
            for copy in fetch(step, piece):
                copy.wait()

        @pl.when(step < BLOCKS - 1)
        def ahead():
            for piece in range(PIECES):
                for copy in fetch(step + 1, piece):
                    copy.start()

        def slab(i):
            return near.at[slot, i]

        pieces = []
        for m in range(batches):
            r = pl.ds(m * ROWS, ROWS)
            values = x[b, r, :].astype(jnp.float32)
            rms = lax.rsqrt(jnp.mean(values * values, axis=1, keepdims=True) + EPSILON)
            normed = values * rms
            h[b, r, :] = normed
            inv[b, r, :] = jnp.broadcast_to(rms, (ROWS, inv.shape[2]))
            shift = mod[b, pl.ds(m, 1), 0:width]
            scale = mod[b, pl.ds(m, 1), width : 2 * width]
            pieces.append((normed * (1.0 + scale) + shift).astype(jnp.bfloat16))
        modulated = jnp.concatenate(pieces, axis=0)
        down = jnp.concatenate([slab(i)[width : width + rank, :] for i in range(MEMBERS)], axis=1)
        low = dot(modulated, down, LAST_DIMS).astype(jnp.bfloat16)
        for j in range(width // CHUNK):
            c = pl.ds(j * CHUNK, CHUNK)
            up = jnp.concatenate([slab(j * per_chunk + i)[width + rank :, :] for i in range(per_chunk)], axis=0)
            weight = jnp.concatenate([slab(i)[c, :] for i in range(MEMBERS)], axis=1)
            preact[:, c] = dot(weight, modulated, LAST_DIMS).T + dot(low, up, LAST_DIMS)
        for j in range(width // CHUNK):
            c = pl.ds(j * CHUNK, CHUNK)
            for m in range(batches):
                r = pl.ds(m * ROWS, ROWS)
                pre = preact[r, c]
                squared = pre * pre
                bent = jnp.tanh(SLOPE * pre * (1.0 + CUBIC * squared))
                half = 0.5 * (1.0 + bent)
                slope = half + 0.5 * pre * (1.0 - bent * bent) * (SLOPE * (1.0 + 3.0 * CUBIC * squared))
                gate = mod[b, pl.ds(m, 1), pl.ds(2 * width + j * CHUNK, CHUNK)]
                d[b, r, c] = slope * gate
                preact[r, c] = gate * (pre * half)

        @pl.when(step == 0)
        def close():
            out = x[b].astype(jnp.float32) + preact[...]
            g[...] = (out - target[...].astype(jnp.float32)).astype(jnp.bfloat16)

        @pl.when(stage[0] == STAGES - 1)
        def relay():
            relay_block(
                b,
                range(batches),
                width,
                rank,
                pl.ds(0, share),
                lambda value, i: dot(value, slab(i)[: width + rank, :]),
                lambda i: slab(i)[width + rank :, :],
                g,
                d,
                h,
                mod,
                inv,
                g_keep,
                u_keep,
            )
            store_u(b).start()
            store_g(b).start()

        return carry

    for piece in range(PIECES):
        for copy in fetch(0, piece):
            copy.start()
    own_copy.start()
    lax.fori_loop(0, BLOCKS, block, 0)
    own_copy.wait()
    for m in range(batches):
        gouts[m][...] = g[m * ROWS : (m + 1) * ROWS, :]

    @pl.when(stage[0] == STAGES - 1)
    def finish():
        for b in range(BLOCKS):
            store_u(b).wait()
            store_g(b).wait()


def relay_kernel(
    active_stage, m, width, rank, stage, gin, heads, rests, d, h, mod, inv, gs_in, us_in, gout, gs, us, g_keep, u_keep, stored
):
    rows = pl.ds(m * ROWS, ROWS)

    def store_u(b):
        return pltpu.make_async_copy(u_keep.at[b], us.at[b, rows, :], stored.at[0, b])

    def store_g(b):
        return pltpu.make_async_copy(g_keep.at[b], gs.at[b, rows, :], stored.at[1, b])

    def block(step, carry):
        b = BLOCKS - 1 - step
        count = heads.shape[2]
        last = width + rank - count

        def times(value, i):
            return dot(value[:, :count], heads[b, i]) + dot(value[:, count:], rests[b, i, :last, :])

        relay_block(
            b, [m], width, rank, rows, times, lambda i: rests[b, i, last:, :], gout, d, h, mod, inv, g_keep, u_keep
        )
        store_u(b).start()
        store_g(b).start()
        return carry

    @pl.when(stage[0] == active_stage)
    def run():
        gout[...] = gin[...]
        lax.fori_loop(0, BLOCKS, block, 0)
        for b in range(BLOCKS):
            store_u(b).wait()
            store_g(b).wait()


def grads_kernel(rank, core, own, pre_ref, mixed_ref, mine, theirs):
    down = jnp.concatenate([own[i, :rank, :] for i in range(MEMBERS)], axis=1)
    up = jnp.concatenate([own[i, rank:, :] for i in range(MEMBERS)], axis=0)
    pre, mixed = pre_ref[...], mixed_ref[...]
    lowrank = dot(mixed, down, LAST_DIMS).astype(jnp.bfloat16)
    grad_low = dot(pre, up).astype(jnp.bfloat16)
    owned = own.shape[2]
    for row, (left, right) in ((0, (grad_low, mixed)), (rank, (lowrank, pre))):
        part = dot(left.T, right).astype(jnp.bfloat16)
        for i in range(MEMBERS // CORES):
            pair = [part[:, (CORES * i + c) * owned : (CORES * i + c + 1) * owned] for c in range(CORES)]
            mine[i, row : row + rank, :] = jnp.where(core[0] == 0, pair[0], pair[1])
            theirs[i, row : row + rank, :] = jnp.where(core[0] == 0, pair[1], pair[0])


def split_kernel(place, kept, own, ahead, behind, sems):
    rows = kept.shape[1]
    half = rows // 2

    def piece(n, turn, first, count, target, start):
        source = kept.at[lax.rem(place[0] + turn, BLOCKS), pl.ds(first, count), :]
        return pltpu.make_async_copy(source, target.at[pl.ds(start, count), :], sems.at[n])

    copies = [
        piece(0, 0, 0, rows, own, 0),
        piece(1, 1, 0, rows, ahead, 0),
        piece(2, 2, 0, half, ahead, rows),
        piece(3, 3, 0, rows, behind, 0),
        piece(4, 2, half, half, behind, rows),
    ]
    for copy in copies:
        copy.start()
    for copy in copies:
        copy.wait()


def input_grads_kernel(place, own, ahead, behind, far_ahead, far_behind, out):
    rows = own.shape[0]
    half = rows // 2
    for turn, first, value in (
        (0, 0, own[...]),
        (1, 0, ahead[:rows, :]),
        (2, 0, far_ahead[...]),
        (2, half, far_behind[...]),
        (3, 0, behind[:rows, :]),
    ):
        start = pl.multiple_of(lax.rem(place[0] - turn + BLOCKS, BLOCKS) * rows + first, half)
        out[0, pl.ds(start, value.shape[0]), :] = value


def total_kernel(rank, scale, parts, down, up):
    total = jnp.sum(parts[...].astype(jnp.float32), axis=0) * scale
    down[0] = total[:rank, :].T
    up[0] = total[rank:, :].T


VMEM = pl.BlockSpec(memory_space=pltpu.VMEM)
ANY = pl.BlockSpec(memory_space=pl.ANY)
HBM = pl.BlockSpec(memory_space=pltpu.HBM)
SMEM = pl.BlockSpec(memory_space=pltpu.SMEM)


def resident(value):
    return pltpu.with_memory_space_constraint(value, pltpu.VMEM)


def far(value):
    return pltpu.with_memory_space_constraint(value, pltpu.HBM)


def per_device(block_inputs, target, frozen_weight, adapter_down, adapter_up, start_modulation, finish_modulation, level_pairs):
    stage = lax.axis_index("y")
    place = lax.axis_index("zh")
    core = lax.axis_index("c")
    tokens, width = block_inputs.shape[1:]
    owned, rank = adapter_down.shape[1:]
    share = tokens // BLOCKS
    batches = share // ROWS
    grad_scale = 1.0 / math.sqrt(tokens * MEMBERS)

    rest_rows = width + 2 * rank - HEAD_ROWS
    head, rest = pl.pallas_call(
        functools.partial(slab_kernel, width, rank),
        out_shape=[
            jax.ShapeDtypeStruct((HEAD_ROWS, owned), jnp.bfloat16),
            jax.ShapeDtypeStruct((rest_rows, owned), jnp.bfloat16),
        ],
        in_specs=[VMEM] * 3,
        out_specs=[VMEM] * 2,
        name="slab",
    )(frozen_weight[0], adapter_down[0], adapter_up[0])
    heads = lax.all_gather(head, PLANE, axis=0, tiled=True).reshape(BLOCKS, MEMBERS, HEAD_ROWS, owned)
    bundles = row_bundles(ring_bundle(rest))
    bundles = bundles + [lax.ppermute(value, "c", [(0, 1), (1, 0)]) for value in bundles]
    indices = [lax.axis_index(("zh", "zl")), lax.axis_index("x"), core]
    rests = pl.pallas_call(
        place_kernel,
        out_shape=pltpu.VMEM((BLOCKS, MEMBERS, rest_rows, owned), jnp.bfloat16),
        in_specs=[SMEM] * 3 + [ANY] * len(bundles),
        out_specs=VMEM,
        scratch_shapes=[pltpu.SemaphoreType.DMA((len(bundles), len(RING)))],
        compiler_params=pltpu.CompilerParams(vmem_limit_bytes=4 * MIB),
        name="place",
    )(*[index.astype(jnp.int32).reshape(1) for index in indices], *bundles)

    own_mod = per_batch_modulation(start_modulation[0], finish_modulation[0], level_pairs)
    mod = lax.all_to_all(own_mod, "zh", 0, 0, tiled=True).reshape(BLOCKS, batches, 3 * width)
    x = lax.all_to_all(block_inputs[0], "zh", 0, 0, tiled=True).reshape(BLOCKS, share, width)
    own_target = lax.dynamic_slice_in_dim(target, place * share, share, 0)

    values = block_inputs[0].astype(jnp.float32)
    normed = values * lax.rsqrt(jnp.mean(values * values, axis=1, keepdims=True) + EPSILON)
    row_mod = jnp.repeat(own_mod[:, : 2 * width], ROWS, axis=0)
    modulated = (normed * (1.0 + row_mod[:, width:]) + row_mod[:, :width]).astype(jnp.bfloat16)
    stage, place, core = (index.astype(jnp.int32).reshape(1) for index in (stage, place, core))
    x, mod, stage, place, core, own_target, modulated = lax.optimization_barrier(
        (x, mod, stage, place, core, own_target, modulated)
    )

    heads_near, rests_near, mod_near = resident(heads), resident(rests), resident(mod)
    kept_shape = (BLOCKS, share, width)
    own, d, h, inv, gs, us, *sent = pl.pallas_call(
        functools.partial(first_kernel, batches, width, rank),
        out_shape=[
            pltpu.VMEM((MEMBERS, 2 * rank, owned), jnp.bfloat16),
            pltpu.VMEM(kept_shape, jnp.float32),
            pltpu.VMEM(kept_shape, jnp.float32),
            pltpu.VMEM((BLOCKS, share, owned), jnp.float32),
            pltpu.HBM(kept_shape, jnp.bfloat16),
            pltpu.HBM(kept_shape, jnp.bfloat16),
        ]
        + [pltpu.VMEM((ROWS, width), jnp.bfloat16)] * batches,
        in_specs=[SMEM] * 2 + [VMEM] * 3 + [HBM] * 2,
        out_specs=[VMEM] * 4 + [HBM] * 2 + [VMEM] * batches,
        scratch_shapes=[
            pltpu.VMEM((share, width), jnp.bfloat16),
            pltpu.VMEM(kept_shape, jnp.bfloat16),
            pltpu.VMEM(kept_shape, jnp.bfloat16),
            pltpu.VMEM((share, width), jnp.float32),
            pltpu.VMEM((2, MEMBERS, width + 2 * rank, owned), jnp.bfloat16),
            pltpu.SemaphoreType.DMA((2, 2, PIECES)),
            pltpu.SemaphoreType.DMA((3, BLOCKS)),
        ],
        compiler_params=pltpu.CompilerParams(vmem_limit_bytes=26 * MIB),
        cost_estimate=pl.CostEstimate(flops=4 * BLOCKS * share * width * width, bytes_accessed=40 * MIB, transcendentals=0),
        name="first",
    )(stage, place, x, mod_near, own_target, far(heads), far(rests))

    d_near, h_near, inv_near = (resident(v) for v in (d, h, inv))

    def relay(active_stage, m, gin, gs, us):
        return pl.pallas_call(
            functools.partial(relay_kernel, active_stage, m, width, rank),
            out_shape=[pltpu.VMEM((ROWS, width), jnp.bfloat16)] + [pltpu.HBM(kept_shape, jnp.bfloat16)] * 2,
            in_specs=[SMEM] + [VMEM] * 7 + [HBM] * 2,
            out_specs=[VMEM] + [HBM] * 2,
            scratch_shapes=[
                pltpu.VMEM((BLOCKS, ROWS, width), jnp.bfloat16),
                pltpu.VMEM((BLOCKS, ROWS, width), jnp.bfloat16),
                pltpu.SemaphoreType.DMA((2, BLOCKS)),
            ],
            input_output_aliases={8: 1, 9: 2},
            compiler_params=pltpu.CompilerParams(vmem_limit_bytes=4 * MIB),
            cost_estimate=pl.CostEstimate(flops=2 * BLOCKS * ROWS * width * width, bytes_accessed=4 * MIB, transcendentals=0),
            name="relay",
        )(stage, resident(gin), heads_near, rests_near, d_near, h_near, mod_near, inv_near, far(gs), far(us))

    _, gs, us = relay(STAGES, 0, sent[0], gs, us)
    for step in range(1, STAGES):
        arrived = [lax.ppermute(out, "y", [(STAGES - step, STAGES - 1 - step)]) for out in sent]
        sent = []
        for m in range(batches):
            gout, gs, us = relay(STAGES - 1 - step, m, arrived[m], gs, us)
            sent.append(gout)

    gs, us, modulated = lax.optimization_barrier((gs, us, modulated))
    own_pre = lax.all_to_all(us.reshape(tokens, width), "zh", 0, 0, tiled=True)
    def shifted(value, turn):
        return lax.ppermute(value, "zh", [(i, (i + turn) % BLOCKS) for i in range(BLOCKS)])

    own_pre, gs = lax.optimization_barrier((own_pre, gs))
    packed = (share + share // 2, width)
    near_grads, ahead, behind = pl.pallas_call(
        split_kernel,
        out_shape=[pltpu.VMEM((share, width), jnp.bfloat16)] + [pltpu.VMEM(packed, jnp.bfloat16)] * 2,
        in_specs=[SMEM, HBM],
        out_specs=[VMEM] * 3,
        scratch_shapes=[pltpu.SemaphoreType.DMA((5,))],
        compiler_params=pltpu.CompilerParams(vmem_limit_bytes=4 * MIB),
        name="split",
    )(place, far(gs))
    ahead, behind = shifted(ahead, 1), shifted(behind, -1)

    half = MEMBERS // CORES
    mine, theirs = pl.pallas_call(
        functools.partial(grads_kernel, rank),
        out_shape=[jax.ShapeDtypeStruct((half, 2 * rank, owned), jnp.bfloat16)] * 2,
        in_specs=[SMEM] + [VMEM] * 3,
        out_specs=[VMEM] * 2,
        compiler_params=pltpu.CompilerParams(vmem_limit_bytes=16 * MIB),
        name="grads",
    )(core, own, own_pre, modulated)
    theirs = lax.ppermute(theirs, "c", [(0, 1), (1, 0)])
    parts = (mine.astype(jnp.float32) + theirs.astype(jnp.float32)).astype(jnp.bfloat16)
    parts = lax.all_to_all(parts, CHIPS, 0, 0, tiled=True)
    ahead, behind, parts = lax.optimization_barrier((ahead, behind, parts))
    far_ahead, far_behind = shifted(ahead[share:], 1), shifted(behind[share:], -1)
    down_grad, up_grad = pl.pallas_call(
        functools.partial(total_kernel, rank, grad_scale),
        out_shape=[jax.ShapeDtypeStruct((1, owned, rank), jnp.float32)] * 2,
        in_specs=[VMEM],
        out_specs=[VMEM] * 2,
        name="total",
    )(parts)
    input_grads = pl.pallas_call(
        input_grads_kernel,
        out_shape=jax.ShapeDtypeStruct((1, tokens, width), jnp.bfloat16),
        in_specs=[SMEM] + [VMEM] * 5,
        out_specs=VMEM,
        compiler_params=pltpu.CompilerParams(vmem_limit_bytes=8 * MIB),
        name="input_grads",
    )(place, near_grads, ahead, behind, far_ahead, far_behind)
    return input_grads, down_grad, up_grad


def solution(mesh):
    split = Mesh(mesh.devices.reshape(SIZES), AXES)
    blocks = ("y", "zh")
    return jax.shard_map(
        per_device,
        mesh=split,
        in_specs=(
            P(blocks, GROUP, None),
            P(GROUP, None),
            P(blocks, GROUP, None),
            P(blocks, GROUP, None),
            P(blocks, GROUP, None),
            P(blocks, None, None),
            P(blocks, None, None),
            P(GROUP, None),
        ),
        out_specs=(P(blocks, GROUP, None), P(blocks, GROUP, None), P(blocks, GROUP, None)),
        check_vma=False,
    )
```

```python
import functools
import math

import jax
import jax.numpy as jnp
from jax import lax
from jax.experimental import pallas as pl
from jax.experimental.pallas import tpu as pltpu
from jax.sharding import Mesh, PartitionSpec as P

EPSILON = 1e-06
AXES = ("y", "zh", "zl", "x", "c")
SIZES = (8, 4, 2, 4, 2)
STAGES, BLOCKS, CORES = SIZES[0], SIZES[1], SIZES[4]
GROUP = ("zl", "x", "c")
CHIPS = ("zl", "x")
PLANE = ("zh", "zl", "x", "c")
MEMBERS = 16
ROWS = 32
CHUNK = 512
PIECES = 4
HEAD_ROWS = 1408
ROW_DOT = (((1,), (0,)), ((), ()))
LAST_DIMS = (((1,), (1,)), ((), ()))
FIRST_DIMS = (((0,), (0,)), ((), ()))
SLOPE = math.sqrt(2.0 / math.pi)
CUBIC = 0.044715
MIB = 2**20


def dot(left, right, dims=ROW_DOT):
    return lax.dot_general(left, right, dims, preferred_element_type=jnp.float32)


def per_batch_modulation(from_table, to_table, level_pairs):
    ladder = jnp.arange(from_table.shape[0], dtype=jnp.int32)[None, :]
    hot_from = (level_pairs[:, 0:1] == ladder).astype(jnp.bfloat16)
    hot_to = (level_pairs[:, 1:2] == ladder).astype(jnp.bfloat16)
    return dot(hot_from, from_table), dot(hot_to, to_table)


def slab_kernel(width, rank, weight, down, up, head, rest):
    count = head.shape[0]
    turned = weight[...].T
    head[...] = turned[:count, :]
    rest[: width - count, :] = turned[count:, :]
    rest[width - count : width - count + rank, :] = down[...].T
    rest[width - count + rank :, :] = up[...]


RING = (0, -1, -2, -3, -4, 1, 2, 3)


def ring_bundle(piece):
    ring = SIZES[1] * SIZES[2]

    def step(value, turn):
        return lax.ppermute(value, ("zh", "zl"), [(i, (i + turn) % ring) for i in range(ring)])

    up_1, down_1 = step(piece, 1), step(piece, -1)
    up_2, down_2 = step(up_1, 1), step(down_1, -1)
    up_3, down_3 = step(up_2, 1), step(down_2, -1)
    return jnp.stack([piece, up_1, up_2, up_3, step(up_3, 1), down_1, down_2, down_3])


def row_bundles(bundle):
    row, middle = SIZES[3], bundle.shape[0] // 2

    def step(value, turn):
        return lax.ppermute(value, "x", [(i, (i + turn) % row) for i in range(row)])

    before, after = step(bundle, 1), step(bundle, -1)
    return [bundle, before, after, step(before[:middle], 1), step(after[middle:], -1)]


def place_kernel(ring_place, row_place, core, *refs):
    bundles, (out, staged, sems) = refs[:-3], refs[-3:]
    ring, row = SIZES[1] * SIZES[2], SIZES[3]
    middle = len(RING) // 2
    copies = []
    for n, bundle in enumerate(bundles):
        kind, other = n % 5, n // 5
        turns = RING[:middle] if kind == 3 else RING[middle:] if kind == 4 else RING
        x = lax.rem(row_place[0] + (0, row - 1, 1, 2, 2)[kind], row)
        c = lax.rem(core[0] + other, CORES)
        for m, turn in enumerate(turns):
            z = lax.rem(ring_place[0] + turn + ring, ring)
            member = (lax.rem(z, SIZES[2]) * row + x) * CORES + c
            held = staged.at[len(copies)]
            copies.append(
                (
                    pltpu.make_async_copy(bundle.at[m], held, sems.at[0, n, m]),
                    pltpu.make_async_copy(held, out.at[z // SIZES[2], member], sems.at[1, n, m]),
                )
            )
    for arrive, _ in copies:
        arrive.start()
    for arrive, leave in copies:
        arrive.wait()
        leave.start()
    for _, leave in copies:
        leave.wait()


def relay_block(b, batches, width, rank, rows, times, up_of, g, d, h, mod, inv, g_keep, u_keep):
    owned = width // MEMBERS
    u = (d[b, rows, :] * g[...].astype(jnp.float32)).astype(jnp.bfloat16)
    u_keep[b] = u
    up = jnp.concatenate([up_of(i) for i in range(MEMBERS)], axis=0)
    low = dot(u, up).astype(jnp.bfloat16)
    joined = jnp.concatenate([u, low], axis=1)
    scaled, total = [], None
    for i in range(MEMBERS):
        c = pl.ds(i * owned, owned)
        grad = times(joined, i)
        scale = [1.0 + mod[b, pl.ds(m, 1), pl.ds(width + i * owned, owned)] for m in batches]
        pieces = [grad[n * ROWS : (n + 1) * ROWS] * scale[n] for n in range(len(batches))]
        grad = pieces[0] if len(pieces) == 1 else jnp.concatenate(pieces, axis=0)
        scaled.append(grad)
        part = grad * h[b, rows, c]
        total = part if total is None else total + part
    centred = jnp.sum(total, axis=1, keepdims=True) * (1.0 / width)
    rms = inv[b, rows, :]
    for i in range(MEMBERS):
        c = pl.ds(i * owned, owned)
        value = g[:, c].astype(jnp.float32) + rms * (scaled[i] - h[b, rows, c] * centred)
        value = value.astype(jnp.bfloat16)
        g[:, c] = value
        g_keep[b, :, c] = value


def first_kernel(
    batches, width, rank, stage, place, x, mod, target, heads, rests, own, d, h, inv, gs, us, *rest
):
    gouts, (g, g_keep, u_keep, preact, near, fetched, stored) = rest[:batches], rest[batches:]
    share = batches * ROWS
    per_chunk = CHUNK // heads.shape[3]
    count = heads.shape[2]
    quarter = MEMBERS // PIECES
    own_copy = pltpu.make_async_copy(rests.at[place[0], :, width - count :, :], own, stored.at[2, 0])

    def fetch(step, piece):
        members = pl.ds(piece * quarter, quarter)
        slot = lax.rem(step, 2)
        b = BLOCKS - 1 - step
        return (
            pltpu.make_async_copy(heads.at[b, members], near.at[slot, members, :count, :], fetched.at[slot, 0, piece]),
            pltpu.make_async_copy(rests.at[b, members], near.at[slot, members, count:, :], fetched.at[slot, 1, piece]),
        )

    def store_u(b):
        return pltpu.make_async_copy(u_keep.at[b], us.at[b], stored.at[0, b])

    def store_g(b):
        return pltpu.make_async_copy(g_keep.at[b], gs.at[b], stored.at[1, b])

    def block(step, carry):
        b = BLOCKS - 1 - step
        slot = lax.rem(step, 2)
        for piece in range(PIECES):
            for copy in fetch(step, piece):
                copy.wait()

        @pl.when(step < BLOCKS - 1)
        def ahead():
            for piece in range(PIECES):
                for copy in fetch(step + 1, piece):
                    copy.start()

        def slab(i):
            return near.at[slot, i]

        pieces = []
        for m in range(batches):
            r = pl.ds(m * ROWS, ROWS)
            values = x[b, r, :].astype(jnp.float32)
            rms = lax.rsqrt(jnp.mean(values * values, axis=1, keepdims=True) + EPSILON)
            normed = values * rms
            h[b, r, :] = normed
            inv[b, r, :] = jnp.broadcast_to(rms, (ROWS, inv.shape[2]))
            shift = mod[b, pl.ds(m, 1), 0:width]
            scale = mod[b, pl.ds(m, 1), width : 2 * width]
            pieces.append((normed * (1.0 + scale) + shift).astype(jnp.bfloat16))
        modulated = jnp.concatenate(pieces, axis=0)
        down = jnp.concatenate([slab(i)[width : width + rank, :] for i in range(MEMBERS)], axis=1)
        low = dot(modulated, down, LAST_DIMS).astype(jnp.bfloat16)
        for j in range(width // CHUNK):
            c = pl.ds(j * CHUNK, CHUNK)
            up = jnp.concatenate([slab(j * per_chunk + i)[width + rank :, :] for i in range(per_chunk)], axis=0)
            weight = jnp.concatenate([slab(i)[c, :] for i in range(MEMBERS)], axis=1)
            preact[:, c] = dot(weight, modulated, LAST_DIMS).T + dot(low, up, LAST_DIMS)
        for j in range(width // CHUNK):
            c = pl.ds(j * CHUNK, CHUNK)
            for m in range(batches):
                r = pl.ds(m * ROWS, ROWS)
                pre = preact[r, c]
                squared = pre * pre
                bent = jnp.tanh(SLOPE * pre * (1.0 + CUBIC * squared))
                half = 0.5 * (1.0 + bent)
                slope = half + 0.5 * pre * (1.0 - bent * bent) * (SLOPE * (1.0 + 3.0 * CUBIC * squared))
                gate = mod[b, pl.ds(m, 1), pl.ds(2 * width + j * CHUNK, CHUNK)]
                d[b, r, c] = slope * gate
                preact[r, c] = gate * (pre * half)

        @pl.when(step == 0)
        def close():
            out = x[b, pl.ds(0, share), :].astype(jnp.float32) + preact[...]
            g[...] = (out - target[...].astype(jnp.float32)).astype(jnp.bfloat16)

        @pl.when(stage[0] == STAGES - 1)
        def relay():
            relay_block(
                b,
                range(batches),
                width,
                rank,
                pl.ds(0, share),
                lambda value, i: dot(value, slab(i)[: width + rank, :]),
                lambda i: slab(i)[width + rank :, :],
                g,
                d,
                h,
                mod,
                inv,
                g_keep,
                u_keep,
            )
            store_u(b).start()
            store_g(b).start()

        return carry

    for piece in range(PIECES):
        for copy in fetch(0, piece):
            copy.start()
    own_copy.start()
    lax.fori_loop(0, BLOCKS, block, 0)
    own_copy.wait()
    for m in range(batches):
        gouts[m][...] = g[m * ROWS : (m + 1) * ROWS, :]

    @pl.when(stage[0] == STAGES - 1)
    def finish():
        for b in range(BLOCKS):
            store_u(b).wait()
            store_g(b).wait()


def relay_kernel(
    active_stage, m, width, rank, stage, gin, heads, rests, d, h, mod, inv, gs_in, us_in, gout, gs, us, g_keep, u_keep, stored
):
    rows = pl.ds(m * ROWS, ROWS)

    def store_u(b):
        return pltpu.make_async_copy(u_keep.at[b], us.at[b, rows, :], stored.at[0, b])

    def store_g(b):
        return pltpu.make_async_copy(g_keep.at[b], gs.at[b, rows, :], stored.at[1, b])

    def block(step, carry):
        b = BLOCKS - 1 - step
        count = heads.shape[2]
        last = width + rank - count

        def times(value, i):
            return dot(value[:, :count], heads[b, i]) + dot(value[:, count:], rests[b, i, :last, :])

        relay_block(
            b, [m], width, rank, rows, times, lambda i: rests[b, i, last:, :], gout, d, h, mod, inv, g_keep, u_keep
        )
        store_u(b).start()
        store_g(b).start()
        return carry

    @pl.when(stage[0] == active_stage)
    def run():
        gout[...] = gin[...]
        lax.fori_loop(0, BLOCKS, block, 0)
        for b in range(BLOCKS):
            store_u(b).wait()
            store_g(b).wait()


def grads_kernel(rank, core, own, pre_ref, mixed_ref, mine, theirs):
    down = jnp.concatenate([own[i, :rank, :] for i in range(MEMBERS)], axis=1)
    up = jnp.concatenate([own[i, rank:, :] for i in range(MEMBERS)], axis=0)
    pre, mixed = pre_ref[...], mixed_ref[...]
    lowrank = dot(mixed, down, LAST_DIMS).astype(jnp.bfloat16)
    grad_low = dot(pre, up).astype(jnp.bfloat16)
    owned = own.shape[2]
    for row, (left, right) in ((0, (grad_low, mixed)), (rank, (lowrank, pre))):
        part = dot(left.T, right).astype(jnp.bfloat16)
        for i in range(MEMBERS // CORES):
            pair = [part[:, (CORES * i + c) * owned : (CORES * i + c + 1) * owned] for c in range(CORES)]
            mine[i, row : row + rank, :] = jnp.where(core[0] == 0, pair[0], pair[1])
            theirs[i, row : row + rank, :] = jnp.where(core[0] == 0, pair[1], pair[0])


def split_kernel(place, core, kept, own, ahead, behind, passed, sems):
    passed[0] = core[0]
    rows = kept.shape[1]
    half = rows // 2

    def piece(n, turn, first, count, target, start):
        source = kept.at[lax.rem(place[0] + turn, BLOCKS), pl.ds(first, count), :]
        return pltpu.make_async_copy(source, target.at[pl.ds(start, count), :], sems.at[n])

    copies = [
        piece(0, 0, 0, rows, own, 0),
        piece(1, 1, 0, rows, ahead, 0),
        piece(2, 2, 0, half, ahead, rows),
        piece(3, 3, 0, rows, behind, 0),
        piece(4, 2, half, half, behind, rows),
    ]
    for copy in copies:
        copy.start()
    for copy in copies:
        copy.wait()


def input_grads_kernel(place, own, ahead, behind, far_ahead, far_behind, out):
    rows = own.shape[0]
    half = rows // 2
    for turn, first, value in (
        (0, 0, own[...]),
        (1, 0, ahead[:rows, :]),
        (2, 0, far_ahead[...]),
        (2, half, far_behind[...]),
        (3, 0, behind[:rows, :]),
    ):
        start = pl.multiple_of(lax.rem(place[0] - turn + BLOCKS, BLOCKS) * rows + first, half)
        out[0, pl.ds(start, value.shape[0]), :] = value


def total_kernel(rank, scale, parts, down, up):
    total = jnp.sum(parts[...].astype(jnp.float32), axis=0) * scale
    down[0] = total[:rank, :].T
    up[0] = total[rank:, :].T


VMEM = pl.BlockSpec(memory_space=pltpu.VMEM)
ANY = pl.BlockSpec(memory_space=pl.ANY)
HBM = pl.BlockSpec(memory_space=pltpu.HBM)
SMEM = pl.BlockSpec(memory_space=pltpu.SMEM)


def resident(value):
    return pltpu.with_memory_space_constraint(value, pltpu.VMEM)


def far(value):
    return pltpu.with_memory_space_constraint(value, pltpu.HBM)


def per_device(block_inputs, target, frozen_weight, adapter_down, adapter_up, start_modulation, finish_modulation, level_pairs):
    stage = lax.axis_index("y")
    place = lax.axis_index("zh")
    core = lax.axis_index("c")
    tokens, width = block_inputs.shape[1:]
    owned, rank = adapter_down.shape[1:]
    share = tokens // BLOCKS
    batches = share // ROWS
    grad_scale = 1.0 / math.sqrt(tokens * MEMBERS)

    rest_rows = width + 2 * rank - HEAD_ROWS
    head, rest = pl.pallas_call(
        functools.partial(slab_kernel, width, rank),
        out_shape=[
            jax.ShapeDtypeStruct((HEAD_ROWS, owned), jnp.bfloat16),
            jax.ShapeDtypeStruct((rest_rows, owned), jnp.bfloat16),
        ],
        in_specs=[VMEM] * 3,
        out_specs=[VMEM] * 2,
        name="slab",
    )(frozen_weight[0], adapter_down[0], adapter_up[0])
    heads = lax.all_gather(head, PLANE, axis=0, tiled=True).reshape(BLOCKS, MEMBERS, HEAD_ROWS, owned)
    picked = per_batch_modulation(start_modulation[0], finish_modulation[0], level_pairs)
    own_mod = picked[0] + picked[1]
    extra = jnp.stack([part.astype(jnp.bfloat16) for part in picked], axis=1).reshape(BLOCKS, -1, width)
    extra_rows = extra.shape[1]
    gap = jnp.zeros((BLOCKS, -extra_rows % 16, width), jnp.bfloat16)
    x = jnp.concatenate([block_inputs[0].reshape(BLOCKS, share, width), extra, gap], axis=1)
    x, bundle = lax.optimization_barrier((x, ring_bundle(rest)))
    x = lax.all_to_all(x, "zh", 0, 0, tiled=True)
    mod = x[:, share : share + extra_rows].reshape(BLOCKS, batches, 2, 3 * width).astype(jnp.float32)
    mod = mod[:, :, 0] + mod[:, :, 1]
    bundles = row_bundles(bundle)
    bundles = bundles + [lax.ppermute(value, "c", [(0, 1), (1, 0)]) for value in bundles]
    indices = [lax.axis_index(("zh", "zl")), lax.axis_index("x"), core]
    rests = pl.pallas_call(
        place_kernel,
        out_shape=pltpu.HBM((BLOCKS, MEMBERS, rest_rows, owned), jnp.bfloat16),
        in_specs=[SMEM] * 3 + [ANY] * len(bundles),
        out_specs=HBM,
        scratch_shapes=[
            pltpu.VMEM((BLOCKS * MEMBERS, rest_rows, owned), jnp.bfloat16),
            pltpu.SemaphoreType.DMA((2, len(bundles), len(RING))),
        ],
        compiler_params=pltpu.CompilerParams(vmem_limit_bytes=20 * MIB),
        name="place",
    )(*[index.astype(jnp.int32).reshape(1) for index in indices], *bundles)

    own_target = lax.dynamic_slice_in_dim(target, place * share, share, 0)

    values = block_inputs[0].astype(jnp.float32)
    normed = values * lax.rsqrt(jnp.mean(values * values, axis=1, keepdims=True) + EPSILON)
    row_mod = jnp.repeat(own_mod[:, : 2 * width], ROWS, axis=0)
    modulated = (normed * (1.0 + row_mod[:, width:]) + row_mod[:, :width]).astype(jnp.bfloat16)
    stage, place, core = (index.astype(jnp.int32).reshape(1) for index in (stage, place, core))
    x, mod, stage, place, core, own_target, modulated = lax.optimization_barrier(
        (x, mod, stage, place, core, own_target, modulated)
    )

    heads_near, rests_near, mod_near = resident(heads), resident(rests), resident(mod)
    kept_shape = (BLOCKS, share, width)
    own, d, h, inv, gs, us, *sent = pl.pallas_call(
        functools.partial(first_kernel, batches, width, rank),
        out_shape=[
            pltpu.VMEM((MEMBERS, 2 * rank, owned), jnp.bfloat16),
            pltpu.VMEM(kept_shape, jnp.float32),
            pltpu.VMEM(kept_shape, jnp.float32),
            pltpu.VMEM((BLOCKS, share, owned), jnp.float32),
            pltpu.HBM(kept_shape, jnp.bfloat16),
            pltpu.HBM(kept_shape, jnp.bfloat16),
        ]
        + [pltpu.VMEM((ROWS, width), jnp.bfloat16)] * batches,
        in_specs=[SMEM] * 2 + [VMEM] * 3 + [HBM] * 2,
        out_specs=[VMEM] * 4 + [HBM] * 2 + [VMEM] * batches,
        scratch_shapes=[
            pltpu.VMEM((share, width), jnp.bfloat16),
            pltpu.VMEM(kept_shape, jnp.bfloat16),
            pltpu.VMEM(kept_shape, jnp.bfloat16),
            pltpu.VMEM((share, width), jnp.float32),
            pltpu.VMEM((2, MEMBERS, width + 2 * rank, owned), jnp.bfloat16),
            pltpu.SemaphoreType.DMA((2, 2, PIECES)),
            pltpu.SemaphoreType.DMA((3, BLOCKS)),
        ],
        compiler_params=pltpu.CompilerParams(vmem_limit_bytes=26 * MIB),
        cost_estimate=pl.CostEstimate(flops=4 * BLOCKS * share * width * width, bytes_accessed=40 * MIB, transcendentals=0),
        name="first",
    )(stage, place, x, mod_near, own_target, far(heads), far(rests))

    d_near, h_near, inv_near = (resident(v) for v in (d, h, inv))

    def relay(active_stage, m, gin, gs, us):
        return pl.pallas_call(
            functools.partial(relay_kernel, active_stage, m, width, rank),
            out_shape=[pltpu.VMEM((ROWS, width), jnp.bfloat16)] + [pltpu.HBM(kept_shape, jnp.bfloat16)] * 2,
            in_specs=[SMEM] + [VMEM] * 7 + [HBM] * 2,
            out_specs=[VMEM] + [HBM] * 2,
            scratch_shapes=[
                pltpu.VMEM((BLOCKS, ROWS, width), jnp.bfloat16),
                pltpu.VMEM((BLOCKS, ROWS, width), jnp.bfloat16),
                pltpu.SemaphoreType.DMA((2, BLOCKS)),
            ],
            input_output_aliases={8: 1, 9: 2},
            compiler_params=pltpu.CompilerParams(vmem_limit_bytes=4 * MIB),
            cost_estimate=pl.CostEstimate(flops=2 * BLOCKS * ROWS * width * width, bytes_accessed=4 * MIB, transcendentals=0),
            name="relay",
        )(stage, resident(gin), heads_near, rests_near, d_near, h_near, mod_near, inv_near, far(gs), far(us))

    _, gs, us = relay(STAGES, 0, sent[0], gs, us)
    for step in range(1, STAGES):
        arrived = [lax.ppermute(out, "y", [(STAGES - step, STAGES - 1 - step)]) for out in sent]
        sent = []
        for m in range(batches):
            gout, gs, us = relay(STAGES - 1 - step, m, arrived[m], gs, us)
            sent.append(gout)

    gs, us, modulated = lax.optimization_barrier((gs, us, modulated))
    own_pre = lax.all_to_all(us.reshape(tokens, width), "zh", 0, 0, tiled=True)
    def shifted(value, turn):
        return lax.ppermute(value, "zh", [(i, (i + turn) % BLOCKS) for i in range(BLOCKS)])

    own_pre, gs = lax.optimization_barrier((own_pre, gs))
    packed = (share + share // 2, width)
    near_grads, ahead, behind, core = pl.pallas_call(
        split_kernel,
        out_shape=[pltpu.VMEM((share, width), jnp.bfloat16)]
        + [pltpu.VMEM(packed, jnp.bfloat16)] * 2
        + [jax.ShapeDtypeStruct((1,), jnp.int32)],
        in_specs=[SMEM] * 2 + [HBM],
        out_specs=[VMEM] * 3 + [SMEM],
        scratch_shapes=[pltpu.SemaphoreType.DMA((5,))],
        compiler_params=pltpu.CompilerParams(vmem_limit_bytes=4 * MIB),
        name="split",
    )(place, core, far(gs))
    ahead, behind = shifted(ahead, 1), shifted(behind, -1)

    half = MEMBERS // CORES
    mine, theirs = pl.pallas_call(
        functools.partial(grads_kernel, rank),
        out_shape=[jax.ShapeDtypeStruct((half, 2 * rank, owned), jnp.bfloat16)] * 2,
        in_specs=[SMEM] + [VMEM] * 3,
        out_specs=[VMEM] * 2,
        compiler_params=pltpu.CompilerParams(vmem_limit_bytes=16 * MIB),
        name="grads",
    )(core, own, own_pre, modulated)
    theirs = lax.ppermute(theirs, "c", [(0, 1), (1, 0)])
    parts = (mine.astype(jnp.float32) + theirs.astype(jnp.float32)).astype(jnp.bfloat16)
    parts = lax.all_to_all(parts, CHIPS, 0, 0, tiled=True)
    ahead, behind, parts = lax.optimization_barrier((ahead, behind, parts))
    far_ahead, far_behind = shifted(ahead[share:], 1), shifted(behind[share:], -1)
    down_grad, up_grad = pl.pallas_call(
        functools.partial(total_kernel, rank, grad_scale),
        out_shape=[jax.ShapeDtypeStruct((1, owned, rank), jnp.float32)] * 2,
        in_specs=[VMEM],
        out_specs=[VMEM] * 2,
        name="total",
    )(parts)
    input_grads = pl.pallas_call(
        input_grads_kernel,
        out_shape=jax.ShapeDtypeStruct((1, tokens, width), jnp.bfloat16),
        in_specs=[SMEM] + [VMEM] * 5,
        out_specs=VMEM,
        compiler_params=pltpu.CompilerParams(vmem_limit_bytes=8 * MIB),
        name="input_grads",
    )(place, near_grads, ahead, behind, far_ahead, far_behind)
    return input_grads, down_grad, up_grad


def solution(mesh):
    split = Mesh(mesh.devices.reshape(SIZES), AXES)
    blocks = ("y", "zh")
    return jax.shard_map(
        per_device,
        mesh=split,
        in_specs=(
            P(blocks, GROUP, None),
            P(GROUP, None),
            P(blocks, GROUP, None),
            P(blocks, GROUP, None),
            P(blocks, GROUP, None),
            P(blocks, None, None),
            P(blocks, None, None),
            P(GROUP, None),
        ),
        out_specs=(P(blocks, GROUP, None), P(blocks, GROUP, None), P(blocks, GROUP, None)),
        check_vma=False,
    )
```

```python
import functools
import math

import jax
import jax.numpy as jnp
from jax import lax
from jax.experimental import pallas as pl
from jax.experimental.pallas import tpu as pltpu
from jax.sharding import Mesh, PartitionSpec as P

EPSILON = 1e-06
AXES = ("y", "zh", "zl", "x", "c")
SIZES = (8, 4, 2, 4, 2)
STAGES, BLOCKS, CORES = SIZES[0], SIZES[1], SIZES[4]
GROUP = ("zl", "x", "c")
CHIPS = ("zl", "x")
PLANE = ("zh", "zl", "x", "c")
MEMBERS = 16
ROWS = 32
CHUNK = 512
PIECES = 4
HEAD_ROWS = 1664
ROW_DOT = (((1,), (0,)), ((), ()))
LAST_DIMS = (((1,), (1,)), ((), ()))
FIRST_DIMS = (((0,), (0,)), ((), ()))
SLOPE = math.sqrt(2.0 / math.pi)
CUBIC = 0.044715
MIB = 2**20


def dot(left, right, dims=ROW_DOT):
    return lax.dot_general(left, right, dims, preferred_element_type=jnp.float32)


def per_batch_modulation(from_table, to_table, level_pairs):
    ladder = jnp.arange(from_table.shape[0], dtype=jnp.int32)[None, :]
    hot_from = (level_pairs[:, 0:1] == ladder).astype(jnp.bfloat16)
    hot_to = (level_pairs[:, 1:2] == ladder).astype(jnp.bfloat16)
    return dot(hot_from, from_table) + dot(hot_to, to_table)


def slab_kernel(width, rank, weight, down, up, head, rest):
    count = head.shape[0]
    turned = weight[...].T
    head[...] = turned[:count, :]
    rest[: width - count, :] = turned[count:, :]
    rest[width - count : width - count + rank, :] = down[...].T
    rest[width - count + rank :, :] = up[...]


RING = (0, -1, -2, -3, -4, 1, 2, 3)


def ring_bundle(piece):
    ring = SIZES[1] * SIZES[2]

    def step(value, turn):
        return lax.ppermute(value, ("zh", "zl"), [(i, (i + turn) % ring) for i in range(ring)])

    up_1, down_1 = step(piece, 1), step(piece, -1)
    up_2, down_2 = step(up_1, 1), step(down_1, -1)
    up_3, down_3 = step(up_2, 1), step(down_2, -1)
    return jnp.stack([piece, up_1, up_2, up_3, step(up_3, 1), down_1, down_2, down_3])


def row_bundles(bundle):
    row, middle = SIZES[3], bundle.shape[0] // 2

    def step(value, turn):
        return lax.ppermute(value, "x", [(i, (i + turn) % row) for i in range(row)])

    before, after = step(bundle, 1), step(bundle, -1)
    return [bundle, before, after, step(before[:middle], 1), step(after[middle:], -1)]


def place_kernel(ring_place, row_place, core, *refs):
    bundles, (out, sems) = refs[:-2], refs[-2:]
    ring, row = SIZES[1] * SIZES[2], SIZES[3]
    middle = len(RING) // 2
    copies = []
    for n, bundle in enumerate(bundles):
        kind, other = n % 5, n // 5
        turns = RING[:middle] if kind == 3 else RING[middle:] if kind == 4 else RING
        x = lax.rem(row_place[0] + (0, row - 1, 1, 2, 2)[kind], row)
        c = lax.rem(core[0] + other, CORES)
        for m, turn in enumerate(turns):
            z = lax.rem(ring_place[0] + turn + ring, ring)
            member = (lax.rem(z, SIZES[2]) * row + x) * CORES + c
            copies.append(pltpu.make_async_copy(bundle.at[m], out.at[z // SIZES[2], member], sems.at[n, m]))
    for copy in copies:
        copy.start()
    for copy in copies:
        copy.wait()


def relay_block(b, batches, width, rank, rows, times, up_of, g, d, h, mod, inv, g_keep, u_keep, l_keep):
    owned = width // MEMBERS
    u = (d[b, rows, :] * g[...].astype(jnp.float32)).astype(jnp.bfloat16)
    u_keep[b] = u
    up = jnp.concatenate([up_of(i) for i in range(MEMBERS)], axis=0)
    low = dot(u, up).astype(jnp.bfloat16)
    l_keep[b] = low
    joined = jnp.concatenate([u, low], axis=1)
    scaled, total = [], None
    for i in range(MEMBERS):
        c = pl.ds(i * owned, owned)
        grad = times(joined, i)
        scale = [1.0 + mod[b, pl.ds(m, 1), pl.ds(width + i * owned, owned)] for m in batches]
        pieces = [grad[n * ROWS : (n + 1) * ROWS] * scale[n] for n in range(len(batches))]
        grad = pieces[0] if len(pieces) == 1 else jnp.concatenate(pieces, axis=0)
        scaled.append(grad)
        part = grad * h[b, rows, c]
        total = part if total is None else total + part
    centred = jnp.sum(total, axis=1, keepdims=True) * (1.0 / width)
    rms = inv[b, rows, :]
    for i in range(MEMBERS):
        c = pl.ds(i * owned, owned)
        value = g[:, c].astype(jnp.float32) + rms * (scaled[i] - h[b, rows, c] * centred)
        value = value.astype(jnp.bfloat16)
        g[:, c] = value
        g_keep[b, :, c] = value


def first_kernel(
    batches, width, rank, stage, x, mod, target, heads, rests, mixed, lows, d, h, inv, gs, us, ls, *rest
):
    gouts, (g, g_keep, u_keep, l_keep, preact, near, fetched, stored) = rest[:batches], rest[batches:]
    share = batches * ROWS
    per_chunk = CHUNK // heads.shape[3]
    count = heads.shape[2]
    quarter = MEMBERS // PIECES

    def fetch(step, piece):
        members = pl.ds(piece * quarter, quarter)
        slot = lax.rem(step, 2)
        b = BLOCKS - 1 - step
        return (
            pltpu.make_async_copy(heads.at[b, members], near.at[slot, members, :count, :], fetched.at[slot, 0, piece]),
            pltpu.make_async_copy(rests.at[b, members], near.at[slot, members, count:, :], fetched.at[slot, 1, piece]),
        )

    def store_u(b):
        return pltpu.make_async_copy(u_keep.at[b], us.at[b], stored.at[0, b])

    def store_g(b):
        return pltpu.make_async_copy(g_keep.at[b], gs.at[b], stored.at[1, b])

    def store_l(b):
        return pltpu.make_async_copy(l_keep.at[b], ls.at[b], stored.at[2, b])

    def block(step, carry):
        b = BLOCKS - 1 - step
        slot = lax.rem(step, 2)
        for piece in range(PIECES):
            for copy in fetch(step, piece):
                copy.wait()

        @pl.when(step < BLOCKS - 1)
        def ahead():
            for piece in range(PIECES):
                for copy in fetch(step + 1, piece):
                    copy.start()

        def slab(i):
            return near.at[slot, i]

        pieces = []
        for m in range(batches):
            r = pl.ds(m * ROWS, ROWS)
            values = x[b, r, :].astype(jnp.float32)
            rms = lax.rsqrt(jnp.mean(values * values, axis=1, keepdims=True) + EPSILON)
            normed = values * rms
            h[b, r, :] = normed
            inv[b, r, :] = jnp.broadcast_to(rms, (ROWS, inv.shape[2]))
            shift = mod[b, pl.ds(m, 1), 0:width]
            scale = mod[b, pl.ds(m, 1), width : 2 * width]
            pieces.append((normed * (1.0 + scale) + shift).astype(jnp.bfloat16))
        modulated = jnp.concatenate(pieces, axis=0)
        down = jnp.concatenate([slab(i)[width : width + rank, :] for i in range(MEMBERS)], axis=1)
        low = dot(modulated, down, LAST_DIMS).astype(jnp.bfloat16)
        mixed[b] = modulated
        lows[b] = low
        for j in range(width // CHUNK):
            c = pl.ds(j * CHUNK, CHUNK)
            up = jnp.concatenate([slab(j * per_chunk + i)[width + rank :, :] for i in range(per_chunk)], axis=0)
            weight = jnp.concatenate([slab(i)[c, :] for i in range(MEMBERS)], axis=1)
            preact[:, c] = dot(weight, modulated, LAST_DIMS).T + dot(low, up, LAST_DIMS)
        for j in range(width // CHUNK):
            c = pl.ds(j * CHUNK, CHUNK)
            for m in range(batches):
                r = pl.ds(m * ROWS, ROWS)
                pre = preact[r, c]
                squared = pre * pre
                bent = jnp.tanh(SLOPE * pre * (1.0 + CUBIC * squared))
                half = 0.5 * (1.0 + bent)
                slope = half + 0.5 * pre * (1.0 - bent * bent) * (SLOPE * (1.0 + 3.0 * CUBIC * squared))
                gate = mod[b, pl.ds(m, 1), pl.ds(2 * width + j * CHUNK, CHUNK)]
                d[b, r, c] = slope * gate
                preact[r, c] = gate * (pre * half)

        @pl.when(step == 0)
        def close():
            out = x[b].astype(jnp.float32) + preact[...]
            g[...] = (out - target[...].astype(jnp.float32)).astype(jnp.bfloat16)

        @pl.when(stage[0] == STAGES - 1)
        def relay():
            relay_block(
                b,
                range(batches),
                width,
                rank,
                pl.ds(0, share),
                lambda value, i: dot(value, slab(i)[: width + rank, :]),
                lambda i: slab(i)[width + rank :, :],
                g,
                d,
                h,
                mod,
                inv,
                g_keep,
                u_keep,
                l_keep,
            )
            store_u(b).start()
            store_g(b).start()
            store_l(b).start()

        return carry

    for piece in range(PIECES):
        for copy in fetch(0, piece):
            copy.start()
    lax.fori_loop(0, BLOCKS, block, 0)
    for m in range(batches):
        gouts[m][...] = g[m * ROWS : (m + 1) * ROWS, :]

    @pl.when(stage[0] == STAGES - 1)
    def finish():
        for b in range(BLOCKS):
            store_u(b).wait()
            store_g(b).wait()
            store_l(b).wait()


def relay_kernel(
    active_stage, m, width, rank, stage, gin, heads, rests, d, h, mod, inv, gs_in, us_in, ls_in, gout, gs, us, ls, g_keep, u_keep, l_keep, stored
):
    rows = pl.ds(m * ROWS, ROWS)

    def store_u(b):
        return pltpu.make_async_copy(u_keep.at[b], us.at[b, rows, :], stored.at[0, b])

    def store_g(b):
        return pltpu.make_async_copy(g_keep.at[b], gs.at[b, rows, :], stored.at[1, b])

    def store_l(b):
        return pltpu.make_async_copy(l_keep.at[b], ls.at[b, rows, :], stored.at[2, b])

    def block(step, carry):
        b = BLOCKS - 1 - step
        count = heads.shape[2]
        last = width + rank - count

        def times(value, i):
            return dot(value[:, :count], heads[b, i]) + dot(value[:, count:], rests[b, i, :last, :])

        relay_block(
            b, [m], width, rank, rows, times, lambda i: rests[b, i, last:, :], gout, d, h, mod, inv, g_keep, u_keep, l_keep
        )
        store_u(b).start()
        store_g(b).start()
        store_l(b).start()
        return carry

    @pl.when(stage[0] == active_stage)
    def run():
        gout[...] = gin[...]
        lax.fori_loop(0, BLOCKS, block, 0)
        for b in range(BLOCKS):
            store_u(b).wait()
            store_g(b).wait()
            store_l(b).wait()


def grads_kernel(rank, core, mixed, lows, us, ls, mine, theirs):
    owned = mine.shape[3]
    for b in range(BLOCKS):
        for row, left, right in ((0, ls[b], mixed[b]), (rank, lows[b], us[b])):
            part = dot(left.T, right).astype(jnp.bfloat16)
            for pair in range(MEMBERS // CORES):
                both = [part[:, (CORES * pair + c) * owned : (CORES * pair + c + 1) * owned] for c in range(CORES)]
                x, z = pair % SIZES[3], b * SIZES[2] + pair // SIZES[3]
                mine[x, z, row : row + rank, :] = jnp.where(core[0] == 0, both[0], both[1])
                theirs[x, z, row : row + rank, :] = jnp.where(core[0] == 0, both[1], both[0])


def split_kernel(place, kept, own, ahead, behind, sems):
    rows = kept.shape[1]
    half = rows // 2

    def piece(n, turn, first, count, target, start):
        source = kept.at[lax.rem(place[0] + turn, BLOCKS), pl.ds(first, count), :]
        return pltpu.make_async_copy(source, target.at[pl.ds(start, count), :], sems.at[n])

    copies = [
        piece(0, 0, 0, rows, own, 0),
        piece(1, 1, 0, rows, ahead, 0),
        piece(2, 2, 0, half, ahead, rows),
        piece(3, 3, 0, rows, behind, 0),
        piece(4, 2, half, half, behind, rows),
    ]
    for copy in copies:
        copy.start()
    for copy in copies:
        copy.wait()


def input_grads_kernel(place, own, ahead, behind, far_ahead, far_behind, out):
    rows = own.shape[0]
    half = rows // 2
    for turn, first, value in (
        (0, 0, own[...]),
        (1, 0, ahead[:rows, :]),
        (2, 0, far_ahead[...]),
        (2, half, far_behind[...]),
        (3, 0, behind[:rows, :]),
    ):
        start = pl.multiple_of(lax.rem(place[0] - turn + BLOCKS, BLOCKS) * rows + first, half)
        out[0, pl.ds(start, value.shape[0]), :] = value


def total_kernel(rank, scale, parts, down, up):
    total = jnp.sum(parts[...].astype(jnp.float32), axis=0) * scale
    down[0] = total[:rank, :].T
    up[0] = total[rank:, :].T


VMEM = pl.BlockSpec(memory_space=pltpu.VMEM)
ANY = pl.BlockSpec(memory_space=pl.ANY)
HBM = pl.BlockSpec(memory_space=pltpu.HBM)
SMEM = pl.BlockSpec(memory_space=pltpu.SMEM)


def resident(value):
    return pltpu.with_memory_space_constraint(value, pltpu.VMEM)


def far(value):
    return pltpu.with_memory_space_constraint(value, pltpu.HBM)


def per_device(block_inputs, target, frozen_weight, adapter_down, adapter_up, start_modulation, finish_modulation, level_pairs):
    stage = lax.axis_index("y")
    place = lax.axis_index("zh")
    core = lax.axis_index("c")
    tokens, width = block_inputs.shape[1:]
    owned, rank = adapter_down.shape[1:]
    share = tokens // BLOCKS
    batches = share // ROWS
    grad_scale = 1.0 / math.sqrt(tokens * MEMBERS)

    rest_rows = width + 2 * rank - HEAD_ROWS
    head, rest = pl.pallas_call(
        functools.partial(slab_kernel, width, rank),
        out_shape=[
            jax.ShapeDtypeStruct((HEAD_ROWS, owned), jnp.bfloat16),
            jax.ShapeDtypeStruct((rest_rows, owned), jnp.bfloat16),
        ],
        in_specs=[VMEM] * 3,
        out_specs=[VMEM] * 2,
        name="slab",
    )(frozen_weight[0], adapter_down[0], adapter_up[0])
    heads = lax.all_gather(head, PLANE, axis=0, tiled=True).reshape(BLOCKS, MEMBERS, HEAD_ROWS, owned)
    bundles = row_bundles(ring_bundle(rest))
    bundles = bundles + [lax.ppermute(value, "c", [(0, 1), (1, 0)]) for value in bundles]
    indices = [lax.axis_index(("zh", "zl")), lax.axis_index("x"), core]
    rests = pl.pallas_call(
        place_kernel,
        out_shape=pltpu.VMEM((BLOCKS, MEMBERS, rest_rows, owned), jnp.bfloat16),
        in_specs=[SMEM] * 3 + [ANY] * len(bundles),
        out_specs=VMEM,
        scratch_shapes=[pltpu.SemaphoreType.DMA((len(bundles), len(RING)))],
        compiler_params=pltpu.CompilerParams(vmem_limit_bytes=4 * MIB),
        name="place",
    )(*[index.astype(jnp.int32).reshape(1) for index in indices], *bundles)

    own_mod = per_batch_modulation(start_modulation[0], finish_modulation[0], level_pairs)
    mod = lax.all_to_all(own_mod, "zh", 0, 0, tiled=True).reshape(BLOCKS, batches, 3 * width)
    x = lax.all_to_all(block_inputs[0], "zh", 0, 0, tiled=True).reshape(BLOCKS, share, width)
    own_target = lax.dynamic_slice_in_dim(target, place * share, share, 0)

    stage, place, core = (index.astype(jnp.int32).reshape(1) for index in (stage, place, core))
    x, mod, stage, place, core, own_target = lax.optimization_barrier((x, mod, stage, place, core, own_target))

    heads_near, rests_near, mod_near = resident(heads), resident(rests), resident(mod)
    kept_shape = (BLOCKS, share, width)
    mixed, lows, d, h, inv, gs, us, ls, *sent = pl.pallas_call(
        functools.partial(first_kernel, batches, width, rank),
        out_shape=[
            jax.ShapeDtypeStruct(kept_shape, jnp.bfloat16),
            jax.ShapeDtypeStruct((BLOCKS, share, rank), jnp.bfloat16),
            pltpu.VMEM(kept_shape, jnp.float32),
            pltpu.VMEM(kept_shape, jnp.float32),
            pltpu.VMEM((BLOCKS, share, owned), jnp.float32),
            pltpu.HBM(kept_shape, jnp.bfloat16),
            pltpu.HBM(kept_shape, jnp.bfloat16),
            pltpu.HBM((BLOCKS, share, rank), jnp.bfloat16),
        ]
        + [pltpu.VMEM((ROWS, width), jnp.bfloat16)] * batches,
        in_specs=[SMEM] + [VMEM] * 3 + [HBM] * 2,
        out_specs=[VMEM] * 5 + [HBM] * 3 + [VMEM] * batches,
        scratch_shapes=[
            pltpu.VMEM((share, width), jnp.bfloat16),
            pltpu.VMEM(kept_shape, jnp.bfloat16),
            pltpu.VMEM(kept_shape, jnp.bfloat16),
            pltpu.VMEM((BLOCKS, share, rank), jnp.bfloat16),
            pltpu.VMEM((share, width), jnp.float32),
            pltpu.VMEM((2, MEMBERS, width + 2 * rank, owned), jnp.bfloat16),
            pltpu.SemaphoreType.DMA((2, 2, PIECES)),
            pltpu.SemaphoreType.DMA((3, BLOCKS)),
        ],
        compiler_params=pltpu.CompilerParams(vmem_limit_bytes=26 * MIB),
        cost_estimate=pl.CostEstimate(flops=4 * BLOCKS * share * width * width, bytes_accessed=40 * MIB, transcendentals=0),
        name="first",
    )(stage, x, mod_near, own_target, far(heads), far(rests))

    d_near, h_near, inv_near = (resident(v) for v in (d, h, inv))

    def relay(active_stage, m, gin, gs, us, ls):
        return pl.pallas_call(
            functools.partial(relay_kernel, active_stage, m, width, rank),
            out_shape=[pltpu.VMEM((ROWS, width), jnp.bfloat16)] + [
                pltpu.HBM(kept_shape, jnp.bfloat16),
                pltpu.HBM(kept_shape, jnp.bfloat16),
                pltpu.HBM((BLOCKS, share, rank), jnp.bfloat16),
            ],
            in_specs=[SMEM] + [VMEM] * 7 + [HBM] * 3,
            out_specs=[VMEM] + [HBM] * 3,
            scratch_shapes=[
                pltpu.VMEM((BLOCKS, ROWS, width), jnp.bfloat16),
                pltpu.VMEM((BLOCKS, ROWS, width), jnp.bfloat16),
                pltpu.VMEM((BLOCKS, ROWS, rank), jnp.bfloat16),
                pltpu.SemaphoreType.DMA((3, BLOCKS)),
            ],
            input_output_aliases={8: 1, 9: 2, 10: 3},
            compiler_params=pltpu.CompilerParams(vmem_limit_bytes=4 * MIB),
            cost_estimate=pl.CostEstimate(flops=2 * BLOCKS * ROWS * width * width, bytes_accessed=4 * MIB, transcendentals=0),
            name="relay",
        )(stage, resident(gin), heads_near, rests_near, d_near, h_near, mod_near, inv_near, far(gs), far(us), far(ls))

    _, gs, us, ls = relay(STAGES, 0, sent[0], gs, us, ls)
    for step in range(1, STAGES):
        arrived = [lax.ppermute(out, "y", [(STAGES - step, STAGES - 1 - step)]) for out in sent]
        sent = []
        for m in range(batches):
            gout, gs, us, ls = relay(STAGES - 1 - step, m, arrived[m], gs, us, ls)
            sent.append(gout)

    gs, us, ls, mixed, lows = lax.optimization_barrier((gs, us, ls, mixed, lows))

    def shifted(value, turn):
        return lax.ppermute(value, "zh", [(i, (i + turn) % BLOCKS) for i in range(BLOCKS)])

    packed = (share + share // 2, width)
    near_grads, ahead, behind = pl.pallas_call(
        split_kernel,
        out_shape=[pltpu.VMEM((share, width), jnp.bfloat16)] + [pltpu.VMEM(packed, jnp.bfloat16)] * 2,
        in_specs=[SMEM, HBM],
        out_specs=[VMEM] * 3,
        scratch_shapes=[pltpu.SemaphoreType.DMA((5,))],
        compiler_params=pltpu.CompilerParams(vmem_limit_bytes=4 * MIB),
        name="split",
    )(place, far(gs))
    ahead, behind = shifted(ahead, 1), shifted(behind, -1)

    row, ring = SIZES[3], SIZES[1] * SIZES[2]
    mine, theirs = pl.pallas_call(
        functools.partial(grads_kernel, rank),
        out_shape=[jax.ShapeDtypeStruct((row, ring, 2 * rank, owned), jnp.bfloat16)] * 2,
        in_specs=[SMEM] + [VMEM] * 4,
        out_specs=[VMEM] * 2,
        compiler_params=pltpu.CompilerParams(vmem_limit_bytes=24 * MIB),
        name="grads",
    )(core, mixed, lows, us, ls)
    theirs = lax.ppermute(theirs, "c", [(0, 1), (1, 0)])
    parts = (mine.astype(jnp.float32) + theirs.astype(jnp.float32)).astype(jnp.bfloat16)
    parts = lax.all_to_all(parts, "x", 0, 0, tiled=True)
    ahead, behind, parts = lax.optimization_barrier((ahead, behind, parts))
    parts = jnp.sum(parts.astype(jnp.float32), axis=0).astype(jnp.bfloat16)
    parts = lax.all_to_all(parts, ("zh", "zl"), 0, 0, tiled=True)
    far_ahead, far_behind = shifted(ahead[share:], 1), shifted(behind[share:], -1)
    down_grad, up_grad = pl.pallas_call(
        functools.partial(total_kernel, rank, grad_scale),
        out_shape=[jax.ShapeDtypeStruct((1, owned, rank), jnp.float32)] * 2,
        in_specs=[VMEM],
        out_specs=[VMEM] * 2,
        name="total",
    )(parts)
    input_grads = pl.pallas_call(
        input_grads_kernel,
        out_shape=jax.ShapeDtypeStruct((1, tokens, width), jnp.bfloat16),
        in_specs=[SMEM] + [VMEM] * 5,
        out_specs=VMEM,
        compiler_params=pltpu.CompilerParams(vmem_limit_bytes=8 * MIB),
        name="input_grads",
    )(place, near_grads, ahead, behind, far_ahead, far_behind)
    return input_grads, down_grad, up_grad


def solution(mesh):
    split = Mesh(mesh.devices.reshape(SIZES), AXES)
    blocks = ("y", "zh")
    return jax.shard_map(
        per_device,
        mesh=split,
        in_specs=(
            P(blocks, GROUP, None),
            P(GROUP, None),
            P(blocks, GROUP, None),
            P(blocks, GROUP, None),
            P(blocks, GROUP, None),
            P(blocks, None, None),
            P(blocks, None, None),
            P(GROUP, None),
        ),
        out_specs=(P(blocks, GROUP, None), P(blocks, GROUP, None), P(blocks, GROUP, None)),
        check_vma=False,
    )
```

```python
import functools
import math

import jax
import jax.numpy as jnp
from jax import lax
from jax.experimental import pallas as pl
from jax.experimental.pallas import tpu as pltpu
from jax.sharding import Mesh, PartitionSpec as P

EPSILON = 1e-06
AXES = ("y", "zh", "zl", "x", "c")
SIZES = (8, 4, 2, 4, 2)
STAGES, BLOCKS, CORES = SIZES[0], SIZES[1], SIZES[4]
GROUP = ("zl", "x", "c")
CHIPS = ("zl", "x")
PLANE = ("zh", "zl", "x", "c")
MEMBERS = 16
ROWS = 32
CHUNK = 512
PIECES = 4
HEAD_ROWS = 1664
ROW_DOT = (((1,), (0,)), ((), ()))
LAST_DIMS = (((1,), (1,)), ((), ()))
FIRST_DIMS = (((0,), (0,)), ((), ()))
SLOPE = math.sqrt(2.0 / math.pi)
CUBIC = 0.044715
MIB = 2**20


def dot(left, right, dims=ROW_DOT):
    return lax.dot_general(left, right, dims, preferred_element_type=jnp.float32)


def per_batch_modulation(from_table, to_table, level_pairs):
    ladder = jnp.arange(from_table.shape[0], dtype=jnp.int32)[None, :]
    hot_from = (level_pairs[:, 0:1] == ladder).astype(jnp.bfloat16)
    hot_to = (level_pairs[:, 1:2] == ladder).astype(jnp.bfloat16)
    return dot(hot_from, from_table) + dot(hot_to, to_table)


def slab_kernel(width, rank, weight, down, up, head, rest):
    count = head.shape[0]
    turned = weight[...].T
    head[...] = turned[:count, :]
    rest[: width - count, :] = turned[count:, :]
    rest[width - count : width - count + rank, :] = down[...].T
    rest[width - count + rank :, :] = up[...]


RING = (0, -1, -2, -3, -4, 1, 2, 3)


def ring_bundle(piece):
    ring = SIZES[1] * SIZES[2]

    def step(value, turn):
        return lax.ppermute(value, ("zh", "zl"), [(i, (i + turn) % ring) for i in range(ring)])

    up_1, down_1 = step(piece, 1), step(piece, -1)
    up_2, down_2 = step(up_1, 1), step(down_1, -1)
    up_3, down_3 = step(up_2, 1), step(down_2, -1)
    return jnp.stack([piece, up_1, up_2, up_3, step(up_3, 1), down_1, down_2, down_3])


def row_bundles(bundle):
    row, middle = SIZES[3], bundle.shape[0] // 2

    def step(value, turn):
        return lax.ppermute(value, "x", [(i, (i + turn) % row) for i in range(row)])

    before, after = step(bundle, 1), step(bundle, -1)
    return [bundle, before, after, step(before[:middle], 1), step(after[middle:], -1)]


def place_kernel(ring_place, row_place, core, *refs):
    bundles, (out, sems) = refs[:-2], refs[-2:]
    ring, row = SIZES[1] * SIZES[2], SIZES[3]
    middle = len(RING) // 2
    copies = []
    for n, bundle in enumerate(bundles):
        kind, other = n % 5, n // 5
        turns = RING[:middle] if kind == 3 else RING[middle:] if kind == 4 else RING
        x = lax.rem(row_place[0] + (0, row - 1, 1, 2, 2)[kind], row)
        c = lax.rem(core[0] + other, CORES)
        for m, turn in enumerate(turns):
            z = lax.rem(ring_place[0] + turn + ring, ring)
            member = (lax.rem(z, SIZES[2]) * row + x) * CORES + c
            copies.append(pltpu.make_async_copy(bundle.at[m], out.at[z // SIZES[2], member], sems.at[n, m]))
    for copy in copies:
        copy.start()
    for copy in copies:
        copy.wait()


def relay_block(b, batches, width, rank, rows, times, up_of, g, d, h, mod, inv, g_keep, u_keep, l_keep):
    owned = width // MEMBERS
    u = (d[b, rows, :] * g[...].astype(jnp.float32)).astype(jnp.bfloat16)
    u_keep[b] = u
    up = jnp.concatenate([up_of(i) for i in range(MEMBERS)], axis=0)
    low = dot(u, up).astype(jnp.bfloat16)
    l_keep[b] = low
    joined = jnp.concatenate([u, low], axis=1)
    scaled, total = [], None
    for i in range(MEMBERS):
        c = pl.ds(i * owned, owned)
        grad = times(joined, i)
        scale = [1.0 + mod[b, pl.ds(m, 1), pl.ds(width + i * owned, owned)] for m in batches]
        pieces = [grad[n * ROWS : (n + 1) * ROWS] * scale[n] for n in range(len(batches))]
        grad = pieces[0] if len(pieces) == 1 else jnp.concatenate(pieces, axis=0)
        scaled.append(grad)
        part = grad * h[b, rows, c]
        total = part if total is None else total + part
    centred = jnp.sum(total, axis=1, keepdims=True) * (1.0 / width)
    rms = inv[b, rows, :]
    for i in range(MEMBERS):
        c = pl.ds(i * owned, owned)
        value = g[:, c].astype(jnp.float32) + rms * (scaled[i] - h[b, rows, c] * centred)
        value = value.astype(jnp.bfloat16)
        g[:, c] = value
        g_keep[b, :, c] = value


def first_kernel(
    batches, width, rank, stage, x, mod, target, heads, rests, mixed, lows, d, h, inv, gs, us, ls, *rest
):
    gouts, (g, g_keep, u_keep, l_keep, preact, near, fetched, stored) = rest[:batches], rest[batches:]
    share = batches * ROWS
    per_chunk = CHUNK // heads.shape[3]
    count = heads.shape[2]
    quarter = MEMBERS // PIECES

    def fetch(step, piece):
        members = pl.ds(piece * quarter, quarter)
        slot = lax.rem(step, 2)
        b = BLOCKS - 1 - step
        return (
            pltpu.make_async_copy(heads.at[b, members], near.at[slot, members, :count, :], fetched.at[slot, 0, piece]),
            pltpu.make_async_copy(rests.at[b, members], near.at[slot, members, count:, :], fetched.at[slot, 1, piece]),
        )

    def store_u(b):
        return pltpu.make_async_copy(u_keep.at[b], us.at[b], stored.at[0, b])

    def store_g(b):
        return pltpu.make_async_copy(g_keep.at[b], gs.at[b], stored.at[1, b])

    def store_l(b):
        return pltpu.make_async_copy(l_keep.at[b], ls.at[b], stored.at[2, b])

    def block(step, carry):
        b = BLOCKS - 1 - step
        slot = lax.rem(step, 2)
        for piece in range(PIECES):
            for copy in fetch(step, piece):
                copy.wait()

        @pl.when(step < BLOCKS - 1)
        def ahead():
            for piece in range(PIECES):
                for copy in fetch(step + 1, piece):
                    copy.start()

        def slab(i):
            return near.at[slot, i]

        pieces = []
        for m in range(batches):
            r = pl.ds(m * ROWS, ROWS)
            values = x[b, r, :].astype(jnp.float32)
            rms = lax.rsqrt(jnp.mean(values * values, axis=1, keepdims=True) + EPSILON)
            normed = values * rms
            h[b, r, :] = normed
            inv[b, r, :] = jnp.broadcast_to(rms, (ROWS, inv.shape[2]))
            shift = mod[b, pl.ds(m, 1), 0:width]
            scale = mod[b, pl.ds(m, 1), width : 2 * width]
            pieces.append((normed * (1.0 + scale) + shift).astype(jnp.bfloat16))
        modulated = jnp.concatenate(pieces, axis=0)
        down = jnp.concatenate([slab(i)[width : width + rank, :] for i in range(MEMBERS)], axis=1)
        low = dot(modulated, down, LAST_DIMS).astype(jnp.bfloat16)
        mixed[b] = modulated
        lows[b] = low
        for j in range(width // CHUNK):
            c = pl.ds(j * CHUNK, CHUNK)
            up = jnp.concatenate([slab(j * per_chunk + i)[width + rank :, :] for i in range(per_chunk)], axis=0)
            weight = jnp.concatenate([slab(i)[c, :] for i in range(MEMBERS)], axis=1)
            preact[:, c] = dot(weight, modulated, LAST_DIMS).T + dot(low, up, LAST_DIMS)
        for j in range(width // CHUNK):
            c = pl.ds(j * CHUNK, CHUNK)
            for m in range(batches):
                r = pl.ds(m * ROWS, ROWS)
                pre = preact[r, c]
                squared = pre * pre
                bent = jnp.tanh(SLOPE * pre * (1.0 + CUBIC * squared))
                half = 0.5 * (1.0 + bent)
                slope = half + 0.5 * pre * (1.0 - bent * bent) * (SLOPE * (1.0 + 3.0 * CUBIC * squared))
                gate = mod[b, pl.ds(m, 1), pl.ds(2 * width + j * CHUNK, CHUNK)]
                d[b, r, c] = slope * gate
                preact[r, c] = gate * (pre * half)

        @pl.when(step == 0)
        def close():
            out = x[b].astype(jnp.float32) + preact[...]
            g[...] = (out - target[...].astype(jnp.float32)).astype(jnp.bfloat16)

        @pl.when(stage[0] == STAGES - 1)
        def relay():
            relay_block(
                b,
                range(batches),
                width,
                rank,
                pl.ds(0, share),
                lambda value, i: dot(value, slab(i)[: width + rank, :]),
                lambda i: slab(i)[width + rank :, :],
                g,
                d,
                h,
                mod,
                inv,
                g_keep,
                u_keep,
                l_keep,
            )
            store_u(b).start()
            store_g(b).start()
            store_l(b).start()

        return carry

    for piece in range(PIECES):
        for copy in fetch(0, piece):
            copy.start()
    lax.fori_loop(0, BLOCKS, block, 0)
    for m in range(batches):
        gouts[m][...] = g[m * ROWS : (m + 1) * ROWS, :]

    @pl.when(stage[0] == STAGES - 1)
    def finish():
        for b in range(BLOCKS):
            store_u(b).wait()
            store_g(b).wait()
            store_l(b).wait()


def relay_kernel(
    active_stage, m, width, rank, stage, gin, heads, rests, d, h, mod, inv, gs_in, us_in, ls_in, gout, gs, us, ls, g_keep, u_keep, l_keep, stored
):
    rows = pl.ds(m * ROWS, ROWS)

    def store_u(b):
        return pltpu.make_async_copy(u_keep.at[b], us.at[b, rows, :], stored.at[0, b])

    def store_g(b):
        return pltpu.make_async_copy(g_keep.at[b], gs.at[b, rows, :], stored.at[1, b])

    def store_l(b):
        return pltpu.make_async_copy(l_keep.at[b], ls.at[b, rows, :], stored.at[2, b])

    def block(step, carry):
        b = BLOCKS - 1 - step
        count = heads.shape[2]
        last = width + rank - count

        def times(value, i):
            return dot(value[:, :count], heads[b, i]) + dot(value[:, count:], rests[b, i, :last, :])

        relay_block(
            b, [m], width, rank, rows, times, lambda i: rests[b, i, last:, :], gout, d, h, mod, inv, g_keep, u_keep, l_keep
        )
        store_u(b).start()
        store_g(b).start()
        store_l(b).start()
        return carry

    @pl.when(stage[0] == active_stage)
    def run():
        gout[...] = gin[...]
        lax.fori_loop(0, BLOCKS, block, 0)
        for b in range(BLOCKS):
            store_u(b).wait()
            store_g(b).wait()
            store_l(b).wait()


def grads_kernel(rank, core, mixed, lows, us, ls, mine, theirs):
    owned = mine.shape[3]
    for b in range(BLOCKS):
        for row, left, right in ((0, ls[b], mixed[b]), (rank, lows[b], us[b])):
            part = dot(left.T, right).astype(jnp.bfloat16)
            for pair in range(MEMBERS // CORES):
                both = [part[:, (CORES * pair + c) * owned : (CORES * pair + c + 1) * owned] for c in range(CORES)]
                x, z = pair % SIZES[3], b * SIZES[2] + pair // SIZES[3]
                mine[x, z, row : row + rank, :] = jnp.where(core[0] == 0, both[0], both[1])
                theirs[x, z, row : row + rank, :] = jnp.where(core[0] == 0, both[1], both[0])


def split_kernel(place, kept, *refs):
    pieces, sems = refs[:-1], refs[-1]
    copies = [
        pltpu.make_async_copy(kept.at[lax.rem(place[0] + turn, BLOCKS)], piece, sems.at[turn])
        for turn, piece in enumerate(pieces)
    ]
    for copy in copies:
        copy.start()
    for copy in copies:
        copy.wait()


def input_grads_kernel(place, *refs):
    pieces, out = refs[:-1], refs[-1]
    for turn, piece in enumerate(pieces):
        rows = piece.shape[0]
        start = pl.multiple_of(lax.rem(place[0] - turn + BLOCKS, BLOCKS) * rows, rows)
        out[0, pl.ds(start, rows), :] = piece[...]


def total_kernel(rank, scale, parts, down, up):
    total = jnp.sum(parts[...].astype(jnp.float32), axis=0) * scale
    down[0] = total[:rank, :].T
    up[0] = total[rank:, :].T


VMEM = pl.BlockSpec(memory_space=pltpu.VMEM)
ANY = pl.BlockSpec(memory_space=pl.ANY)
HBM = pl.BlockSpec(memory_space=pltpu.HBM)
SMEM = pl.BlockSpec(memory_space=pltpu.SMEM)


def resident(value):
    return pltpu.with_memory_space_constraint(value, pltpu.VMEM)


def far(value):
    return pltpu.with_memory_space_constraint(value, pltpu.HBM)


def per_device(block_inputs, target, frozen_weight, adapter_down, adapter_up, start_modulation, finish_modulation, level_pairs):
    stage = lax.axis_index("y")
    place = lax.axis_index("zh")
    core = lax.axis_index("c")
    tokens, width = block_inputs.shape[1:]
    owned, rank = adapter_down.shape[1:]
    share = tokens // BLOCKS
    batches = share // ROWS
    grad_scale = 1.0 / math.sqrt(tokens * MEMBERS)

    rest_rows = width + 2 * rank - HEAD_ROWS
    head, rest = pl.pallas_call(
        functools.partial(slab_kernel, width, rank),
        out_shape=[
            jax.ShapeDtypeStruct((HEAD_ROWS, owned), jnp.bfloat16),
            jax.ShapeDtypeStruct((rest_rows, owned), jnp.bfloat16),
        ],
        in_specs=[VMEM] * 3,
        out_specs=[VMEM] * 2,
        name="slab",
    )(frozen_weight[0], adapter_down[0], adapter_up[0])
    heads = lax.all_gather(head, PLANE, axis=0, tiled=True).reshape(BLOCKS, MEMBERS, HEAD_ROWS, owned)
    bundles = row_bundles(ring_bundle(rest))
    bundles = bundles + [lax.ppermute(value, "c", [(0, 1), (1, 0)]) for value in bundles]
    indices = [lax.axis_index(("zh", "zl")), lax.axis_index("x"), core]
    rests = pl.pallas_call(
        place_kernel,
        out_shape=pltpu.VMEM((BLOCKS, MEMBERS, rest_rows, owned), jnp.bfloat16),
        in_specs=[SMEM] * 3 + [ANY] * len(bundles),
        out_specs=VMEM,
        scratch_shapes=[pltpu.SemaphoreType.DMA((len(bundles), len(RING)))],
        compiler_params=pltpu.CompilerParams(vmem_limit_bytes=4 * MIB),
        name="place",
    )(*[index.astype(jnp.int32).reshape(1) for index in indices], *bundles)

    own_mod = per_batch_modulation(start_modulation[0], finish_modulation[0], level_pairs)
    mod = lax.all_to_all(own_mod, "zh", 0, 0, tiled=True).reshape(BLOCKS, batches, 3 * width)
    x = lax.all_to_all(block_inputs[0], "zh", 0, 0, tiled=True).reshape(BLOCKS, share, width)
    own_target = lax.dynamic_slice_in_dim(target, place * share, share, 0)

    stage, place, core = (index.astype(jnp.int32).reshape(1) for index in (stage, place, core))
    x, mod, stage, place, core, own_target = lax.optimization_barrier((x, mod, stage, place, core, own_target))

    heads_near, rests_near, mod_near = resident(heads), resident(rests), resident(mod)
    kept_shape = (BLOCKS, share, width)
    mixed, lows, d, h, inv, gs, us, ls, *sent = pl.pallas_call(
        functools.partial(first_kernel, batches, width, rank),
        out_shape=[
            jax.ShapeDtypeStruct(kept_shape, jnp.bfloat16),
            jax.ShapeDtypeStruct((BLOCKS, share, rank), jnp.bfloat16),
            pltpu.VMEM(kept_shape, jnp.float32),
            pltpu.VMEM(kept_shape, jnp.float32),
            pltpu.VMEM((BLOCKS, share, owned), jnp.float32),
            pltpu.HBM(kept_shape, jnp.bfloat16),
            pltpu.HBM(kept_shape, jnp.bfloat16),
            pltpu.HBM((BLOCKS, share, rank), jnp.bfloat16),
        ]
        + [pltpu.VMEM((ROWS, width), jnp.bfloat16)] * batches,
        in_specs=[SMEM] + [VMEM] * 3 + [HBM] * 2,
        out_specs=[VMEM] * 5 + [HBM] * 3 + [VMEM] * batches,
        scratch_shapes=[
            pltpu.VMEM((share, width), jnp.bfloat16),
            pltpu.VMEM(kept_shape, jnp.bfloat16),
            pltpu.VMEM(kept_shape, jnp.bfloat16),
            pltpu.VMEM((BLOCKS, share, rank), jnp.bfloat16),
            pltpu.VMEM((share, width), jnp.float32),
            pltpu.VMEM((2, MEMBERS, width + 2 * rank, owned), jnp.bfloat16),
            pltpu.SemaphoreType.DMA((2, 2, PIECES)),
            pltpu.SemaphoreType.DMA((3, BLOCKS)),
        ],
        compiler_params=pltpu.CompilerParams(vmem_limit_bytes=26 * MIB),
        cost_estimate=pl.CostEstimate(flops=4 * BLOCKS * share * width * width, bytes_accessed=40 * MIB, transcendentals=0),
        name="first",
    )(stage, x, mod_near, own_target, far(heads), far(rests))

    d_near, h_near, inv_near = (resident(v) for v in (d, h, inv))

    def relay(active_stage, m, gin, gs, us, ls):
        return pl.pallas_call(
            functools.partial(relay_kernel, active_stage, m, width, rank),
            out_shape=[pltpu.VMEM((ROWS, width), jnp.bfloat16)] + [
                pltpu.HBM(kept_shape, jnp.bfloat16),
                pltpu.HBM(kept_shape, jnp.bfloat16),
                pltpu.HBM((BLOCKS, share, rank), jnp.bfloat16),
            ],
            in_specs=[SMEM] + [VMEM] * 7 + [HBM] * 3,
            out_specs=[VMEM] + [HBM] * 3,
            scratch_shapes=[
                pltpu.VMEM((BLOCKS, ROWS, width), jnp.bfloat16),
                pltpu.VMEM((BLOCKS, ROWS, width), jnp.bfloat16),
                pltpu.VMEM((BLOCKS, ROWS, rank), jnp.bfloat16),
                pltpu.SemaphoreType.DMA((3, BLOCKS)),
            ],
            input_output_aliases={8: 1, 9: 2, 10: 3},
            compiler_params=pltpu.CompilerParams(vmem_limit_bytes=4 * MIB),
            cost_estimate=pl.CostEstimate(flops=2 * BLOCKS * ROWS * width * width, bytes_accessed=4 * MIB, transcendentals=0),
            name="relay",
        )(stage, resident(gin), heads_near, rests_near, d_near, h_near, mod_near, inv_near, far(gs), far(us), far(ls))

    _, gs, us, ls = relay(STAGES, 0, sent[0], gs, us, ls)
    for step in range(1, STAGES):
        arrived = [lax.ppermute(out, "y", [(STAGES - step, STAGES - 1 - step)]) for out in sent]
        sent = []
        for m in range(batches):
            gout, gs, us, ls = relay(STAGES - 1 - step, m, arrived[m], gs, us, ls)
            sent.append(gout)

    gs, us, ls, mixed, lows = lax.optimization_barrier((gs, us, ls, mixed, lows))

    def shifted(value, turn):
        return lax.ppermute(value, "zh", [(i, (i + turn) % BLOCKS) for i in range(BLOCKS)])

    pieces = pl.pallas_call(
        split_kernel,
        out_shape=[pltpu.VMEM((share, width), jnp.bfloat16)] * BLOCKS,
        in_specs=[SMEM, HBM],
        out_specs=[VMEM] * BLOCKS,
        scratch_shapes=[pltpu.SemaphoreType.DMA((BLOCKS,))],
        compiler_params=pltpu.CompilerParams(vmem_limit_bytes=4 * MIB),
        name="split",
    )(place, far(gs))
    pieces = [pieces[0]] + [shifted(pieces[turn], turn) for turn in range(1, BLOCKS)]

    row, ring = SIZES[3], SIZES[1] * SIZES[2]
    mine, theirs = pl.pallas_call(
        functools.partial(grads_kernel, rank),
        out_shape=[jax.ShapeDtypeStruct((row, ring, 2 * rank, owned), jnp.bfloat16)] * 2,
        in_specs=[SMEM] + [VMEM] * 4,
        out_specs=[VMEM] * 2,
        compiler_params=pltpu.CompilerParams(vmem_limit_bytes=24 * MIB),
        name="grads",
    )(core, mixed, lows, us, ls)
    theirs = lax.ppermute(theirs, "c", [(0, 1), (1, 0)])
    parts = (mine.astype(jnp.float32) + theirs.astype(jnp.float32)).astype(jnp.bfloat16)
    parts = lax.all_to_all(parts, "x", 0, 0, tiled=True)
    parts = jnp.sum(parts.astype(jnp.float32), axis=0).astype(jnp.bfloat16)
    parts = lax.all_to_all(parts, ("zh", "zl"), 0, 0, tiled=True)
    pieces, parts = lax.optimization_barrier((pieces, parts))
    down_grad, up_grad = pl.pallas_call(
        functools.partial(total_kernel, rank, grad_scale),
        out_shape=[jax.ShapeDtypeStruct((1, owned, rank), jnp.float32)] * 2,
        in_specs=[VMEM],
        out_specs=[VMEM] * 2,
        name="total",
    )(parts)
    input_grads = pl.pallas_call(
        input_grads_kernel,
        out_shape=jax.ShapeDtypeStruct((1, tokens, width), jnp.bfloat16),
        in_specs=[SMEM] + [VMEM] * BLOCKS,
        out_specs=VMEM,
        compiler_params=pltpu.CompilerParams(vmem_limit_bytes=8 * MIB),
        name="input_grads",
    )(place, *pieces)
    return input_grads, down_grad, up_grad


def solution(mesh):
    split = Mesh(mesh.devices.reshape(SIZES), AXES)
    blocks = ("y", "zh")
    return jax.shard_map(
        per_device,
        mesh=split,
        in_specs=(
            P(blocks, GROUP, None),
            P(GROUP, None),
            P(blocks, GROUP, None),
            P(blocks, GROUP, None),
            P(blocks, GROUP, None),
            P(blocks, None, None),
            P(blocks, None, None),
            P(GROUP, None),
        ),
        out_specs=(P(blocks, GROUP, None), P(blocks, GROUP, None), P(blocks, GROUP, None)),
        check_vma=False,
    )
```

```python
import functools
import math

import jax
import jax.numpy as jnp
from jax import lax
from jax.experimental import pallas as pl
from jax.experimental.pallas import tpu as pltpu
from jax.sharding import Mesh, PartitionSpec as P

EPSILON = 1e-06
AXES = ("y", "zh", "zl", "x", "c")
SIZES = (8, 4, 2, 4, 2)
STAGES, BLOCKS, CORES = SIZES[0], SIZES[1], SIZES[4]
GROUP = ("zl", "x", "c")
CHIPS = ("zl", "x")
PLANE = ("zh", "zl", "x", "c")
MEMBERS = 16
ROWS = 32
CHUNK = 512
PIECES = 4
HEAD_ROWS = 1664
ROW_DOT = (((1,), (0,)), ((), ()))
LAST_DIMS = (((1,), (1,)), ((), ()))
FIRST_DIMS = (((0,), (0,)), ((), ()))
SLOPE = math.sqrt(2.0 / math.pi)
CUBIC = 0.044715
MIB = 2**20


def dot(left, right, dims=ROW_DOT):
    return lax.dot_general(left, right, dims, preferred_element_type=jnp.float32)


def per_batch_modulation(from_table, to_table, level_pairs):
    ladder = jnp.arange(from_table.shape[0], dtype=jnp.int32)[None, :]
    hot_from = (level_pairs[:, 0:1] == ladder).astype(jnp.bfloat16)
    hot_to = (level_pairs[:, 1:2] == ladder).astype(jnp.bfloat16)
    return dot(hot_from, from_table) + dot(hot_to, to_table)


def slab_kernel(width, rank, weight, down, up, head, rest):
    count = head.shape[0]
    turned = weight[...].T
    head[...] = turned[:count, :]
    rest[: width - count, :] = turned[count:, :]
    rest[width - count : width - count + rank, :] = down[...].T
    rest[width - count + rank :, :] = up[...]


RING = (0, -1, -2, -3, -4, 1, 2, 3)


def ring_bundle(piece):
    ring = SIZES[1] * SIZES[2]

    def step(value, turn):
        return lax.ppermute(value, ("zh", "zl"), [(i, (i + turn) % ring) for i in range(ring)])

    up_1, down_1 = step(piece, 1), step(piece, -1)
    up_2, down_2 = step(up_1, 1), step(down_1, -1)
    up_3, down_3 = step(up_2, 1), step(down_2, -1)
    return jnp.stack([piece, up_1, up_2, up_3, step(up_3, 1), down_1, down_2, down_3])


def row_bundles(bundle):
    row, middle = SIZES[3], bundle.shape[0] // 2

    def step(value, turn):
        return lax.ppermute(value, "x", [(i, (i + turn) % row) for i in range(row)])

    before, after = step(bundle, 1), step(bundle, -1)
    return [bundle, before, after, step(before[:middle], 1), step(after[middle:], -1)]


def place_kernel(ring_place, row_place, core, *refs):
    bundles, (out, sems) = refs[:-2], refs[-2:]
    ring, row = SIZES[1] * SIZES[2], SIZES[3]
    middle = len(RING) // 2
    copies = []
    for n, bundle in enumerate(bundles):
        kind, other = n % 5, n // 5
        turns = RING[:middle] if kind == 3 else RING[middle:] if kind == 4 else RING
        x = lax.rem(row_place[0] + (0, row - 1, 1, 2, 2)[kind], row)
        c = lax.rem(core[0] + other, CORES)
        for m, turn in enumerate(turns):
            z = lax.rem(ring_place[0] + turn + ring, ring)
            member = (lax.rem(z, SIZES[2]) * row + x) * CORES + c
            copies.append(pltpu.make_async_copy(bundle.at[m], out.at[z // SIZES[2], member], sems.at[n, m]))
    for copy in copies:
        copy.start()
    for copy in copies:
        copy.wait()


def relay_block(b, batches, width, rank, rows, times, up_of, g, d, h, mod, inv, g_keep, u_keep, l_keep):
    owned = width // MEMBERS
    u = (d[b, rows, :] * g[...].astype(jnp.float32)).astype(jnp.bfloat16)
    u_keep[b] = u
    up = jnp.concatenate([up_of(i) for i in range(MEMBERS)], axis=0)
    low = dot(u, up).astype(jnp.bfloat16)
    l_keep[b] = low
    joined = jnp.concatenate([u, low], axis=1)
    scaled, total = [], None
    for i in range(MEMBERS):
        c = pl.ds(i * owned, owned)
        grad = times(joined, i)
        scale = [1.0 + mod[b, pl.ds(m, 1), pl.ds(width + i * owned, owned)] for m in batches]
        pieces = [grad[n * ROWS : (n + 1) * ROWS] * scale[n] for n in range(len(batches))]
        grad = pieces[0] if len(pieces) == 1 else jnp.concatenate(pieces, axis=0)
        scaled.append(grad)
        part = grad * h[b, rows, c]
        total = part if total is None else total + part
    centred = jnp.sum(total, axis=1, keepdims=True) * (1.0 / width)
    rms = inv[b, rows, :]
    for i in range(MEMBERS):
        c = pl.ds(i * owned, owned)
        value = g[:, c].astype(jnp.float32) + rms * (scaled[i] - h[b, rows, c] * centred)
        value = value.astype(jnp.bfloat16)
        g[:, c] = value
        g_keep[b, :, c] = value


def first_kernel(
    batches, width, rank, stage, x, mod, target, heads, rests, mixed, lows, d, h, inv, gs, us, ls, *rest
):
    gouts, (g, g_keep, u_keep, l_keep, preact, near, fetched, stored) = rest[:batches], rest[batches:]
    share = batches * ROWS
    per_chunk = CHUNK // heads.shape[3]
    count = heads.shape[2]
    quarter = MEMBERS // PIECES

    def fetch(step, piece):
        members = pl.ds(piece * quarter, quarter)
        slot = lax.rem(step, 2)
        b = BLOCKS - 1 - step
        return (
            pltpu.make_async_copy(heads.at[b, members], near.at[slot, members, :count, :], fetched.at[slot, 0, piece]),
            pltpu.make_async_copy(rests.at[b, members], near.at[slot, members, count:, :], fetched.at[slot, 1, piece]),
        )

    def store_u(b):
        return pltpu.make_async_copy(u_keep.at[b], us.at[b], stored.at[0, b])

    def store_g(b):
        return pltpu.make_async_copy(g_keep.at[b], gs.at[b], stored.at[1, b])

    def store_l(b):
        return pltpu.make_async_copy(l_keep.at[b], ls.at[b], stored.at[2, b])

    def block(step, carry):
        b = BLOCKS - 1 - step
        slot = lax.rem(step, 2)
        for piece in range(PIECES):
            for copy in fetch(step, piece):
                copy.wait()

        @pl.when(step < BLOCKS - 1)
        def ahead():
            for piece in range(PIECES):
                for copy in fetch(step + 1, piece):
                    copy.start()

        def slab(i):
            return near.at[slot, i]

        pieces = []
        for m in range(batches):
            r = pl.ds(m * ROWS, ROWS)
            values = x[b, r, :].astype(jnp.float32)
            rms = lax.rsqrt(jnp.mean(values * values, axis=1, keepdims=True) + EPSILON)
            normed = values * rms
            h[b, r, :] = normed
            inv[b, r, :] = jnp.broadcast_to(rms, (ROWS, inv.shape[2]))
            shift = mod[b, pl.ds(m, 1), 0:width]
            scale = mod[b, pl.ds(m, 1), width : 2 * width]
            pieces.append((normed * (1.0 + scale) + shift).astype(jnp.bfloat16))
        modulated = jnp.concatenate(pieces, axis=0)
        down = jnp.concatenate([slab(i)[width : width + rank, :] for i in range(MEMBERS)], axis=1)
        low = dot(modulated, down, LAST_DIMS).astype(jnp.bfloat16)
        mixed[b] = modulated
        lows[b] = low
        for j in range(width // CHUNK):
            c = pl.ds(j * CHUNK, CHUNK)
            up = jnp.concatenate([slab(j * per_chunk + i)[width + rank :, :] for i in range(per_chunk)], axis=0)
            weight = jnp.concatenate([slab(i)[c, :] for i in range(MEMBERS)], axis=1)
            preact[:, c] = dot(weight, modulated, LAST_DIMS).T + dot(low, up, LAST_DIMS)
        for j in range(width // CHUNK):
            c = pl.ds(j * CHUNK, CHUNK)
            for m in range(batches):
                r = pl.ds(m * ROWS, ROWS)
                pre = preact[r, c]
                squared = pre * pre
                bent = jnp.tanh(SLOPE * pre * (1.0 + CUBIC * squared))
                half = 0.5 * (1.0 + bent)
                slope = half + 0.5 * pre * (1.0 - bent * bent) * (SLOPE * (1.0 + 3.0 * CUBIC * squared))
                gate = mod[b, pl.ds(m, 1), pl.ds(2 * width + j * CHUNK, CHUNK)]
                d[b, r, c] = slope * gate
                preact[r, c] = gate * (pre * half)

        @pl.when(step == 0)
        def close():
            out = x[b].astype(jnp.float32) + preact[...]
            g[...] = (out - target[...].astype(jnp.float32)).astype(jnp.bfloat16)

        @pl.when(stage[0] == STAGES - 1)
        def relay():
            relay_block(
                b,
                range(batches),
                width,
                rank,
                pl.ds(0, share),
                lambda value, i: dot(value, slab(i)[: width + rank, :]),
                lambda i: slab(i)[width + rank :, :],
                g,
                d,
                h,
                mod,
                inv,
                g_keep,
                u_keep,
                l_keep,
            )
            store_u(b).start()
            store_g(b).start()
            store_l(b).start()

        return carry

    for piece in range(PIECES):
        for copy in fetch(0, piece):
            copy.start()
    lax.fori_loop(0, BLOCKS, block, 0)
    for m in range(batches):
        gouts[m][...] = g[m * ROWS : (m + 1) * ROWS, :]

    @pl.when(stage[0] == STAGES - 1)
    def finish():
        for b in range(BLOCKS):
            store_u(b).wait()
            store_g(b).wait()
            store_l(b).wait()


def relay_kernel(
    active_stage, m, width, rank, stage, gin, heads, rests, d, h, mod, inv, gs_in, us_in, ls_in, gout, gs, us, ls, g_keep, u_keep, l_keep, stored
):
    rows = pl.ds(m * ROWS, ROWS)

    def store_u(b):
        return pltpu.make_async_copy(u_keep.at[b], us.at[b, rows, :], stored.at[0, b])

    def store_g(b):
        return pltpu.make_async_copy(g_keep.at[b], gs.at[b, rows, :], stored.at[1, b])

    def store_l(b):
        return pltpu.make_async_copy(l_keep.at[b], ls.at[b, rows, :], stored.at[2, b])

    def block(step, carry):
        b = BLOCKS - 1 - step
        count = heads.shape[2]
        last = width + rank - count

        def times(value, i):
            return dot(value[:, :count], heads[b, i]) + dot(value[:, count:], rests[b, i, :last, :])

        relay_block(
            b, [m], width, rank, rows, times, lambda i: rests[b, i, last:, :], gout, d, h, mod, inv, g_keep, u_keep, l_keep
        )
        store_u(b).start()
        store_g(b).start()
        store_l(b).start()
        return carry

    @pl.when(stage[0] == active_stage)
    def run():
        gout[...] = gin[...]
        lax.fori_loop(0, BLOCKS, block, 0)
        for b in range(BLOCKS):
            store_u(b).wait()
            store_g(b).wait()
            store_l(b).wait()


def grads_kernel(rank, core, mixed, lows, us, ls, mine, theirs):
    owned = mine.shape[3]
    for b in range(BLOCKS):
        for row, left, right in ((0, ls[b], mixed[b]), (rank, lows[b], us[b])):
            part = dot(left.T, right).astype(jnp.bfloat16)
            for pair in range(MEMBERS // CORES):
                both = [part[:, (CORES * pair + c) * owned : (CORES * pair + c + 1) * owned] for c in range(CORES)]
                x, z = pair % SIZES[3], b * SIZES[2] + pair // SIZES[3]
                mine[x, z, row : row + rank, :] = jnp.where(core[0] == 0, both[0], both[1])
                theirs[x, z, row : row + rank, :] = jnp.where(core[0] == 0, both[1], both[0])


def split_kernel(place, kept, *refs):
    pieces, sems = refs[:-1], refs[-1]
    copies = [
        pltpu.make_async_copy(kept.at[lax.rem(place[0] + turn, BLOCKS)], piece, sems.at[turn])
        for turn, piece in enumerate(pieces)
    ]
    for copy in copies:
        copy.start()
    for copy in copies:
        copy.wait()


def input_grads_kernel(place, *refs):
    pieces, out = refs[:-1], refs[-1]
    for turn, piece in enumerate(pieces):
        rows = piece.shape[0]
        start = pl.multiple_of(lax.rem(place[0] - turn + BLOCKS, BLOCKS) * rows, rows)
        out[0, pl.ds(start, rows), :] = piece[...]


def total_kernel(rank, scale, parts, down, up):
    total = jnp.sum(parts[...].astype(jnp.float32), axis=0) * scale
    down[0] = total[:rank, :].T
    up[0] = total[rank:, :].T


VMEM = pl.BlockSpec(memory_space=pltpu.VMEM)
ANY = pl.BlockSpec(memory_space=pl.ANY)
HBM = pl.BlockSpec(memory_space=pltpu.HBM)
SMEM = pl.BlockSpec(memory_space=pltpu.SMEM)


def resident(value):
    return pltpu.with_memory_space_constraint(value, pltpu.VMEM)


def far(value):
    return pltpu.with_memory_space_constraint(value, pltpu.HBM)


def per_device(block_inputs, target, frozen_weight, adapter_down, adapter_up, start_modulation, finish_modulation, level_pairs):
    stage = lax.axis_index("y")
    place = lax.axis_index("zh")
    core = lax.axis_index("c")
    tokens, width = block_inputs.shape[1:]
    owned, rank = adapter_down.shape[1:]
    share = tokens // BLOCKS
    batches = share // ROWS
    grad_scale = 1.0 / math.sqrt(tokens * MEMBERS)

    rest_rows = width + 2 * rank - HEAD_ROWS
    head, rest = pl.pallas_call(
        functools.partial(slab_kernel, width, rank),
        out_shape=[
            jax.ShapeDtypeStruct((HEAD_ROWS, owned), jnp.bfloat16),
            jax.ShapeDtypeStruct((rest_rows, owned), jnp.bfloat16),
        ],
        in_specs=[VMEM] * 3,
        out_specs=[VMEM] * 2,
        name="slab",
    )(frozen_weight[0], adapter_down[0], adapter_up[0])
    heads = lax.all_gather(head, PLANE, axis=0, tiled=True).reshape(BLOCKS, MEMBERS, HEAD_ROWS, owned)
    bundles = row_bundles(ring_bundle(rest))
    bundles = bundles + [lax.ppermute(value, "c", [(0, 1), (1, 0)]) for value in bundles]
    indices = [lax.axis_index(("zh", "zl")), lax.axis_index("x"), core]
    rests = pl.pallas_call(
        place_kernel,
        out_shape=pltpu.VMEM((BLOCKS, MEMBERS, rest_rows, owned), jnp.bfloat16),
        in_specs=[SMEM] * 3 + [ANY] * len(bundles),
        out_specs=VMEM,
        scratch_shapes=[pltpu.SemaphoreType.DMA((len(bundles), len(RING)))],
        compiler_params=pltpu.CompilerParams(vmem_limit_bytes=4 * MIB),
        name="place",
    )(*[index.astype(jnp.int32).reshape(1) for index in indices], *bundles)

    own_mod = per_batch_modulation(start_modulation[0], finish_modulation[0], level_pairs)
    mod = lax.all_to_all(own_mod, "zh", 0, 0, tiled=True).reshape(BLOCKS, batches, 3 * width)
    x = lax.all_to_all(block_inputs[0], "zh", 0, 0, tiled=True).reshape(BLOCKS, share, width)
    own_target = lax.dynamic_slice_in_dim(target, place * share, share, 0)

    stage, place, core = (index.astype(jnp.int32).reshape(1) for index in (stage, place, core))
    x, mod, stage, place, core, own_target = lax.optimization_barrier((x, mod, stage, place, core, own_target))

    heads_near, rests_near, mod_near = resident(heads), resident(rests), resident(mod)
    kept_shape = (BLOCKS, share, width)
    mixed, lows, d, h, inv, gs, us, ls, *sent = pl.pallas_call(
        functools.partial(first_kernel, batches, width, rank),
        out_shape=[
            jax.ShapeDtypeStruct(kept_shape, jnp.bfloat16),
            jax.ShapeDtypeStruct((BLOCKS, share, rank), jnp.bfloat16),
            pltpu.VMEM(kept_shape, jnp.float32),
            pltpu.VMEM(kept_shape, jnp.float32),
            pltpu.VMEM((BLOCKS, share, owned), jnp.float32),
            pltpu.HBM(kept_shape, jnp.bfloat16),
            pltpu.HBM(kept_shape, jnp.bfloat16),
            pltpu.HBM((BLOCKS, share, rank), jnp.bfloat16),
        ]
        + [pltpu.VMEM((ROWS, width), jnp.bfloat16)] * batches,
        in_specs=[SMEM] + [VMEM] * 3 + [HBM] * 2,
        out_specs=[VMEM] * 5 + [HBM] * 3 + [VMEM] * batches,
        scratch_shapes=[
            pltpu.VMEM((share, width), jnp.bfloat16),
            pltpu.VMEM(kept_shape, jnp.bfloat16),
            pltpu.VMEM(kept_shape, jnp.bfloat16),
            pltpu.VMEM((BLOCKS, share, rank), jnp.bfloat16),
            pltpu.VMEM((share, width), jnp.float32),
            pltpu.VMEM((2, MEMBERS, width + 2 * rank, owned), jnp.bfloat16),
            pltpu.SemaphoreType.DMA((2, 2, PIECES)),
            pltpu.SemaphoreType.DMA((3, BLOCKS)),
        ],
        compiler_params=pltpu.CompilerParams(vmem_limit_bytes=26 * MIB),
        cost_estimate=pl.CostEstimate(flops=4 * BLOCKS * share * width * width, bytes_accessed=40 * MIB, transcendentals=0),
        name="first",
    )(stage, x, mod_near, own_target, far(heads), far(rests))

    d_near, h_near, inv_near = (resident(v) for v in (d, h, inv))

    def relay(active_stage, m, gin, gs, us, ls):
        return pl.pallas_call(
            functools.partial(relay_kernel, active_stage, m, width, rank),
            out_shape=[pltpu.VMEM((ROWS, width), jnp.bfloat16)] + [
                pltpu.HBM(kept_shape, jnp.bfloat16),
                pltpu.HBM(kept_shape, jnp.bfloat16),
                pltpu.HBM((BLOCKS, share, rank), jnp.bfloat16),
            ],
            in_specs=[SMEM] + [VMEM] * 7 + [HBM] * 3,
            out_specs=[VMEM] + [HBM] * 3,
            scratch_shapes=[
                pltpu.VMEM((BLOCKS, ROWS, width), jnp.bfloat16),
                pltpu.VMEM((BLOCKS, ROWS, width), jnp.bfloat16),
                pltpu.VMEM((BLOCKS, ROWS, rank), jnp.bfloat16),
                pltpu.SemaphoreType.DMA((3, BLOCKS)),
            ],
            input_output_aliases={8: 1, 9: 2, 10: 3},
            compiler_params=pltpu.CompilerParams(vmem_limit_bytes=4 * MIB),
            cost_estimate=pl.CostEstimate(flops=2 * BLOCKS * ROWS * width * width, bytes_accessed=4 * MIB, transcendentals=0),
            name="relay",
        )(stage, resident(gin), heads_near, rests_near, d_near, h_near, mod_near, inv_near, far(gs), far(us), far(ls))

    _, gs, us, ls = relay(STAGES, 0, sent[0], gs, us, ls)
    for step in range(1, STAGES):
        arrived = [lax.ppermute(out, "y", [(STAGES - step, STAGES - 1 - step)]) for out in sent]
        sent = []
        for m in range(batches):
            gout, gs, us, ls = relay(STAGES - 1 - step, m, arrived[m], gs, us, ls)
            sent.append(gout)

    gs, us, ls, mixed, lows = lax.optimization_barrier((gs, us, ls, mixed, lows))

    def shifted(value, turn):
        return lax.ppermute(value, "zh", [(i, (i + turn) % BLOCKS) for i in range(BLOCKS)])

    pieces = pl.pallas_call(
        split_kernel,
        out_shape=[pltpu.VMEM((share, width), jnp.bfloat16)] * BLOCKS,
        in_specs=[SMEM, HBM],
        out_specs=[VMEM] * BLOCKS,
        scratch_shapes=[pltpu.SemaphoreType.DMA((BLOCKS,))],
        compiler_params=pltpu.CompilerParams(vmem_limit_bytes=4 * MIB),
        name="split",
    )(place, far(gs))
    pieces = [pieces[0]] + [shifted(pieces[turn], turn) for turn in range(1, BLOCKS)]

    row, ring = SIZES[3], SIZES[1] * SIZES[2]
    mine, theirs = pl.pallas_call(
        functools.partial(grads_kernel, rank),
        out_shape=[jax.ShapeDtypeStruct((row, ring, 2 * rank, owned), jnp.bfloat16)] * 2,
        in_specs=[SMEM] + [VMEM] * 4,
        out_specs=[VMEM] * 2,
        compiler_params=pltpu.CompilerParams(vmem_limit_bytes=24 * MIB),
        name="grads",
    )(core, mixed, lows, us, ls)
    theirs = lax.ppermute(theirs, "c", [(0, 1), (1, 0)])
    parts = (mine.astype(jnp.float32) + theirs.astype(jnp.float32)).astype(jnp.bfloat16)
    parts = lax.all_to_all(parts, "x", 0, 0, tiled=True)
    near, parts = lax.optimization_barrier(([pieces[1], pieces[3]], parts))
    parts = jnp.sum(parts.astype(jnp.float32), axis=0).astype(jnp.bfloat16)
    parts = lax.all_to_all(parts, ("zh", "zl"), 0, 0, tiled=True)
    far_piece, parts = lax.optimization_barrier((pieces[2], parts))
    pieces = [pieces[0], near[0], far_piece, near[1]]
    down_grad, up_grad = pl.pallas_call(
        functools.partial(total_kernel, rank, grad_scale),
        out_shape=[jax.ShapeDtypeStruct((1, owned, rank), jnp.float32)] * 2,
        in_specs=[VMEM],
        out_specs=[VMEM] * 2,
        name="total",
    )(parts)
    input_grads = pl.pallas_call(
        input_grads_kernel,
        out_shape=jax.ShapeDtypeStruct((1, tokens, width), jnp.bfloat16),
        in_specs=[SMEM] + [VMEM] * BLOCKS,
        out_specs=VMEM,
        compiler_params=pltpu.CompilerParams(vmem_limit_bytes=8 * MIB),
        name="input_grads",
    )(place, *pieces)
    return input_grads, down_grad, up_grad


def solution(mesh):
    split = Mesh(mesh.devices.reshape(SIZES), AXES)
    blocks = ("y", "zh")
    return jax.shard_map(
        per_device,
        mesh=split,
        in_specs=(
            P(blocks, GROUP, None),
            P(GROUP, None),
            P(blocks, GROUP, None),
            P(blocks, GROUP, None),
            P(blocks, GROUP, None),
            P(blocks, None, None),
            P(blocks, None, None),
            P(GROUP, None),
        ),
        out_specs=(P(blocks, GROUP, None), P(blocks, GROUP, None), P(blocks, GROUP, None)),
        check_vma=False,
    )
```

```python
import functools
import math

import jax
import jax.numpy as jnp
from jax import lax
from jax.experimental import pallas as pl
from jax.experimental.pallas import tpu as pltpu
from jax.sharding import Mesh, PartitionSpec as P

EPSILON = 1e-06
AXES = ("y", "zh", "zl", "x", "c")
SIZES = (8, 4, 2, 4, 2)
STAGES, BLOCKS, CORES = SIZES[0], SIZES[1], SIZES[4]
GROUP = ("zl", "x", "c")
CHIPS = ("zl", "x")
PLANE = ("zh", "zl", "x", "c")
MEMBERS = 16
ROWS = 32
CHUNK = 1024
PIECES = 4
HEAD_ROWS = 1664
ROW_DOT = (((1,), (0,)), ((), ()))
LAST_DIMS = (((1,), (1,)), ((), ()))
FIRST_DIMS = (((0,), (0,)), ((), ()))
SLOPE = math.sqrt(2.0 / math.pi)
CUBIC = 0.044715
MIB = 2**20


def dot(left, right, dims=ROW_DOT):
    return lax.dot_general(left, right, dims, preferred_element_type=jnp.float32)


def per_batch_modulation(from_table, to_table, level_pairs):
    ladder = jnp.arange(from_table.shape[0], dtype=jnp.int32)[None, :]
    hot_from = (level_pairs[:, 0:1] == ladder).astype(jnp.bfloat16)
    hot_to = (level_pairs[:, 1:2] == ladder).astype(jnp.bfloat16)
    return dot(hot_from, from_table) + dot(hot_to, to_table)


def slab_kernel(width, rank, weight, down, up, head, rest):
    count = head.shape[0]
    turned = weight[...].T
    head[...] = turned[:count, :]
    rest[: width - count, :] = turned[count:, :]
    rest[width - count : width - count + rank, :] = down[...].T
    rest[width - count + rank :, :] = up[...]


RING = (0, -1, -2, -3, -4, 1, 2, 3)


def ring_bundle(piece):
    ring = SIZES[1] * SIZES[2]

    def step(value, turn):
        return lax.ppermute(value, ("zh", "zl"), [(i, (i + turn) % ring) for i in range(ring)])

    up_1, down_1 = step(piece, 1), step(piece, -1)
    up_2, down_2 = step(up_1, 1), step(down_1, -1)
    up_3, down_3 = step(up_2, 1), step(down_2, -1)
    return jnp.stack([piece, up_1, up_2, up_3, step(up_3, 1), down_1, down_2, down_3])


def row_bundles(bundle):
    row, middle = SIZES[3], bundle.shape[0] // 2

    def step(value, turn):
        return lax.ppermute(value, "x", [(i, (i + turn) % row) for i in range(row)])

    before, after = step(bundle, 1), step(bundle, -1)
    return [bundle, before, after, step(before[:middle], 1), step(after[middle:], -1)]


def place_kernel(ring_place, row_place, core, *refs):
    bundles, (out, sems) = refs[:-2], refs[-2:]
    ring, row = SIZES[1] * SIZES[2], SIZES[3]
    middle = len(RING) // 2
    copies = []
    for n, bundle in enumerate(bundles):
        kind, other = n % 5, n // 5
        turns = RING[:middle] if kind == 3 else RING[middle:] if kind == 4 else RING
        x = lax.rem(row_place[0] + (0, row - 1, 1, 2, 2)[kind], row)
        c = lax.rem(core[0] + other, CORES)
        for m, turn in enumerate(turns):
            z = lax.rem(ring_place[0] + turn + ring, ring)
            member = (lax.rem(z, SIZES[2]) * row + x) * CORES + c
            copies.append(pltpu.make_async_copy(bundle.at[m], out.at[z // SIZES[2], member], sems.at[n, m]))
    for copy in copies:
        copy.start()
    for copy in copies:
        copy.wait()


def relay_block(b, batches, width, rank, rows, times, up_of, g, d, h, mod, inv, g_keep, u_keep, l_keep):
    owned = width // MEMBERS
    u = (d[b, rows, :] * g[...].astype(jnp.float32)).astype(jnp.bfloat16)
    u_keep[b] = u
    up = jnp.concatenate([up_of(i) for i in range(MEMBERS)], axis=0)
    low = dot(u, up).astype(jnp.bfloat16)
    l_keep[b] = low
    joined = jnp.concatenate([u, low], axis=1)
    scaled, total = [], None
    for i in range(MEMBERS):
        c = pl.ds(i * owned, owned)
        grad = times(joined, i)
        scale = [1.0 + mod[b, pl.ds(m, 1), pl.ds(width + i * owned, owned)] for m in batches]
        pieces = [grad[n * ROWS : (n + 1) * ROWS] * scale[n] for n in range(len(batches))]
        grad = pieces[0] if len(pieces) == 1 else jnp.concatenate(pieces, axis=0)
        scaled.append(grad)
        part = grad * h[b, rows, c]
        total = part if total is None else total + part
    centred = jnp.sum(total, axis=1, keepdims=True) * (1.0 / width)
    rms = inv[b, rows, :]
    for i in range(MEMBERS):
        c = pl.ds(i * owned, owned)
        value = g[:, c].astype(jnp.float32) + rms * (scaled[i] - h[b, rows, c] * centred)
        value = value.astype(jnp.bfloat16)
        g[:, c] = value
        g_keep[b, :, c] = value


def first_kernel(
    batches, width, rank, stage, x, mod, target, heads, rests, mixed, lows, d, h, inv, gs, us, ls, *rest
):
    gouts, (g, g_keep, u_keep, l_keep, preact, near, fetched, stored) = rest[:batches], rest[batches:]
    share = batches * ROWS
    per_chunk = CHUNK // heads.shape[3]
    count = heads.shape[2]
    quarter = MEMBERS // PIECES

    def fetch(step, piece):
        members = pl.ds(piece * quarter, quarter)
        slot = lax.rem(step, 2)
        b = BLOCKS - 1 - step
        return (
            pltpu.make_async_copy(heads.at[b, members], near.at[slot, members, :count, :], fetched.at[slot, 0, piece]),
            pltpu.make_async_copy(rests.at[b, members], near.at[slot, members, count:, :], fetched.at[slot, 1, piece]),
        )

    def store_u(b):
        return pltpu.make_async_copy(u_keep.at[b], us.at[b], stored.at[0, b])

    def store_g(b):
        return pltpu.make_async_copy(g_keep.at[b], gs.at[b], stored.at[1, b])

    def store_l(b):
        return pltpu.make_async_copy(l_keep.at[b], ls.at[b], stored.at[2, b])

    def block(step, carry):
        b = BLOCKS - 1 - step
        slot = lax.rem(step, 2)
        for piece in range(PIECES):
            for copy in fetch(step, piece):
                copy.wait()

        @pl.when(step < BLOCKS - 1)
        def ahead():
            for piece in range(PIECES):
                for copy in fetch(step + 1, piece):
                    copy.start()

        def slab(i):
            return near.at[slot, i]

        pieces = []
        for m in range(batches):
            r = pl.ds(m * ROWS, ROWS)
            values = x[b, r, :].astype(jnp.float32)
            rms = lax.rsqrt(jnp.mean(values * values, axis=1, keepdims=True) + EPSILON)
            normed = values * rms
            h[b, r, :] = normed
            inv[b, r, :] = jnp.broadcast_to(rms, (ROWS, inv.shape[2]))
            shift = mod[b, pl.ds(m, 1), 0:width]
            scale = mod[b, pl.ds(m, 1), width : 2 * width]
            pieces.append((normed * (1.0 + scale) + shift).astype(jnp.bfloat16))
        modulated = jnp.concatenate(pieces, axis=0)
        down = jnp.concatenate([slab(i)[width : width + rank, :] for i in range(MEMBERS)], axis=1)
        low = dot(modulated, down, LAST_DIMS).astype(jnp.bfloat16)
        mixed[b] = modulated
        lows[b] = low
        for j in range(width // CHUNK):
            c = pl.ds(j * CHUNK, CHUNK)
            up = jnp.concatenate([slab(j * per_chunk + i)[width + rank :, :] for i in range(per_chunk)], axis=0)
            weight = jnp.concatenate([slab(i)[c, :] for i in range(MEMBERS)], axis=1)
            preact[:, c] = dot(weight, modulated, LAST_DIMS).T + dot(low, up, LAST_DIMS)
        for j in range(width // CHUNK):
            c = pl.ds(j * CHUNK, CHUNK)
            for m in range(batches):
                r = pl.ds(m * ROWS, ROWS)
                pre = preact[r, c]
                squared = pre * pre
                bent = jnp.tanh(SLOPE * pre * (1.0 + CUBIC * squared))
                half = 0.5 * (1.0 + bent)
                slope = half + 0.5 * pre * (1.0 - bent * bent) * (SLOPE * (1.0 + 3.0 * CUBIC * squared))
                gate = mod[b, pl.ds(m, 1), pl.ds(2 * width + j * CHUNK, CHUNK)]
                d[b, r, c] = slope * gate
                preact[r, c] = gate * (pre * half)

        @pl.when(step == 0)
        def close():
            out = x[b].astype(jnp.float32) + preact[...]
            g[...] = (out - target[...].astype(jnp.float32)).astype(jnp.bfloat16)

        @pl.when(stage[0] == STAGES - 1)
        def relay():
            relay_block(
                b,
                range(batches),
                width,
                rank,
                pl.ds(0, share),
                lambda value, i: dot(value, slab(i)[: width + rank, :]),
                lambda i: slab(i)[width + rank :, :],
                g,
                d,
                h,
                mod,
                inv,
                g_keep,
                u_keep,
                l_keep,
            )
            store_u(b).start()
            store_g(b).start()
            store_l(b).start()

        return carry

    for piece in range(PIECES):
        for copy in fetch(0, piece):
            copy.start()
    lax.fori_loop(0, BLOCKS, block, 0)
    for m in range(batches):
        gouts[m][...] = g[m * ROWS : (m + 1) * ROWS, :]

    @pl.when(stage[0] == STAGES - 1)
    def finish():
        for b in range(BLOCKS):
            store_u(b).wait()
            store_g(b).wait()
            store_l(b).wait()


def relay_kernel(
    active_stage, m, width, rank, stage, gin, heads, rests, d, h, mod, inv, gs_in, us_in, ls_in, gout, gs, us, ls, g_keep, u_keep, l_keep, stored
):
    rows = pl.ds(m * ROWS, ROWS)

    def store_u(b):
        return pltpu.make_async_copy(u_keep.at[b], us.at[b, rows, :], stored.at[0, b])

    def store_g(b):
        return pltpu.make_async_copy(g_keep.at[b], gs.at[b, rows, :], stored.at[1, b])

    def store_l(b):
        return pltpu.make_async_copy(l_keep.at[b], ls.at[b, rows, :], stored.at[2, b])

    def block(step, carry):
        b = BLOCKS - 1 - step
        count = heads.shape[2]
        last = width + rank - count

        def times(value, i):
            return dot(value[:, :count], heads[b, i]) + dot(value[:, count:], rests[b, i, :last, :])

        relay_block(
            b, [m], width, rank, rows, times, lambda i: rests[b, i, last:, :], gout, d, h, mod, inv, g_keep, u_keep, l_keep
        )
        store_u(b).start()
        store_g(b).start()
        store_l(b).start()
        return carry

    @pl.when(stage[0] == active_stage)
    def run():
        gout[...] = gin[...]
        lax.fori_loop(0, BLOCKS, block, 0)
        for b in range(BLOCKS):
            store_u(b).wait()
            store_g(b).wait()
            store_l(b).wait()


def grads_kernel(rank, core, mixed, lows, us, ls, mine, theirs):
    owned = mine.shape[3]
    for b in range(BLOCKS):
        for row, left, right in ((0, ls[b], mixed[b]), (rank, lows[b], us[b])):
            part = dot(left.T, right).astype(jnp.bfloat16)
            for pair in range(MEMBERS // CORES):
                both = [part[:, (CORES * pair + c) * owned : (CORES * pair + c + 1) * owned] for c in range(CORES)]
                x, z = pair % SIZES[3], b * SIZES[2] + pair // SIZES[3]
                mine[x, z, row : row + rank, :] = jnp.where(core[0] == 0, both[0], both[1])
                theirs[x, z, row : row + rank, :] = jnp.where(core[0] == 0, both[1], both[0])


def split_kernel(place, kept, own, ahead, behind, sems):
    rows = kept.shape[1]
    half = rows // 2

    def piece(n, turn, first, count, target, start):
        source = kept.at[lax.rem(place[0] + turn, BLOCKS), pl.ds(first, count), :]
        return pltpu.make_async_copy(source, target.at[pl.ds(start, count), :], sems.at[n])

    copies = [
        piece(0, 0, 0, rows, own, 0),
        piece(1, 1, 0, rows, ahead, 0),
        piece(2, 2, 0, half, ahead, rows),
        piece(3, 3, 0, rows, behind, 0),
        piece(4, 2, half, half, behind, rows),
    ]
    for copy in copies:
        copy.start()
    for copy in copies:
        copy.wait()


def input_grads_kernel(place, own, ahead, behind, far_ahead, far_behind, out):
    rows = own.shape[0]
    half = rows // 2
    for turn, first, value in (
        (0, 0, own[...]),
        (1, 0, ahead[:rows, :]),
        (2, 0, far_ahead[...]),
        (2, half, far_behind[...]),
        (3, 0, behind[:rows, :]),
    ):
        start = pl.multiple_of(lax.rem(place[0] - turn + BLOCKS, BLOCKS) * rows + first, half)
        out[0, pl.ds(start, value.shape[0]), :] = value


def total_kernel(rank, scale, parts, down, up):
    total = jnp.sum(parts[...].astype(jnp.float32), axis=0) * scale
    down[0] = total[:rank, :].T
    up[0] = total[rank:, :].T


VMEM = pl.BlockSpec(memory_space=pltpu.VMEM)
ANY = pl.BlockSpec(memory_space=pl.ANY)
HBM = pl.BlockSpec(memory_space=pltpu.HBM)
SMEM = pl.BlockSpec(memory_space=pltpu.SMEM)


def resident(value):
    return pltpu.with_memory_space_constraint(value, pltpu.VMEM)


def far(value):
    return pltpu.with_memory_space_constraint(value, pltpu.HBM)


def per_device(block_inputs, target, frozen_weight, adapter_down, adapter_up, start_modulation, finish_modulation, level_pairs):
    stage = lax.axis_index("y")
    place = lax.axis_index("zh")
    core = lax.axis_index("c")
    tokens, width = block_inputs.shape[1:]
    owned, rank = adapter_down.shape[1:]
    share = tokens // BLOCKS
    batches = share // ROWS
    grad_scale = 1.0 / math.sqrt(tokens * MEMBERS)

    rest_rows = width + 2 * rank - HEAD_ROWS
    head, rest = pl.pallas_call(
        functools.partial(slab_kernel, width, rank),
        out_shape=[
            jax.ShapeDtypeStruct((HEAD_ROWS, owned), jnp.bfloat16),
            jax.ShapeDtypeStruct((rest_rows, owned), jnp.bfloat16),
        ],
        in_specs=[VMEM] * 3,
        out_specs=[VMEM] * 2,
        name="slab",
    )(frozen_weight[0], adapter_down[0], adapter_up[0])
    heads = lax.all_gather(head, PLANE, axis=0, tiled=True).reshape(BLOCKS, MEMBERS, HEAD_ROWS, owned)
    bundles = row_bundles(ring_bundle(rest))
    bundles = bundles + [lax.ppermute(value, "c", [(0, 1), (1, 0)]) for value in bundles]
    indices = [lax.axis_index(("zh", "zl")), lax.axis_index("x"), core]
    rests = pl.pallas_call(
        place_kernel,
        out_shape=pltpu.VMEM((BLOCKS, MEMBERS, rest_rows, owned), jnp.bfloat16),
        in_specs=[SMEM] * 3 + [ANY] * len(bundles),
        out_specs=VMEM,
        scratch_shapes=[pltpu.SemaphoreType.DMA((len(bundles), len(RING)))],
        compiler_params=pltpu.CompilerParams(vmem_limit_bytes=4 * MIB),
        name="place",
    )(*[index.astype(jnp.int32).reshape(1) for index in indices], *bundles)

    own_mod = per_batch_modulation(start_modulation[0], finish_modulation[0], level_pairs)
    mod = lax.all_to_all(own_mod, "zh", 0, 0, tiled=True).reshape(BLOCKS, batches, 3 * width)
    x = lax.all_to_all(block_inputs[0], "zh", 0, 0, tiled=True).reshape(BLOCKS, share, width)
    own_target = lax.dynamic_slice_in_dim(target, place * share, share, 0)

    stage, place, core = (index.astype(jnp.int32).reshape(1) for index in (stage, place, core))
    x, mod, stage, place, core, own_target = lax.optimization_barrier((x, mod, stage, place, core, own_target))

    heads_near, rests_near, mod_near = resident(heads), resident(rests), resident(mod)
    kept_shape = (BLOCKS, share, width)
    mixed, lows, d, h, inv, gs, us, ls, *sent = pl.pallas_call(
        functools.partial(first_kernel, batches, width, rank),
        out_shape=[
            jax.ShapeDtypeStruct(kept_shape, jnp.bfloat16),
            jax.ShapeDtypeStruct((BLOCKS, share, rank), jnp.bfloat16),
            pltpu.VMEM(kept_shape, jnp.float32),
            pltpu.VMEM(kept_shape, jnp.float32),
            pltpu.VMEM((BLOCKS, share, owned), jnp.float32),
            pltpu.HBM(kept_shape, jnp.bfloat16),
            pltpu.HBM(kept_shape, jnp.bfloat16),
            pltpu.HBM((BLOCKS, share, rank), jnp.bfloat16),
        ]
        + [pltpu.VMEM((ROWS, width), jnp.bfloat16)] * batches,
        in_specs=[SMEM] + [VMEM] * 3 + [HBM] * 2,
        out_specs=[VMEM] * 5 + [HBM] * 3 + [VMEM] * batches,
        scratch_shapes=[
            pltpu.VMEM((share, width), jnp.bfloat16),
            pltpu.VMEM(kept_shape, jnp.bfloat16),
            pltpu.VMEM(kept_shape, jnp.bfloat16),
            pltpu.VMEM((BLOCKS, share, rank), jnp.bfloat16),
            pltpu.VMEM((share, width), jnp.float32),
            pltpu.VMEM((2, MEMBERS, width + 2 * rank, owned), jnp.bfloat16),
            pltpu.SemaphoreType.DMA((2, 2, PIECES)),
            pltpu.SemaphoreType.DMA((3, BLOCKS)),
        ],
        compiler_params=pltpu.CompilerParams(vmem_limit_bytes=26 * MIB),
        cost_estimate=pl.CostEstimate(flops=4 * BLOCKS * share * width * width, bytes_accessed=40 * MIB, transcendentals=0),
        name="first",
    )(stage, x, mod_near, own_target, far(heads), far(rests))

    d_near, h_near, inv_near = (resident(v) for v in (d, h, inv))

    def relay(active_stage, m, gin, gs, us, ls):
        return pl.pallas_call(
            functools.partial(relay_kernel, active_stage, m, width, rank),
            out_shape=[pltpu.VMEM((ROWS, width), jnp.bfloat16)] + [
                pltpu.HBM(kept_shape, jnp.bfloat16),
                pltpu.HBM(kept_shape, jnp.bfloat16),
                pltpu.HBM((BLOCKS, share, rank), jnp.bfloat16),
            ],
            in_specs=[SMEM] + [VMEM] * 7 + [HBM] * 3,
            out_specs=[VMEM] + [HBM] * 3,
            scratch_shapes=[
                pltpu.VMEM((BLOCKS, ROWS, width), jnp.bfloat16),
                pltpu.VMEM((BLOCKS, ROWS, width), jnp.bfloat16),
                pltpu.VMEM((BLOCKS, ROWS, rank), jnp.bfloat16),
                pltpu.SemaphoreType.DMA((3, BLOCKS)),
            ],
            input_output_aliases={8: 1, 9: 2, 10: 3},
            compiler_params=pltpu.CompilerParams(vmem_limit_bytes=4 * MIB),
            cost_estimate=pl.CostEstimate(flops=2 * BLOCKS * ROWS * width * width, bytes_accessed=4 * MIB, transcendentals=0),
            name="relay",
        )(stage, resident(gin), heads_near, rests_near, d_near, h_near, mod_near, inv_near, far(gs), far(us), far(ls))

    _, gs, us, ls = relay(STAGES, 0, sent[0], gs, us, ls)
    for step in range(1, STAGES):
        arrived = [lax.ppermute(out, "y", [(STAGES - step, STAGES - 1 - step)]) for out in sent]
        sent = []
        for m in range(batches):
            gout, gs, us, ls = relay(STAGES - 1 - step, m, arrived[m], gs, us, ls)
            sent.append(gout)

    gs, us, ls, mixed, lows = lax.optimization_barrier((gs, us, ls, mixed, lows))

    def shifted(value, turn):
        return lax.ppermute(value, "zh", [(i, (i + turn) % BLOCKS) for i in range(BLOCKS)])

    packed = (share + share // 2, width)
    near_grads, ahead, behind = pl.pallas_call(
        split_kernel,
        out_shape=[pltpu.VMEM((share, width), jnp.bfloat16)] + [pltpu.VMEM(packed, jnp.bfloat16)] * 2,
        in_specs=[SMEM, HBM],
        out_specs=[VMEM] * 3,
        scratch_shapes=[pltpu.SemaphoreType.DMA((5,))],
        compiler_params=pltpu.CompilerParams(vmem_limit_bytes=4 * MIB),
        name="split",
    )(place, far(gs))
    ahead, behind = shifted(ahead, 1), shifted(behind, -1)

    row, ring = SIZES[3], SIZES[1] * SIZES[2]
    mine, theirs = pl.pallas_call(
        functools.partial(grads_kernel, rank),
        out_shape=[jax.ShapeDtypeStruct((row, ring, 2 * rank, owned), jnp.bfloat16)] * 2,
        in_specs=[SMEM] + [VMEM] * 4,
        out_specs=[VMEM] * 2,
        compiler_params=pltpu.CompilerParams(vmem_limit_bytes=24 * MIB),
        name="grads",
    )(core, mixed, lows, us, ls)
    theirs = lax.ppermute(theirs, "c", [(0, 1), (1, 0)])
    parts = (mine.astype(jnp.float32) + theirs.astype(jnp.float32)).astype(jnp.bfloat16)
    parts = lax.all_to_all(parts, "x", 0, 0, tiled=True)
    ahead, behind, parts = lax.optimization_barrier((ahead, behind, parts))
    parts = jnp.sum(parts.astype(jnp.float32), axis=0).astype(jnp.bfloat16)
    parts = lax.all_to_all(parts, ("zh", "zl"), 0, 0, tiled=True)
    far_ahead, far_behind = shifted(ahead[share:], 1), shifted(behind[share:], -1)
    down_grad, up_grad = pl.pallas_call(
        functools.partial(total_kernel, rank, grad_scale),
        out_shape=[jax.ShapeDtypeStruct((1, owned, rank), jnp.float32)] * 2,
        in_specs=[VMEM],
        out_specs=[VMEM] * 2,
        name="total",
    )(parts)
    input_grads = pl.pallas_call(
        input_grads_kernel,
        out_shape=jax.ShapeDtypeStruct((1, tokens, width), jnp.bfloat16),
        in_specs=[SMEM] + [VMEM] * 5,
        out_specs=VMEM,
        compiler_params=pltpu.CompilerParams(vmem_limit_bytes=8 * MIB),
        name="input_grads",
    )(place, near_grads, ahead, behind, far_ahead, far_behind)
    return input_grads, down_grad, up_grad


def solution(mesh):
    split = Mesh(mesh.devices.reshape(SIZES), AXES)
    blocks = ("y", "zh")
    return jax.shard_map(
        per_device,
        mesh=split,
        in_specs=(
            P(blocks, GROUP, None),
            P(GROUP, None),
            P(blocks, GROUP, None),
            P(blocks, GROUP, None),
            P(blocks, GROUP, None),
            P(blocks, None, None),
            P(blocks, None, None),
            P(GROUP, None),
        ),
        out_specs=(P(blocks, GROUP, None), P(blocks, GROUP, None), P(blocks, GROUP, None)),
        check_vma=False,
    )
```
